32 devices in a mesh: segment: 4 (over y, x), node: 8 (over z, core).
Axes of the slice: x: 2, y: 2, z: 4, core: 2. Of those that a mesh axis runs over, the one named last changes fastest.
Arguments:
- activations: bfloat16 [4, 2048, 512], P('segment', 'node'), may hold values from -8 to 8
- norm_gain: float32 [4, 512], P('segment'), may hold values from 0.5 to 1.5
- project_in: bfloat16 [4, 512, 1536], P('segment'), may hold values from -0.25 to 0.25
- project_out: bfloat16 [4, 512, 512], P('segment'), may hold values from -0.5 to 0.5
- virtual_keys: bfloat16 [4, 4, 512], P('segment'), may hold values from -6 to 6
- virtual_id: int32 [2048, 1], P('node'), may hold values from 0 to 3
- local_rows: int32 [16, 2048], P(None, 'node'), may hold values from 0 to 127
- slot_block: int32 [16, 8], P('node'), may hold values from 0 to 15, as said below
- slot_count: int32 [16], P('node'), may hold values from 1 to 8, as said below
- slot_rows: int32 [16, 8, 4, 128], P('node'), may hold values from 0 to 127
Outputs:
- handed: bfloat16 [4, 2048, 512], P('segment', 'node')
The draws below stay inside these ranges and needn't reach their ends.
Inputs may be any that keep to these rules, and one draw needn't show every extreme that they name: `virtual_id`: every virtual node has a member. `slot_block`: blocks d * 2 to (d + 1) * 2 - 1 lie on device d of node; every entry names a block of another device than the destination block's, and all entries of one device's rows that name blocks of the same device name the same block. `slot_count`: some block has 8 live slots.
All inputs are finite; a program needn't handle non-finite values.
Results may differ from the reference program's by a relative error of at most 0.0065.
Values may be sent and summed in bfloat16 or wider, within the bound.
No kernel may reach another device: no remote copies, remote signals or barrier semaphores. Data moves between devices by JAX's collectives and lax.ppermute only.
A program may use at most 64 MiB of HBM per device.

```python
import jax
import jax.numpy as jnp
from jax import lax

D = 512
HEADS = 8
HDIM = 64
VN = 4
BLK = 128
BLK_DEV = 2
EX = 8
KL = 16
KE = 4
GROUP = 8
LAYERS = 4
NODES = 2048
NBLK = 16


def draw_activations(key, part):
    noise_key, mean_key = jax.random.split(key, 2)
    common = jax.random.normal(mean_key, (LAYERS, 1, D), jnp.float32)
    position = jnp.arange(NODES, dtype=jnp.float32) / NODES
    noise = jax.random.normal(noise_key, (LAYERS, NODES, D), jnp.float32)
    ramp = 0.5 + position
    field = noise + ramp[None, :, None] * common
    return jnp.clip(field, -8.0, 8.0).astype(jnp.bfloat16)


def draw_slot_block(key, part):
    offset_key, block_key = jax.random.split(jax.random.fold_in(key, 11))
    offsets = jax.random.randint(offset_key, (GROUP,), 0, GROUP - 1)
    wanted = jax.random.randint(block_key, (GROUP, GROUP), 0, BLK_DEV)
    block_ids = jnp.arange(NBLK, dtype=jnp.int32)
    owner = block_ids // BLK_DEV
    slot_ids = (block_ids % BLK_DEV)[:, None] * EX + jnp.arange(EX, dtype=jnp.int32)[None, :]
    stepped = (slot_ids + offsets[owner][:, None]) % (GROUP - 1)
    peer = (owner[:, None] + 1 + stepped) % GROUP
    return (peer * BLK_DEV + wanted[owner[:, None], peer]).astype(jnp.int32)


def draw_slot_count(key, part):
    level_key, count_key, pick_key = jax.random.split(jax.random.fold_in(key, 23), 3)
    levels = jax.random.randint(level_key, (GROUP,), 0, 4)
    picked = jax.random.randint(pick_key, (), 0, GROUP)
    levels = jnp.where(jnp.arange(GROUP, dtype=jnp.int32) == picked, 3, levels)
    owner = jnp.arange(NBLK, dtype=jnp.int32) // BLK_DEV
    reach = jnp.minimum(EX, jnp.left_shift(1, levels[owner]))
    counts = 1 + jax.random.randint(count_key, (NBLK,), 0, reach)
    first = jnp.arange(NBLK, dtype=jnp.int32) == picked * BLK_DEV
    return jnp.where(first, EX, jnp.minimum(counts, EX)).astype(jnp.int32)


def place_ends(entries, stream_key, least, top_value):
    longest = entries.shape.index(max(entries.shape))
    spots = []
    for shift in (0, 1):
        where = [jax.random.randint(jax.random.fold_in(stream_key, axis), (), 0, length) for axis, length in enumerate(entries.shape)]
        where[longest] = (where[longest] + shift) % entries.shape[longest]
        spots.append(tuple(where))
    return entries.at[spots[0]].set(least).at[spots[1]].set(top_value)


def shard_levels(stream_key, extent, cuts, smallest, top_value):
    def one(axis_at, shards_of):
        steps = jax.random.uniform(jax.random.fold_in(jax.random.fold_in(stream_key, 6), axis_at), (shards_of,), jnp.float32, smallest / len(cuts), top_value / len(cuts))
        return jnp.repeat(jnp.exp(steps), extent[axis_at] // shards_of).reshape((-1,) + (1,) * (len(extent) - axis_at - 1))

    level = one(*cuts[0])
    for cut in cuts[1:]:
        level = level * one(*cut)
    return level


def distinct(key, rows, count, top, lift):
    order = jax.random.permutation(jax.random.fold_in(key, 1), count)
    favour = order
    for power in range(3):
        favour = favour * favour // count
    favour = favour * lift // count
    chance = jax.random.randint(jax.random.fold_in(key, 2), (rows, count), 0, 4096) + favour
    sure = jax.random.permutation(jax.random.fold_in(key, 3), rows)[jnp.arange(count) % rows]
    chance = jnp.where(jnp.arange(rows)[:, None] == sure[None, :], 1 << 14, chance)
    priority = chance * count + jnp.arange(count)
    return lax.top_k(priority.astype(jnp.int32), top)[1].astype(jnp.int32)


def centred(stream_key, shape, scale, bound, shards=(), kind=jnp.bfloat16):
    array = scale * jax.random.normal(stream_key, shape, jnp.float32)
    if shards:
        array = array * shard_levels(stream_key, shape, shards, -0.22, 0.18)
    return jnp.clip(array, -bound, bound).astype(kind)


def setup_inputs(seed: int = 0) -> dict:
    key_list = jax.random.split(jax.random.key(seed), 11)
    activations = draw_activations(jax.random.fold_in(key_list[10], 71), 0)
    norm_gain = jnp.clip(1.0 + 0.1 * jax.random.normal(key_list[1], (LAYERS, D), jnp.float32), 0.5, 1.5)
    project_in = centred(key_list[2], (LAYERS, D, 3 * D), D ** -0.5, 0.25, ((0, 4),))
    project_out = centred(key_list[3], (LAYERS, D, D), (D // 4) ** -0.5, 0.5, ((0, 4),))
    virtual_keys = centred(key_list[4], (LAYERS, VN, D), 1.0, 6.0, ((0, 4),))
    virtual_id = distinct(key_list[5], NODES, VN, 1, 0)
    local_rows = place_ends(jax.random.randint(key_list[6], (KL, NODES), 0, BLK), jax.random.fold_in(key_list[6], 1), 0, BLK - 1).astype(jnp.int32)
    slot_block = draw_slot_block(jax.random.fold_in(key_list[10], 71), 0)
    slot_count = draw_slot_count(jax.random.fold_in(key_list[10], 71), 0)
    slot_rows = place_ends(jax.random.randint(key_list[9], (NBLK, EX, KE, BLK), 0, BLK), jax.random.fold_in(key_list[9], 1), 0, BLK - 1).astype(jnp.int32)
    return {"activations": activations, "norm_gain": norm_gain, "project_in": project_in, "project_out": project_out, "virtual_keys": virtual_keys, "virtual_id": virtual_id, "local_rows": local_rows, "slot_block": slot_block, "slot_count": slot_count, "slot_rows": slot_rows}


cap_limit = 10.0
epsilon = 1e-05

def capped(raw_score):
    return cap_limit * jnp.tanh(raw_score / cap_limit)

def layer_norm(rows_in, gain_row):
    widened = rows_in.astype(jnp.float32)
    center = widened - lax.optimization_barrier(jnp.mean(widened, axis=-1, keepdims=True))
    spread = lax.optimization_barrier(jnp.mean(center * center, axis=-1, keepdims=True))
    return (center * lax.rsqrt(spread + epsilon) * gain_row).astype(jnp.bfloat16)

def edge_counts(index_rows):
    columns = jnp.arange(BLK, dtype=jnp.int32)
    return lax.optimization_barrier(jnp.sum((index_rows.astype(jnp.int32)[..., None] == columns).astype(jnp.float32), axis=0))

def pair_single(query_rows, key_rows, value_rows, counts):
    shaped = (BLK, HEADS, HDIM)
    query_wide = query_rows.astype(jnp.float32).reshape(shaped)
    key_wide = key_rows.astype(jnp.float32).reshape(shaped)
    value_wide = value_rows.astype(jnp.float32).reshape(shaped)
    raw_score = jnp.einsum('qhd,khd->hqk', query_wide, key_wide) * HDIM ** (-0.5)
    weights = (counts[None] * jnp.exp(capped(raw_score))).astype(jnp.bfloat16)
    numerator = jnp.einsum('hqk,khd->qhd', weights.astype(jnp.float32), value_wide)
    denominator = lax.optimization_barrier(jnp.sum(weights.astype(jnp.float32), axis=2)).T
    return (numerator, denominator)

def reference(activations, norm_gain, project_in, project_out, virtual_keys, virtual_id, local_rows, slot_block, slot_count, slot_rows):
    member = (virtual_id[:, 0].astype(jnp.int32)[:, None] == jnp.arange(VN, dtype=jnp.int32)[None, :]).astype(jnp.float32)
    block_list = jnp.arange(NBLK, dtype=jnp.int32)
    slot_list = jnp.arange(EX, dtype=jnp.int32)

    def one_layer(layer_index):
        normed = layer_norm(activations[layer_index], norm_gain[layer_index])
        projected = jnp.dot(normed, project_in[layer_index], preferred_element_type=jnp.float32)
        queries = projected[:, :D].astype(jnp.bfloat16)
        keys_all = projected[:, D:2 * D].astype(jnp.bfloat16)
        values_all = projected[:, 2 * D:].astype(jnp.bfloat16)
        own_key = jnp.dot(member, virtual_keys[layer_index].astype(jnp.float32), precision=lax.Precision.HIGHEST)
        pool_raw = lax.optimization_barrier(jnp.sum((own_key * keys_all.astype(jnp.float32)).reshape(NODES, HEADS, HDIM), axis=2)) * HDIM ** (-0.5)
        pool_weight = jnp.exp(capped(pool_raw)).astype(jnp.bfloat16)
        weighted = pool_weight.astype(jnp.float32)[:, :, None] * values_all.astype(jnp.float32).reshape(NODES, HEADS, HDIM)
        pool_num = jnp.einsum('rj,rhd->jhd', member, weighted, precision=lax.Precision.HIGHEST)
        pool_den = jnp.dot(member.T, pool_weight.astype(jnp.float32), precision=lax.Precision.HIGHEST)
        pooled = pool_num / pool_den[:, :, None]

        def one_block(block_index):
            start = (block_index * BLK).astype(jnp.int32)
            query_rows = lax.dynamic_slice_in_dim(queries, start, BLK, 0)
            key_rows = lax.dynamic_slice_in_dim(keys_all, start, BLK, 0)
            value_rows = lax.dynamic_slice_in_dim(values_all, start, BLK, 0)
            local_index = lax.dynamic_slice_in_dim(local_rows, start, BLK, 1)
            numerator, denominator = pair_single(query_rows, key_rows, value_rows, edge_counts(local_index))

            def add_slot(running, slot_index):
                source = (slot_block[block_index, slot_index] * BLK).astype(jnp.int32)
                live_flag = (slot_index < slot_count[block_index]).astype(jnp.float32)
                counts_now = edge_counts(slot_rows[block_index, slot_index]) * live_flag
                extra_num, extra_den = pair_single(query_rows, lax.dynamic_slice_in_dim(keys_all, source, BLK, 0), lax.dynamic_slice_in_dim(values_all, source, BLK, 0), counts_now)
                return ((running[0] + extra_num, running[1] + extra_den), None)
            (numerator, denominator), _ = lax.scan(add_slot, (numerator, denominator), slot_list)
            return numerator / denominator[:, :, None]
        attended = lax.map(one_block, block_list).reshape(NODES, D)
        broadcast_pool = jnp.dot(member, pooled.reshape(VN, D), precision=lax.Precision.HIGHEST)
        mixed = (attended + broadcast_pool).astype(jnp.bfloat16)
        return (activations[layer_index].astype(jnp.float32) + jnp.dot(mixed, project_out[layer_index], preferred_element_type=jnp.float32)).astype(jnp.bfloat16)
    layers_out = lax.map(one_layer, jnp.arange(LAYERS, dtype=jnp.int32))
    return jnp.roll(layers_out, 1, axis=0)
```

```python
import functools

import jax
import jax.numpy as jnp
from jax import lax
from jax.experimental import pallas as pl
from jax.experimental.pallas import tpu as pltpu
from jax.sharding import PartitionSpec as P

HEADS = 8
EPSILON = 1e-05
CAP_LIMIT = 10.0
LOG2E = 1.4426950408889634
ONES_ROWS = 16
F32 = jnp.float32
BF16 = jnp.bfloat16
VMEM = pl.BlockSpec(memory_space=pltpu.VMEM)
SMEM = pl.BlockSpec(memory_space=pltpu.SMEM)


def shifted(value, axis, steps):
    count = lax.axis_size(axis)
    pairs = [(source, (source + steps) % count) for source in range(count)]
    return lax.ppermute(value, axis, pairs)


def norm_rows(rows_in, gain_row):
    widened = rows_in.astype(F32)
    center = widened - jnp.mean(widened, axis=-1, keepdims=True)
    spread = jnp.mean(center * center, axis=-1, keepdims=True)
    return (center * lax.rsqrt(spread + EPSILON) * gain_row).astype(BF16)


def exp_capped(raw, scale):
    return jnp.exp2((CAP_LIMIT * LOG2E) * jnp.tanh(raw * (scale / CAP_LIMIT)))


def counts_of(index_rows, block_rows):
    rows = lax.broadcasted_iota(jnp.int32, (block_rows, index_rows.shape[1]), 0)
    total = jnp.zeros(rows.shape, F32)
    for j in range(index_rows.shape[0]):
        total = total + jnp.where(index_rows[j : j + 1, :] == rows, 1.0, 0.0)
    return total


def mm(a, b):
    return jnp.dot(a, b, preferred_element_type=F32)


def mm_nt(a, b):
    return lax.dot_general(a, b, (((1,), (1,)), ((), ())), preferred_element_type=F32)


def mm_tn(a, b):
    return lax.dot_general(a, b, (((0,), (0,)), ((), ())), preferred_element_type=F32)


def local_kernel(
    x_ref, gain_ref, win_ref, vk_ref, vid_ref, lrows_ref,
    qbd_ref, num_ref, den_ref, pool_ref, wvt_ref,
):
    rows, width = x_ref.shape
    blocks, pairs, wide, _ = qbd_ref.shape
    br = rows // blocks
    head = width // HEADS
    scale = head ** (-0.5)
    virtual = vk_ref.shape[0]
    normed = norm_rows(x_ref[...], gain_ref[...])
    q = mm(normed, win_ref[:, :width]).astype(BF16)
    k = mm(normed, win_ref[:, width : 2 * width]).astype(BF16)
    v = mm(normed, win_ref[:, 2 * width :]).astype(BF16)
    qt = q.T
    vt = v.T
    wvt_ref[...] = win_ref[:, 2 * width :].T
    zero = jnp.zeros((head, br), BF16)
    ones = jnp.ones((ONES_ROWS, br), BF16)

    head_of_lane = lax.broadcasted_iota(jnp.int32, (HEADS, width), 1) // head
    head_of_row = lax.broadcasted_iota(jnp.int32, (HEADS, width), 0)
    own_head = head_of_lane == head_of_row
    vkf = vk_ref[...].astype(F32)
    vkbd = jnp.concatenate(
        [
            jnp.where(own_head, jnp.broadcast_to(vkf[j : j + 1, :], (HEADS, width)), 0.0)
            for j in range(virtual)
        ],
        axis=0,
    ).astype(BF16)
    raw = mm_nt(k, vkbd)
    lanes = lax.broadcasted_iota(jnp.int32, raw.shape, 1) // HEADS
    pool_w = jnp.where(vid_ref[...] == lanes, exp_capped(raw, scale), 0.0).astype(BF16)
    pool_num = mm_tn(pool_w, v)
    pool_den = mm_tn(pool_w, jnp.ones((rows, width), BF16))
    for j in range(virtual):
        part = slice(j * HEADS, (j + 1) * HEADS)
        pool_ref[j : j + 1, :] = jnp.sum(
            jnp.where(own_head, pool_num[part], 0.0), axis=0, keepdims=True
        )
        pool_ref[virtual + j : virtual + j + 1, :] = jnp.sum(
            jnp.where(own_head, pool_den[part], 0.0), axis=0, keepdims=True
        )

    for b in range(blocks):
        cols = slice(b * br, (b + 1) * br)
        counts = counts_of(lrows_ref[:, cols], br)
        counts2 = jnp.concatenate([counts, counts], axis=1)
        for t in range(pairs):
            r0 = t * wide
            mid = r0 + head
            end = r0 + wide
            bd = jnp.concatenate(
                [
                    jnp.concatenate([qt[r0:mid, cols], zero], axis=1),
                    jnp.concatenate([zero, qt[mid:end, cols]], axis=1),
                ],
                axis=0,
            )
            qbd_ref[b, t] = bd
            p = (counts2 * exp_capped(mm(k[cols, r0:end], bd), scale)).astype(BF16)
            o = mm(jnp.concatenate([vt[r0:end, cols], ones], axis=0), p)
            num_ref[b, r0:mid, :] = o[:head, :br]
            num_ref[b, mid:end, :] = o[head:wide, br:]
            den_ref[b, 2 * t : 2 * t + 1, :] = o[wide : wide + 1, :br]
            den_ref[b, 2 * t + 1 : 2 * t + 2, :] = o[wide : wide + 1, br:]


def slot_kernel(
    sblock_ref, scount_ref, xg_ref, gain_ref, win_ref, wvt_ref, srows_ref,
    qbd_ref, num_ref, den_ref, pool_ref, vid_ref, x_ref, wo_ref,
    out_ref, k_scr, vt_scr, num_scr, den_scr, want_ref,
):
    peers = xg_ref.shape[0]
    rows, width = x_ref.shape
    blocks, pairs, wide, _ = qbd_ref.shape
    br = rows // blocks
    head = width // HEADS
    scale = head ** (-0.5)
    virtual = pool_ref.shape[1] // 2
    slots = sblock_ref.shape[1]

    for d in range(peers):
        want_ref[d] = 0
    for b in range(blocks):
        for e in range(slots):
            entry = sblock_ref[b, e]
            want_ref[entry // blocks] = entry % blocks
    ones = jnp.ones((ONES_ROWS, br), BF16)

    def project(c, carry):
        d0 = 2 * c
        d1 = 2 * c + 1
        w0 = pl.multiple_of(want_ref[d0] * br, br)
        w1 = pl.multiple_of(want_ref[d1] * br, br)
        xs = jnp.concatenate([xg_ref[d0, pl.ds(w0, br), :], xg_ref[d1, pl.ds(w1, br), :]], axis=0)
        normed = norm_rows(xs, gain_ref[...])
        k = mm(normed, win_ref[:, width : 2 * width]).astype(BF16)
        vt = mm_nt(wvt_ref[...], normed).astype(BF16)
        k_scr[d0] = k[:br]
        k_scr[d1] = k[br:]
        for t in range(pairs):
            part = slice(t * wide, (t + 1) * wide)
            vt_scr[d0, t, :wide, :] = vt[part, :br]
            vt_scr[d1, t, :wide, :] = vt[part, br:]
            vt_scr[d0, t, wide:, :] = ones
            vt_scr[d1, t, wide:, :] = ones
        return carry

    lax.fori_loop(0, peers // 2, project, 0, unroll=peers <= 8)

    num_scr[...] = num_ref[...]
    den_scr[...] = den_ref[...]
    for b in range(blocks):
        live = scount_ref[b]

        def two_slots(i, carry, b=b, live=live):
            e0 = 2 * i
            e1 = e0 + 1
            d0 = sblock_ref[b, e0] // blocks
            d1 = sblock_ref[b, e1] // blocks
            flag = jnp.where(e1 < live, 1.0, 0.0).astype(F32)
            c0 = counts_of(srows_ref[b, e0], br)
            c1 = counts_of(srows_ref[b, e1], br) * flag
            counts = jnp.concatenate([c0, c1], axis=0)
            counts2 = jnp.concatenate([counts, counts], axis=1)
            for t in range(pairs):
                r0 = t * wide
                mid = r0 + head
                end = r0 + wide
                keys = jnp.concatenate([k_scr[d0, :, r0:end], k_scr[d1, :, r0:end]], axis=0)
                p = (counts2 * exp_capped(mm(keys, qbd_ref[b, t]), scale)).astype(BF16)
                o = mm(jnp.concatenate([vt_scr[d0, t], vt_scr[d1, t]], axis=1), p)
                num_scr[b, r0:mid, :] += o[:head, :br]
                num_scr[b, mid:end, :] += o[head:wide, br:]
                den_scr[b, 2 * t : 2 * t + 1, :] += o[wide : wide + 1, :br]
                den_scr[b, 2 * t + 1 : 2 * t + 2, :] += o[wide : wide + 1, br:]
            return carry

        lax.fori_loop(0, (live + 1) // 2, two_slots, 0)

    total = pool_ref[0]
    for d in range(1, peers):
        total = total + pool_ref[d]
    pooled = total[:virtual] / total[virtual:]
    vid = vid_ref[...]
    spread = jnp.broadcast_to(pooled[0:1, :], (rows, width))
    for j in range(1, virtual):
        spread = jnp.where(vid == j, pooled[j : j + 1, :], spread)
    for b in range(blocks):
        part = slice(b * br, (b + 1) * br)
        att = jnp.concatenate(
            [
                num_scr[b, h * head : (h + 1) * head, :] / den_scr[b, h : h + 1, :]
                for h in range(HEADS)
            ],
            axis=0,
        )
        mixed = (att.T + spread[part]).astype(BF16)
        out_ref[part, :] = (x_ref[part, :].astype(F32) + mm(mixed, wo_ref[...])).astype(BF16)


def body(
    activations,
    norm_gain,
    project_in,
    project_out,
    virtual_keys,
    virtual_id,
    local_rows,
    slot_block,
    slot_count,
    slot_rows,
):
    _, rows, width = activations.shape
    br = slot_rows.shape[3]
    blocks = rows // br
    peers = lax.axis_size("node")
    virtual = virtual_keys.shape[1]
    pairs = HEADS // 2
    wide = width // pairs
    x = activations[0]
    gathered = lax.all_gather(x, "node", axis=0, tiled=False)
    qbd, num, den, pool, wvt = pl.pallas_call(
        local_kernel,
        out_shape=(
            jax.ShapeDtypeStruct((blocks, pairs, wide, 2 * br), BF16),
            jax.ShapeDtypeStruct((blocks, width, br), F32),
            jax.ShapeDtypeStruct((blocks, HEADS, br), F32),
            jax.ShapeDtypeStruct((2 * virtual, width), F32),
            jax.ShapeDtypeStruct((width, width), BF16),
        ),
        in_specs=[VMEM] * 6,
        out_specs=[VMEM] * 5,
        compiler_params=pltpu.CompilerParams(vmem_limit_bytes=40 * 2**20),
        cost_estimate=pl.CostEstimate(
            flops=2 * rows * width * 4 * width, bytes_accessed=4 * 2**20, transcendentals=2**20
        ),
        name="own_rows",
    )(x, norm_gain, project_in[0], virtual_keys[0], virtual_id, local_rows)
    pools = lax.all_to_all(
        jnp.broadcast_to(pool[None], (peers,) + pool.shape), "node", split_axis=0, concat_axis=0, tiled=True
    )
    updated = pl.pallas_call(
        slot_kernel,
        out_shape=jax.ShapeDtypeStruct((rows, width), BF16),
        in_specs=[SMEM, SMEM] + [VMEM] * 12,
        out_specs=VMEM,
        scratch_shapes=[
            pltpu.VMEM((peers, br, width), BF16),
            pltpu.VMEM((peers, pairs, wide + ONES_ROWS, br), BF16),
            pltpu.VMEM((blocks, width, br), F32),
            pltpu.VMEM((blocks, HEADS, br), F32),
            pltpu.SMEM((peers,), jnp.int32),
        ],
        compiler_params=pltpu.CompilerParams(vmem_limit_bytes=48 * 2**20),
        cost_estimate=pl.CostEstimate(
            flops=2 * peers * br * width * 3 * width, bytes_accessed=6 * 2**20, transcendentals=2**22
        ),
        name="expander_slots",
    )(
        slot_block, slot_count, gathered, norm_gain, project_in[0], wvt, slot_rows,
        qbd, num, den, pools, virtual_id, x, project_out[0],
    )
    return shifted(updated[None], "segment", 1)


def solution(mesh):
    placed = (
        P("segment", "node", None),
        P("segment", None),
        P("segment", None, None),
        P("segment", None, None),
        P("segment", None, None),
        P("node", None),
        P(None, "node"),
        P("node", None),
        P("node"),
        P("node", None, None, None),
    )
    return jax.shard_map(
        body, mesh=mesh, in_specs=placed, out_specs=P("segment", "node", None), check_vma=False
    )
```

```python
import functools

import jax
import jax.numpy as jnp
from jax import lax
from jax.experimental import pallas as pl
from jax.experimental.pallas import tpu as pltpu
from jax.sharding import PartitionSpec as P

HEADS = 8
CORES = 2
EPSILON = 1e-05
CAP_LIMIT = 10.0
LOG2E = 1.4426950408889634
EXTRA = 16
F32 = jnp.float32
BF16 = jnp.bfloat16
ANY = pl.BlockSpec(memory_space=pl.ANY)
VMEM = pl.BlockSpec(memory_space=pltpu.VMEM)


def ring_order(chips):
    return list(range(0, 1)) + list(range(1, chips, 2)) + list(range((chips - 1) // 2 * 2, 0, -2))


def ring_place(chip, chips):
    return jnp.where(chip % 2 == 1, (chip + 1) // 2, (chips - chip // 2) % chips)


def to_next_chip(value, devices):
    chips = devices // CORES
    order = ring_order(chips)
    pairs = [
        (order[i] * CORES + c, order[(i + 1) % chips] * CORES + c)
        for i in range(chips)
        for c in range(CORES)
    ]
    return lax.ppermute(value, "node", pairs)


def to_other_core(value, devices):
    return lax.ppermute(value, "node", [(d, d ^ 1) for d in range(devices)])


def to_next_segment(value):
    count = lax.axis_size("segment")
    return lax.ppermute(value, "segment", [(s, (s + 1) % count) for s in range(count)])


def norm_rows(rows_in, gain_row):
    widened = rows_in.astype(F32)
    center = widened - jnp.mean(widened, axis=-1, keepdims=True)
    spread = jnp.mean(center * center, axis=-1, keepdims=True)
    return (center * lax.rsqrt(spread + EPSILON) * gain_row).astype(BF16)


def exp_capped(raw, scale):
    return jnp.exp2((CAP_LIMIT * LOG2E) * jnp.tanh(raw * (scale / CAP_LIMIT)))


def counts_of(index_rows, block_rows):
    rows = lax.broadcasted_iota(jnp.int32, (block_rows, index_rows.shape[1]), 0)
    total = jnp.zeros(rows.shape, F32)
    for j in range(index_rows.shape[0]):
        total = total + jnp.where(index_rows[j : j + 1, :] == rows, 1.0, 0.0)
    return total


def mm(a, b):
    return jnp.dot(a, b, preferred_element_type=F32)


def mm_nt(a, b):
    return lax.dot_general(a, b, (((1,), (1,)), ((), ())), preferred_element_type=F32)


def halves(value):
    high = value.astype(BF16)
    return high, (value - high.astype(F32)).astype(BF16)


def choose(mask_row, first, second):
    rows, width = first.shape
    lanes = mask_row.shape[1]
    mask = jnp.broadcast_to(mask_row, (rows, lanes))
    mask = jnp.concatenate([mask] * (width // lanes), axis=1)
    return jnp.where(mask > 0.5, second.astype(F32), first.astype(F32)).astype(first.dtype)


def own_kernel(
    x_hbm, gain_hbm, win_hbm, vk_hbm, vid_hbm,
    qt_ref, k_ref, vt_ref, wk_ref, wvt_ref, gain_ref, load_ref,
    x_ref, win_ref, vk_ref, vid_ref, sems,
):
    rows, width = x_ref.shape
    virtual = vk_ref.shape[0]
    scale = (width // HEADS) ** (-0.5)
    copies = [
        pltpu.make_async_copy(src, dst, sems.at[i])
        for i, (src, dst) in enumerate(
            [
                (x_hbm, x_ref), (gain_hbm, gain_ref), (win_hbm, win_ref),
                (vk_hbm, vk_ref), (vid_hbm, vid_ref),
            ]
        )
    ]
    for copy in copies:
        copy.start()
    copies[0].wait()
    copies[1].wait()
    normed = norm_rows(x_ref[...], gain_ref[...])
    for copy in copies[2:]:
        copy.wait()
    k = mm(normed, win_ref[:, width : 2 * width]).astype(BF16)
    v = mm(normed, win_ref[:, 2 * width :]).astype(BF16)

    head_of_lane = lax.broadcasted_iota(jnp.int32, (HEADS, width), 1) // (width // HEADS)
    own_head = head_of_lane == lax.broadcasted_iota(jnp.int32, (HEADS, width), 0)
    vkf = vk_ref[...].astype(F32)
    vkbd = jnp.concatenate(
        [
            jnp.where(own_head, jnp.broadcast_to(vkf[j : j + 1, :], (HEADS, width)), 0.0)
            for j in range(virtual)
        ],
        axis=0,
    ).astype(BF16)
    raw = mm_nt(vkbd, k)
    owner = lax.broadcasted_iota(jnp.int32, raw.shape, 0) // HEADS
    pool_w = jnp.where(vid_ref[...] == owner, exp_capped(raw, scale), 0.0).astype(BF16)
    pool_num = mm(pool_w, v)
    pool_den = mm(pool_w, jnp.ones((rows, width), BF16))
    parts = [
        jnp.sum(jnp.where(own_head, whole[j * HEADS : (j + 1) * HEADS], 0.0), axis=0, keepdims=True)
        for whole in (pool_num, pool_den)
        for j in range(virtual)
    ]
    high, low = halves(jnp.concatenate(parts, axis=0))
    br = load_ref.shape[0] - 4 * virtual
    load_ref[:br, :] = x_ref[rows - br :, :]
    load_ref[br:, :] = jnp.concatenate([high.astype(F32), low.astype(F32)], axis=0).astype(BF16)

    k_ref[...] = k
    vt_ref[...] = v.T
    qt_ref[...] = mm(normed, win_ref[:, :width]).astype(BF16).T
    wk_ref[...] = win_ref[:, width : 2 * width]
    wvt_ref[...] = win_ref[:, 2 * width :].T


def attend(keys, values, counts, qbd, scale):
    p = (counts * exp_capped(mm(keys, qbd), scale)).astype(BF16)
    return mm(values, p)


def fold(o, num_ref, den_ref, b, t, add):
    wide = o.shape[0] - EXTRA
    head = wide // 2
    br = o.shape[1] // 2
    r0 = t * wide
    places = (
        (num_ref, slice(r0, r0 + head), o[:head, :br]),
        (num_ref, slice(r0 + head, r0 + wide), o[head:wide, br:]),
        (den_ref, slice(2 * t, 2 * t + 1), o[wide : wide + 1, :br]),
        (den_ref, slice(2 * t + 1, 2 * t + 2), o[wide : wide + 1, br:]),
    )
    for ref, part, value in places:
        if add:
            ref[b, part, :] += value
        else:
            ref[b, part, :] = value


def prep_kernel(
    qt_ref, k_ref, vt_ref, lrows_hbm, srows_hbm, sblock_hbm, other_hbm, vid_hbm,
    qbd_ref, num_ref, den_ref, counts_ref, mask_ref, vcol_ref,
    lrows_ref, srows_ref, vid_ref, sblock_ref, other_ref, want_ref, sems,
):
    width, rows = qt_ref.shape
    blocks, pairs, wide, _ = qbd_ref.shape
    chips = mask_ref.shape[1]
    slots = sblock_ref.shape[1]
    br = rows // blocks
    head = width // HEADS
    scale = head ** (-0.5)
    copies = [
        pltpu.make_async_copy(src, dst, sems.at[i])
        for i, (src, dst) in enumerate(
            [
                (lrows_hbm, lrows_ref), (srows_hbm, srows_ref), (vid_hbm, vid_ref),
                (sblock_hbm, sblock_ref), (other_hbm, other_ref),
            ]
        )
    ]
    for copy in copies:
        copy.start()
    for copy in copies:
        copy.wait()
    me = lax.axis_index("node")
    place = ring_place(me // CORES, chips)
    core = me % CORES
    for which, table in enumerate((sblock_ref, other_ref)):
        for d in range(chips * CORES):
            want_ref[d] = 0
        for b in range(blocks):
            for e in range(slots):
                entry = table[b, e]
                want_ref[entry // blocks] = entry % blocks
        for z in range(chips):
            step = (place - ring_place(jnp.int32(z), chips) + chips) % chips
            value = want_ref[z * CORES + core].astype(F32)
            mask_ref[which, step] = jnp.full(mask_ref.shape[2:], value, F32)

    vcol_ref[...] = jnp.broadcast_to(vid_ref[...].astype(F32), (128, rows)).T
    zero = jnp.zeros((head, br), BF16)
    ones = jnp.ones((EXTRA, br), BF16)
    for b in range(blocks):
        cols = slice(b * br, (b + 1) * br)
        for e in range(slots):
            counts_ref[b, e] = counts_of(srows_ref[b, e], br)
        counts = counts_of(lrows_ref[:, cols], br)
        counts2 = jnp.concatenate([counts, counts], axis=1)
        for t in range(pairs):
            r0 = t * wide
            mid = r0 + head
            end = r0 + wide
            bd = jnp.concatenate(
                [
                    jnp.concatenate([qt_ref[r0:mid, cols], zero], axis=1),
                    jnp.concatenate([zero, qt_ref[mid:end, cols]], axis=1),
                ],
                axis=0,
            )
            qbd_ref[b, t] = bd
            values = jnp.concatenate([vt_ref[r0:end, cols], ones], axis=0)
            fold(attend(k_ref[cols, r0:end], values, counts2, bd, scale), num_ref, den_ref, b, t, False)


def swap_kernel(mask_ref, *refs):
    out_ref = refs[-1]
    chips = (len(refs) - 1) // 2
    firsts, seconds = refs[:chips], refs[chips:-1]
    br = firsts[0].shape[0]
    extra = seconds[0].shape[0] - br
    total = jnp.zeros((extra // 2, firsts[0].shape[1]), F32)
    for s in range(chips):
        out_ref[s * br : (s + 1) * br, :] = choose(
            mask_ref[1, s, :1, :], firsts[s][...], seconds[s][:br, :]
        )
        part = seconds[s][br:, :].astype(F32)
        total = total + (part[: extra // 2] + part[extra // 2 :])
    high, low = halves(total)
    out_ref[chips * br :, :] = jnp.concatenate(
        [high.astype(F32), low.astype(F32)], axis=0
    ).astype(BF16)


def project(xs, gain_ref, wk_ref, wvt_ref, k_scr, vt_scr):
    count, br, _ = k_scr.shape
    _, pairs, tall, _ = vt_scr.shape
    wide = tall - EXTRA
    ones = jnp.ones((EXTRA, br), BF16)
    step = 2 if count % 2 == 0 else count
    for s0 in range(0, count, step):
        normed = norm_rows(jnp.concatenate(xs[s0 : s0 + step], axis=0), gain_ref[...])
        k = mm(normed, wk_ref[...]).astype(BF16)
        vt = mm_nt(wvt_ref[...], normed).astype(BF16)
        for i in range(step):
            part = slice(i * br, (i + 1) * br)
            k_scr[s0 + i] = k[part]
            for t in range(pairs):
                vt_scr[s0 + i, t, :wide, :] = vt[t * wide : (t + 1) * wide, part]
                vt_scr[s0 + i, t, wide:, :] = ones


def run_slots(
    same_core, first_step, sblock_ref, scount_ref, list_ref, counts_ref, qbd_ref,
    k_scr, vt_scr, num_ref, den_ref, chips, scale,
):
    blocks, slots = sblock_ref.shape
    _, pairs, wide, _ = qbd_ref.shape
    me = lax.axis_index("node")
    place = ring_place(me // CORES, chips)
    core = me % CORES
    for b in range(blocks):
        live = scount_ref[b]
        found = jnp.int32(0)
        for e in range(slots):
            device = sblock_ref[b, e] // blocks
            step = (place - ring_place(device // CORES, chips) + chips) % chips
            mine = (device % CORES == core) == same_core
            list_ref[0, found] = jnp.maximum(step - first_step, 0)
            list_ref[1, found] = e
            found = found + jnp.where(mine & (e < live), 1, 0)

        def two_slots(i, carry, b=b, found=found):
            n0 = 2 * i
            odd = n0 + 1 < found
            n1 = jnp.where(odd, n0 + 1, n0)
            flag = jnp.where(odd, 1.0, 0.0).astype(F32)
            s0, s1 = list_ref[0, n0], list_ref[0, n1]
            counts = jnp.concatenate(
                [counts_ref[b, list_ref[1, n0]], counts_ref[b, list_ref[1, n1]] * flag], axis=0
            )
            counts2 = jnp.concatenate([counts, counts], axis=1)
            for t in range(pairs):
                cols = slice(t * wide, (t + 1) * wide)
                keys = jnp.concatenate([k_scr[s0, :, cols], k_scr[s1, :, cols]], axis=0)
                values = jnp.concatenate([vt_scr[s0, t], vt_scr[s1, t]], axis=1)
                fold(attend(keys, values, counts2, qbd_ref[b, t], scale), num_ref, den_ref, b, t, True)
            return carry

        lax.fori_loop(0, (found + 1) // 2, two_slots, 0)


def near_kernel(
    sblock_hbm, scount_hbm, mask_ref, gain_ref, wk_ref, wvt_ref, counts_ref, qbd_ref,
    num_in, den_in, *refs
):
    num_ref, den_ref, k_scr, vt_scr, sblock_ref, scount_ref, list_ref, sems = refs[-8:]
    rest = refs[:-8]
    others = len(rest) // 2
    firsts, seconds = rest[:others], rest[others:]
    chips = others + 1
    copies = [
        pltpu.make_async_copy(sblock_hbm, sblock_ref, sems.at[0]),
        pltpu.make_async_copy(scount_hbm, scount_ref, sems.at[1]),
    ]
    for copy in copies:
        copy.start()
    br = k_scr.shape[1]
    num_ref[...] = num_in[...]
    den_ref[...] = den_in[...]
    xs = [
        choose(mask_ref[0, s + 1, :1, :], firsts[s][...], seconds[s][:br, :])
        for s in range(others)
    ]
    project(xs, gain_ref, wk_ref, wvt_ref, k_scr, vt_scr)
    for copy in copies:
        copy.wait()
    scale = (k_scr.shape[2] // HEADS) ** (-0.5)
    run_slots(
        True, 1, sblock_ref, scount_ref, list_ref, counts_ref, qbd_ref,
        k_scr, vt_scr, num_ref, den_ref, chips, scale,
    )


def far_kernel(
    sblock_hbm, scount_hbm, wo_hbm, x_hbm, swapped_ref, gain_ref, wk_ref, wvt_ref, counts_ref,
    qbd_ref, num_in, den_in, vcol_ref, *refs
):
    (
        out_ref, num_ref, den_ref, k_scr, vt_scr, wo_ref, x_ref,
        sblock_ref, scount_ref, list_ref, sems,
    ) = refs[-11:]
    seconds = refs[:-11]
    chips = len(seconds)
    copies = [
        pltpu.make_async_copy(sblock_hbm, sblock_ref, sems.at[0]),
        pltpu.make_async_copy(scount_hbm, scount_ref, sems.at[1]),
        pltpu.make_async_copy(wo_hbm, wo_ref, sems.at[2]),
        pltpu.make_async_copy(x_hbm, x_ref, sems.at[3]),
    ]
    for copy in copies:
        copy.start()
    rows, width = x_ref.shape
    blocks = num_ref.shape[0]
    br = rows // blocks
    head = width // HEADS
    num_ref[...] = num_in[...]
    den_ref[...] = den_in[...]
    xs = [swapped_ref[s * br : (s + 1) * br, :] for s in range(chips)]
    project(xs, gain_ref, wk_ref, wvt_ref, k_scr, vt_scr)
    for copy in copies:
        copy.wait()
    run_slots(
        False, 0, sblock_ref, scount_ref, list_ref, counts_ref, qbd_ref,
        k_scr, vt_scr, num_ref, den_ref, chips, head ** (-0.5),
    )
    total = swapped_ref[chips * br :, :].astype(F32)
    extra = total.shape[0]
    for second in seconds:
        total = total + second[br:, :].astype(F32)
    total = total[: extra // 2] + total[extra // 2 :]
    virtual = extra // 4
    pooled = total[:virtual] / total[virtual:]
    lanes = vcol_ref.shape[1]
    for b in range(blocks):
        part = slice(b * br, (b + 1) * br)
        vid = vcol_ref[part, :]
        att = jnp.concatenate(
            [
                num_ref[b, h * head : (h + 1) * head, :] / den_ref[b, h : h + 1, :]
                for h in range(HEADS)
            ],
            axis=0,
        ).T
        pieces = []
        for c in range(0, width, lanes):
            own = jnp.broadcast_to(pooled[0:1, c : c + lanes], (br, lanes))
            for j in range(1, virtual):
                own = jnp.where(vid == float(j), pooled[j : j + 1, c : c + lanes], own)
            pieces.append((att[:, c : c + lanes] + own).astype(BF16))
        mixed = jnp.concatenate(pieces, axis=1)
        out_ref[part, :] = (x_ref[part, :].astype(F32) + mm(mixed, wo_ref[...])).astype(BF16)


def params(mib):
    return pltpu.CompilerParams(vmem_limit_bytes=mib * 2**20)


def cost(flops):
    return pl.CostEstimate(flops=flops, bytes_accessed=2**20, transcendentals=flops // 1024)


def body(
    activations,
    norm_gain,
    project_in,
    project_out,
    virtual_keys,
    virtual_id,
    local_rows,
    slot_block,
    slot_count,
    slot_rows,
):
    _, rows, width = activations.shape
    br = slot_rows.shape[3]
    slots = slot_block.shape[1]
    blocks = rows // br
    devices = lax.axis_size("node")
    chips = devices // CORES
    virtual = virtual_keys.shape[1]
    pairs = HEADS // 2
    wide = width // pairs
    extra = 4 * virtual
    shape = jax.ShapeDtypeStruct
    x = activations[0]
    vid = virtual_id.reshape(1, rows)

    firsts = [x[:br]]
    firsts.append(to_next_chip(firsts[0], devices))
    other_block = to_other_core(slot_block, devices)
    qt, k, vt, wk, wvt, gain, load = pl.pallas_call(
        own_kernel,
        out_shape=(
            shape((width, rows), BF16),
            shape((rows, width), BF16),
            shape((width, rows), BF16),
            shape((width, width), BF16),
            shape((width, width), BF16),
            shape((1, width), F32),
            shape((br + extra, width), BF16),
        ),
        in_specs=[ANY] * 5,
        out_specs=[VMEM] * 7,
        scratch_shapes=[
            pltpu.VMEM((rows, width), BF16),
            pltpu.VMEM((width, 3 * width), BF16),
            pltpu.VMEM((virtual, width), BF16),
            pltpu.VMEM((1, rows), jnp.int32),
            pltpu.SemaphoreType.DMA((5,)),
        ],
        compiler_params=params(24),
        cost_estimate=cost(8 * rows * width * width),
        name="own_rows",
    )(x, norm_gain, project_in[0], virtual_keys[0], vid)
    seconds = [load]
    for s in range(1, chips):
        seconds.append(to_next_chip(seconds[-1], devices))
        if s < chips - 1:
            firsts.append(to_next_chip(firsts[-1], devices))

    accumulators = (shape((blocks, width, br), F32), shape((blocks, HEADS, br), F32))
    qbd, num, den, counts, mask, vcol = pl.pallas_call(
        prep_kernel,
        out_shape=(
            (shape((blocks, pairs, wide, 2 * br), BF16),)
            + accumulators
            + (
                shape((blocks, slots, br, br), F32),
                shape((2, chips, 8, 128), F32),
                shape((rows, 128), F32),
            )
        ),
        in_specs=[VMEM] * 3 + [ANY] * 5,
        out_specs=[VMEM] * 6,
        scratch_shapes=[
            pltpu.VMEM(local_rows.shape, jnp.int32),
            pltpu.VMEM(slot_rows.shape, jnp.int32),
            pltpu.VMEM((1, rows), jnp.int32),
            pltpu.SMEM((blocks, slots), jnp.int32),
            pltpu.SMEM((blocks, slots), jnp.int32),
            pltpu.SMEM((devices,), jnp.int32),
            pltpu.SemaphoreType.DMA((5,)),
        ],
        compiler_params=params(24),
        cost_estimate=cost(8 * rows * width * width),
        name="prepare",
    )(qt, k, vt, local_rows, slot_rows, slot_block, other_block, vid)

    swap = pl.pallas_call(
        swap_kernel,
        out_shape=shape((chips * br + extra, width), BF16),
        in_specs=[VMEM] * (1 + 2 * chips),
        out_specs=VMEM,
        compiler_params=params(24),
        cost_estimate=cost(2**20),
        name="swap_blocks",
    )(mask, *firsts, *seconds)
    swapped = to_other_core(swap, devices)

    def work(count):
        return [
            pltpu.VMEM((count, br, width), BF16),
            pltpu.VMEM((count, pairs, wide + EXTRA, br), BF16),
        ]

    tables = [
        pltpu.SMEM((blocks, slots), jnp.int32),
        pltpu.SMEM((blocks,), jnp.int32),
        pltpu.SMEM((2, slots + 1), jnp.int32),
    ]
    num, den = pl.pallas_call(
        near_kernel,
        out_shape=accumulators,
        in_specs=[ANY] * 2 + [VMEM] * (8 + 2 * (chips - 1)),
        out_specs=[VMEM] * 2,
        scratch_shapes=work(chips - 1) + tables + [pltpu.SemaphoreType.DMA((2,))],
        compiler_params=params(40),
        cost_estimate=cost(8 * rows * width * width),
        name="near_slots",
    )(
        slot_block, slot_count, mask, gain, wk, wvt, counts, qbd, num, den,
        *firsts[1:], *seconds[1:],
    )
    updated = pl.pallas_call(
        far_kernel,
        out_shape=shape((rows, width), BF16),
        in_specs=[ANY] * 4 + [VMEM] * (9 + chips),
        out_specs=VMEM,
        scratch_shapes=[
            pltpu.VMEM((blocks, width, br), F32),
            pltpu.VMEM((blocks, HEADS, br), F32),
        ]
        + work(chips)
        + [pltpu.VMEM((width, width), BF16), pltpu.VMEM((rows, width), BF16)]
        + tables
        + [pltpu.SemaphoreType.DMA((4,))],
        compiler_params=params(40),
        cost_estimate=cost(8 * rows * width * width),
        name="far_slots",
    )(
        slot_block, slot_count, project_out[0], x, swapped, gain, wk, wvt, counts, qbd, num, den,
        vcol, *seconds,
    )
    return to_next_segment(updated[None])


def solution(mesh):
    placed = (
        P("segment", "node", None),
        P("segment", None),
        P("segment", None, None),
        P("segment", None, None),
        P("segment", None, None),
        P("node", None),
        P(None, "node"),
        P("node", None),
        P("node"),
        P("node", None, None, None),
    )
    return jax.shard_map(
        body, mesh=mesh, in_specs=placed, out_specs=P("segment", "node", None), check_vma=False
    )
```

```python
import functools

import jax
import jax.numpy as jnp
from jax import lax
from jax.experimental import pallas as pl
from jax.experimental.pallas import tpu as pltpu
from jax.sharding import PartitionSpec as P

HEADS = 8
CORES = 2
EPSILON = 1e-05
CAP_LIMIT = 10.0
LOG2E = 1.4426950408889634
EXTRA = 16
F32 = jnp.float32
BF16 = jnp.bfloat16
HBM = pl.BlockSpec(memory_space=pltpu.HBM)
VMEM = pl.BlockSpec(memory_space=pltpu.VMEM)


def ring_order(chips):
    return list(range(0, 1)) + list(range(1, chips, 2)) + list(range((chips - 1) // 2 * 2, 0, -2))


def ring_place(chip, chips):
    return jnp.where(chip % 2 == 1, (chip + 1) // 2, (chips - chip // 2) % chips)


def to_next_chip(value, devices, way):
    chips = devices // CORES
    order = ring_order(chips)
    pairs = [
        (order[i] * CORES + c, order[(i + way) % chips] * CORES + c)
        for i in range(chips)
        for c in range(CORES)
    ]
    return lax.ppermute(value, "node", pairs)


def to_other_core(value, devices):
    return lax.ppermute(value, "node", [(d, d ^ 1) for d in range(devices)])


def to_next_segment(value):
    count = lax.axis_size("segment")
    return lax.ppermute(value, "segment", [(s, (s + 1) % count) for s in range(count)])


def norm_rows(rows_in, gain_row):
    widened = rows_in.astype(F32)
    center = widened - jnp.mean(widened, axis=-1, keepdims=True)
    spread = jnp.mean(center * center, axis=-1, keepdims=True)
    return (center * lax.rsqrt(spread + EPSILON) * gain_row).astype(BF16)


def exp_capped(raw, scale):
    return jnp.exp2((CAP_LIMIT * LOG2E) * jnp.tanh(raw * (scale / CAP_LIMIT)))


def counts_of(index_rows, block_rows):
    rows = lax.broadcasted_iota(jnp.int32, (block_rows, index_rows.shape[1]), 0)
    total = jnp.zeros(rows.shape, F32)
    for j in range(index_rows.shape[0]):
        total = total + jnp.where(index_rows[j : j + 1, :] == rows, 1.0, 0.0)
    return total


def mm(a, b):
    return jnp.dot(a, b, preferred_element_type=F32)


def mm_nt(a, b):
    return lax.dot_general(a, b, (((1,), (1,)), ((), ())), preferred_element_type=F32)


def halves(value):
    high = value.astype(BF16)
    return high, (value - high.astype(F32)).astype(BF16)


def choose(mask_row, first, second):
    rows, width = first.shape
    lanes = mask_row.shape[1]
    mask = jnp.broadcast_to(mask_row, (rows, lanes))
    mask = jnp.concatenate([mask] * (width // lanes), axis=1)
    return jnp.where(mask > 0.5, second.astype(F32), first.astype(F32)).astype(first.dtype)


def start_copies(pairs, sems):
    copies = [pltpu.make_async_copy(src, dst, sems.at[i]) for i, (src, dst) in enumerate(pairs)]
    for copy in copies:
        copy.start()
    return copies


def block_pair(refs, br):
    if len(refs) == 2:
        return refs[0][...], refs[1][:br, :]
    return refs[0][:br, :], refs[0][br : 2 * br, :]


def tail_sum(refs, extra):
    last = refs[-1]
    part = last[last.shape[0] - extra :, :].astype(F32)
    return part[: extra // 2] + part[extra // 2 :]


def deal(refs, sizes):
    groups = []
    for size in sizes:
        groups.append(refs[:size])
        refs = refs[size:]
    return groups


def own_kernel(
    x_hbm, gain_hbm, win_hbm, vk_hbm, vid_hbm,
    normed_ref, k_ref, v_ref, gain_ref, load_ref, second_ref,
    x_ref, wk_ref, wv_ref, vk_ref, vid_ref, sems,
):
    rows, width = x_ref.shape
    virtual = vk_ref.shape[0]
    scale = (width // HEADS) ** (-0.5)
    copies = start_copies(
        [
            (x_hbm, x_ref), (gain_hbm, gain_ref),
            (win_hbm.at[:, width : 2 * width], wk_ref), (win_hbm.at[:, 2 * width :], wv_ref),
            (vk_hbm, vk_ref), (vid_hbm, vid_ref),
        ],
        sems,
    )
    copies[0].wait()
    copies[1].wait()
    normed = norm_rows(x_ref[...], gain_ref[...])
    normed_ref[...] = normed
    for copy in copies[2:]:
        copy.wait()
    k = mm(normed, wk_ref[...]).astype(BF16)
    v = mm(normed, wv_ref[...]).astype(BF16)
    k_ref[...] = k
    v_ref[...] = v

    head_of_lane = lax.broadcasted_iota(jnp.int32, (HEADS, width), 1) // (width // HEADS)
    own_head = head_of_lane == lax.broadcasted_iota(jnp.int32, (HEADS, width), 0)
    vkf = vk_ref[...].astype(F32)
    vkbd = jnp.concatenate(
        [
            jnp.where(own_head, jnp.broadcast_to(vkf[j : j + 1, :], (HEADS, width)), 0.0)
            for j in range(virtual)
        ],
        axis=0,
    ).astype(BF16)
    raw = mm_nt(vkbd, k)
    owner = lax.broadcasted_iota(jnp.int32, raw.shape, 0) // HEADS
    pool_w = jnp.where(vid_ref[...] == owner, exp_capped(raw, scale), 0.0).astype(BF16)
    pool_num = mm(pool_w, v)
    pool_den = mm(pool_w, jnp.ones((rows, width), BF16))
    parts = [
        jnp.sum(jnp.where(own_head, whole[j * HEADS : (j + 1) * HEADS], 0.0), axis=0, keepdims=True)
        for whole in (pool_num, pool_den)
        for j in range(virtual)
    ]
    high, low = halves(jnp.concatenate(parts, axis=0))
    tail = jnp.concatenate([high.astype(F32), low.astype(F32)], axis=0).astype(BF16)
    br = second_ref.shape[0] - 4 * virtual
    load_ref[:rows, :] = x_ref[...]
    load_ref[rows:, :] = tail
    second_ref[:br, :] = x_ref[rows - br :, :]
    second_ref[br:, :] = tail


def attend(keys, values, counts, qbd, scale):
    p = (counts * exp_capped(mm(keys, qbd), scale)).astype(BF16)
    return mm(values, p)


def fold(o, num_ref, den_ref, b, t, add):
    wide = o.shape[0] - EXTRA
    head = wide // 2
    br = o.shape[1] // 2
    r0 = t * wide
    places = (
        (num_ref, slice(r0, r0 + head), o[:head, :br]),
        (num_ref, slice(r0 + head, r0 + wide), o[head:wide, br:]),
        (den_ref, slice(2 * t, 2 * t + 1), o[wide : wide + 1, :br]),
        (den_ref, slice(2 * t + 1, 2 * t + 2), o[wide : wide + 1, br:]),
    )
    for ref, part, value in places:
        if add:
            ref[b, part, :] += value
        else:
            ref[b, part, :] = value


def prep_kernel(
    normed_ref, k_ref, v_ref, win_hbm, lrows_hbm, srows_hbm, sblock_hbm, scount_hbm, other_hbm,
    vid_hbm, wo_hbm,
    qbd_ref, num_ref, den_ref, counts_ref, mask_ref, vcol_ref, wk_ref, wvt_ref, wo_ref,
    wq_ref, wv_ref, lrows_ref, srows_ref, vid_ref, sblock_ref, scount_ref, other_ref, want_ref,
    sems,
):
    rows, width = normed_ref.shape
    blocks, pairs, wide, _ = qbd_ref.shape
    chips = mask_ref.shape[1]
    slots = sblock_ref.shape[1]
    br = rows // blocks
    head = width // HEADS
    scale = head ** (-0.5)
    copies = start_copies(
        [
            (sblock_hbm, sblock_ref), (scount_hbm, scount_ref), (other_hbm, other_ref),
            (win_hbm.at[:, :width], wq_ref), (lrows_hbm, lrows_ref), (srows_hbm, srows_ref),
            (vid_hbm, vid_ref), (win_hbm.at[:, width : 2 * width], wk_ref),
            (win_hbm.at[:, 2 * width :], wv_ref), (wo_hbm, wo_ref),
        ],
        sems,
    )
    counts_ref[...] = jnp.zeros(counts_ref.shape, F32)
    for copy in copies:
        copy.wait()
    me = lax.axis_index("node")
    place = ring_place(me // CORES, chips)
    core = me % CORES
    for which, table in enumerate((sblock_ref, other_ref)):
        for d in range(chips * CORES):
            want_ref[d] = 0
        for b in range(blocks):
            for e in range(slots):
                entry = table[b, e]
                want_ref[entry // blocks] = entry % blocks
        for z in range(chips):
            step = (place - ring_place(jnp.int32(z), chips) + chips) % chips
            value = want_ref[z * CORES + core].astype(F32)
            mask_ref[which, step] = jnp.full(mask_ref.shape[2:], value, F32)
    for b in range(blocks):
        for e in range(slots):
            device = sblock_ref[b, e] // blocks
            step = (place - ring_place(device // CORES, chips) + chips) % chips
            far = jnp.where(device % CORES == core, 0, 1)
            live = jnp.where(e < scount_ref[b], 1.0, 0.0).astype(F32)
            counts_ref[far, step, b] += counts_of(srows_ref[b, e], br) * live

    vcol_ref[...] = jnp.broadcast_to(vid_ref[...].astype(F32), (128, rows)).T
    wvt_ref[...] = wv_ref[...].T
    qt = mm(normed_ref[...], wq_ref[...]).astype(BF16).T
    vt = v_ref[...].T
    zero = jnp.zeros((head, br), BF16)
    ones = jnp.ones((EXTRA, br), BF16)
    for b in range(blocks):
        cols = slice(b * br, (b + 1) * br)
        counts = counts_of(lrows_ref[:, cols], br)
        counts2 = jnp.concatenate([counts, counts], axis=1)
        for t in range(pairs):
            r0 = t * wide
            mid = r0 + head
            end = r0 + wide
            bd = jnp.concatenate(
                [
                    jnp.concatenate([qt[r0:mid, cols], zero], axis=1),
                    jnp.concatenate([zero, qt[mid:end, cols]], axis=1),
                ],
                axis=0,
            )
            qbd_ref[b, t] = bd
            values = jnp.concatenate([vt[r0:end, cols], ones], axis=0)
            fold(attend(k_ref[cols, r0:end], values, counts2, bd, scale), num_ref, den_ref, b, t, False)


def swap_kernel(steps, sizes, br, mask_ref, *refs):
    out_ref = refs[-1]
    for i, (step, pieces) in enumerate(zip(steps, deal(refs, sizes))):
        first, second = block_pair(pieces, br)
        out_ref[i * br : (i + 1) * br, :] = choose(mask_ref[1, step, :1, :], first, second)


def last_swap_kernel(steps, sizes, br, mask_ref, *refs):
    out_ref, total_ref = refs[-2:]
    swap_kernel(steps, sizes[: len(steps)], br, mask_ref, *refs[: sum(sizes[: len(steps)])], out_ref)
    extra = 2 * total_ref.shape[0]
    total = jnp.zeros(total_ref.shape, F32)
    for pieces in deal(refs, sizes):
        total = total + tail_sum(pieces, extra)
    total_ref[...] = total
    high, low = halves(total)
    out_ref[len(steps) * br :, :] = jnp.concatenate(
        [high.astype(F32), low.astype(F32)], axis=0
    ).astype(BF16)


def project(xs, start, gain_ref, wk_ref, wvt_ref, k_ref, vt_ref):
    normed = norm_rows(jnp.concatenate(xs, axis=0), gain_ref[...])
    part = slice(start, start + normed.shape[0])
    k_ref[part, :] = mm(normed, wk_ref[...]).astype(BF16)
    vt_ref[:, part] = mm_nt(wvt_ref[...], normed).astype(BF16)


def add_sources(names, start, b, counts_ref, qbd_ref, k_ref, vt_ref, num_ref, den_ref):
    _, pairs, wide, _ = qbd_ref.shape
    scale = (2 / wide) ** 0.5
    counts = jnp.concatenate([counts_ref[far, step, b] for far, step in names], axis=0)
    part = slice(start, start + counts.shape[0])
    counts2 = jnp.concatenate([counts, counts], axis=1)
    ones = jnp.ones((EXTRA, counts.shape[0]), BF16)
    for t in range(pairs):
        cols = slice(t * wide, (t + 1) * wide)
        values = jnp.concatenate([vt_ref[cols, part], ones], axis=0)
        o = attend(k_ref[part, cols], values, counts2, qbd_ref[b, t], scale)
        fold(o, num_ref, den_ref, b, t, True)


def slots_kernel(
    names, sizes, chunk, mask_ref, gain_ref, wk_ref, wvt_ref, counts_ref, qbd_ref, num_in, den_in,
    *refs
):
    num_ref, den_ref, k_ref, vt_ref = refs[-4:]
    groups = deal(refs, sizes)
    blocks, _, br = num_ref.shape
    num_ref[...] = num_in[...]
    den_ref[...] = den_in[...]
    xs = []
    chosen = 0
    for far, step in names:
        if far:
            xs.append(groups[-1][0][chosen * br : (chosen + 1) * br, :])
            chosen += 1
        else:
            first, second = block_pair(groups[len(xs)], br)
            xs.append(choose(mask_ref[0, step, :1, :], first, second))
    for s in range(0, len(names), chunk):
        project(xs[s : s + chunk], s * br, gain_ref, wk_ref, wvt_ref, k_ref, vt_ref)
        for b in range(blocks):
            add_sources(
                names[s : s + chunk], s * br, b, counts_ref, qbd_ref, k_ref, vt_ref, num_ref, den_ref
            )


def finish_kernel(names, chunk, b, lead, *refs):
    if lead:
        (
            swapped_ref, gain_ref, wk_ref, wvt_ref, counts_ref, qbd_ref, num_in, den_in,
            total_ref, vcol_ref, load_ref, wo_ref, out_ref, k_ref, vt_ref, num_ref, den_ref,
        ) = refs
    else:
        (
            swapped_ref, k_ref, vt_ref, counts_ref, qbd_ref, num_in, den_in,
            total_ref, vcol_ref, load_ref, wo_ref, out_ref, num_ref, den_ref,
        ) = refs
    _, width, br = num_ref.shape
    head = width // HEADS
    num_ref[b] = num_in[b]
    den_ref[b] = den_in[b]
    for s in range(0, len(names), chunk):
        some = names[s : s + chunk]
        if lead:
            xs = [swapped_ref[(s + i) * br : (s + i + 1) * br, :] for i in range(len(some))]
            project(xs, s * br, gain_ref, wk_ref, wvt_ref, k_ref, vt_ref)
        add_sources(some, s * br, b, counts_ref, qbd_ref, k_ref, vt_ref, num_ref, den_ref)
    half = total_ref.shape[0]
    total = total_ref[...] + tail_sum([swapped_ref], 2 * half)
    virtual = half // 2
    pooled = total[:virtual] / total[virtual:]
    lanes = vcol_ref.shape[1]
    part = slice(b * br, (b + 1) * br)
    vid = vcol_ref[part, :]
    att = jnp.concatenate(
        [
            num_ref[b, h * head : (h + 1) * head, :] / den_ref[b, h : h + 1, :]
            for h in range(HEADS)
        ],
        axis=0,
    ).T
    pieces = []
    for c in range(0, width, lanes):
        own = jnp.broadcast_to(pooled[0:1, c : c + lanes], (br, lanes))
        for j in range(1, virtual):
            own = jnp.where(vid == float(j), pooled[j : j + 1, c : c + lanes], own)
        pieces.append((att[:, c : c + lanes] + own).astype(BF16))
    mixed = jnp.concatenate(pieces, axis=1)
    out_ref[...] = (load_ref[part, :].astype(F32) + mm(mixed, wo_ref[...])).astype(BF16)


def params(mib):
    return pltpu.CompilerParams(vmem_limit_bytes=mib * 2**20)


def cost(flops):
    return pl.CostEstimate(flops=flops, bytes_accessed=2**20, transcendentals=flops // 1024)


def body(
    activations,
    norm_gain,
    project_in,
    project_out,
    virtual_keys,
    virtual_id,
    local_rows,
    slot_block,
    slot_count,
    slot_rows,
):
    _, rows, width = activations.shape
    br = slot_rows.shape[3]
    slots = slot_block.shape[1]
    blocks = rows // br
    devices = lax.axis_size("node")
    chips = devices // CORES
    virtual = virtual_keys.shape[1]
    pairs = HEADS // 2
    wide = width // pairs
    extra = 4 * virtual
    shape = jax.ShapeDtypeStruct
    x = activations[0]
    vid = virtual_id.reshape(1, rows)
    unit = 8 * rows * width * width

    ahead = chips // 2
    firsts = [x[:br]]
    firsts.append(to_next_chip(firsts[0], devices, 1))
    other_block = to_other_core(slot_block, devices)
    normed, k, v, gain, load, second = pl.pallas_call(
        own_kernel,
        out_shape=(
            shape((rows, width), BF16),
            shape((rows, width), BF16),
            shape((rows, width), BF16),
            shape((1, width), F32),
            shape((rows + extra, width), BF16),
            shape((br + extra, width), BF16),
        ),
        in_specs=[HBM] * 5,
        out_specs=[VMEM] * 6,
        scratch_shapes=[
            pltpu.VMEM((rows, width), BF16),
            pltpu.VMEM((width, width), BF16),
            pltpu.VMEM((width, width), BF16),
            pltpu.VMEM((virtual, width), BF16),
            pltpu.VMEM((1, rows), jnp.int32),
            pltpu.SemaphoreType.DMA((6,)),
        ],
        compiler_params=params(24),
        cost_estimate=cost(unit),
        name="own_rows",
    )(x, norm_gain, project_in[0], virtual_keys[0], vid)
    arrived = {0: (load,)}
    seconds = [second, to_next_chip(second, devices, 1)]
    backward = load
    for j in range(1, chips - ahead):
        backward = to_next_chip(backward, devices, -1)
        arrived[chips - j] = (backward,)
    for s in range(1, ahead + 1):
        if s > 1:
            firsts.append(to_next_chip(firsts[-1], devices, 1))
            seconds.append(to_next_chip(seconds[-1], devices, 1))
        arrived[s] = (firsts[s], seconds[s])

    accumulators = (shape((blocks, width, br), F32), shape((blocks, HEADS, br), F32))
    qbd, num, den, counts, mask, vcol, wk, wvt, wo = pl.pallas_call(
        prep_kernel,
        out_shape=(
            (shape((blocks, pairs, wide, 2 * br), BF16),)
            + accumulators
            + (
                shape((CORES, chips, blocks, br, br), F32),
                shape((CORES, chips, 8, 128), F32),
                shape((rows, 128), F32),
                shape((width, width), BF16),
                shape((width, width), BF16),
                shape((width, width), BF16),
            )
        ),
        in_specs=[VMEM] * 3 + [HBM] * 8,
        out_specs=[VMEM] * 9,
        scratch_shapes=[
            pltpu.VMEM((width, width), BF16),
            pltpu.VMEM((width, width), BF16),
            pltpu.VMEM(local_rows.shape, jnp.int32),
            pltpu.VMEM(slot_rows.shape, jnp.int32),
            pltpu.VMEM((1, rows), jnp.int32),
            pltpu.SMEM((blocks, slots), jnp.int32),
            pltpu.SMEM((blocks,), jnp.int32),
            pltpu.SMEM((blocks, slots), jnp.int32),
            pltpu.SMEM((devices,), jnp.int32),
            pltpu.SemaphoreType.DMA((10,)),
        ],
        compiler_params=params(32),
        cost_estimate=cost(unit),
        name="prepare",
    )(
        normed, k, v, project_in[0], local_rows, slot_rows, slot_block, slot_count, other_block,
        vid, project_out[0],
    )

    def swap(steps, last):
        sources = [arrived[s] for s in steps]
        if last:
            sources += [arrived[s] for s in range(chips) if s not in steps]
        sizes = tuple(len(source) for source in sources)
        count = len(steps)
        outs = [shape((count * br + (extra if last else 0), width), BF16)]
        if last:
            outs.append(shape((extra // 2, width), F32))
        outs = pl.pallas_call(
            functools.partial(last_swap_kernel if last else swap_kernel, tuple(steps), sizes, br),
            out_shape=tuple(outs),
            in_specs=[VMEM] * (1 + sum(sizes)),
            out_specs=tuple([VMEM] * len(outs)),
            compiler_params=params(24),
            cost_estimate=cost(2**20),
            name="last_swap" if last else "first_swap",
        )(mask, *[ref for source in sources for ref in source])
        return [to_other_core(outs[0], devices)] + list(outs[1:])

    def slots_call(names, swapped, num, den, name):
        sources = [arrived[s] for far, s in names if not far]
        sources += [] if swapped is None else [(swapped,)]
        sizes = tuple(len(source) for source in sources)
        return pl.pallas_call(
            functools.partial(slots_kernel, tuple(names), sizes, 4),
            out_shape=accumulators,
            in_specs=[VMEM] * (8 + sum(sizes)),
            out_specs=[VMEM] * 2,
            scratch_shapes=[
                pltpu.VMEM((len(names) * br, width), BF16),
                pltpu.VMEM((width, len(names) * br), BF16),
            ],
            compiler_params=params(40),
            cost_estimate=cost(unit),
            name=name,
        )(
            mask, gain, wk, wvt, counts, qbd, num, den,
            *[ref for source in sources for ref in source],
        )

    (swapped,) = swap((0, 1), False)
    num, den = slots_call([(0, 1), (1, 0), (1, 1)], swapped, num, den, "first_slots")
    late = tuple(range(2, chips))
    swapped, total = swap(late, True)
    num, den = slots_call([(0, s) for s in late], None, num, den, "near_slots")
    names = tuple((1, s) for s in late)
    out_shape = shape((br, width), BF16)
    shared = (counts, qbd, num, den, total, vcol, load, wo)
    sums = [pltpu.VMEM((blocks, width, br), F32), pltpu.VMEM((blocks, HEADS, br), F32)]
    results = []
    for b in range(blocks):
        lead = b == 0
        kernel = functools.partial(finish_kernel, names, 4, b, lead)
        if lead:
            result, far_k, far_vt = pl.pallas_call(
                kernel,
                out_shape=(
                    out_shape,
                    shape((len(late) * br, width), BF16),
                    shape((width, len(late) * br), BF16),
                ),
                in_specs=[VMEM] * 12,
                out_specs=[VMEM] * 3,
                scratch_shapes=sums,
                compiler_params=params(40),
                cost_estimate=cost(unit // 2),
                name="finish_first",
            )(swapped, gain, wk, wvt, *shared)
        else:
            result = pl.pallas_call(
                kernel,
                out_shape=out_shape,
                in_specs=[VMEM] * 11,
                out_specs=VMEM,
                scratch_shapes=sums,
                compiler_params=params(40),
                cost_estimate=cost(unit // 2),
                name="finish_rest",
            )(swapped, far_k, far_vt, *shared)
        results.append(to_next_segment(result))
    return jnp.concatenate(results, axis=0)[None]


def solution(mesh):
    placed = (
        P("segment", "node", None),
        P("segment", None),
        P("segment", None, None),
        P("segment", None, None),
        P("segment", None, None),
        P("node", None),
        P(None, "node"),
        P("node", None),
        P("node"),
        P("node", None, None, None),
    )
    return jax.shard_map(
        body, mesh=mesh, in_specs=placed, out_specs=P("segment", "node", None), check_vma=False
    )
```

```python
import functools

import jax
import jax.numpy as jnp
from jax import lax
from jax.experimental import pallas as pl
from jax.experimental.pallas import tpu as pltpu
from jax.sharding import PartitionSpec as P

HEADS = 8
CORES = 2
EPSILON = 1e-05
CAP_LIMIT = 10.0
LOG2E = 1.4426950408889634
EXTRA = 16
F32 = jnp.float32
BF16 = jnp.bfloat16
HBM = pl.BlockSpec(memory_space=pltpu.HBM)
VMEM = pl.BlockSpec(memory_space=pltpu.VMEM)


def ring_order(chips):
    return list(range(0, 1)) + list(range(1, chips, 2)) + list(range((chips - 1) // 2 * 2, 0, -2))


def ring_place(chip, chips):
    return jnp.where(chip % 2 == 1, (chip + 1) // 2, (chips - chip // 2) % chips)


def to_next_chip(value, devices, way):
    chips = devices // CORES
    order = ring_order(chips)
    pairs = [
        (order[i] * CORES + c, order[(i + way) % chips] * CORES + c)
        for i in range(chips)
        for c in range(CORES)
    ]
    return lax.ppermute(value, "node", pairs)


def swapped(value, devices, distance):
    return lax.ppermute(value, "node", [(d, d ^ distance) for d in range(devices)])


def to_next_segment(value):
    count = lax.axis_size("segment")
    return lax.ppermute(value, "segment", [(s, (s + 1) % count) for s in range(count)])


def norm_rows(rows_in, gain_row):
    widened = rows_in.astype(F32)
    center = widened - jnp.mean(widened, axis=-1, keepdims=True)
    spread = jnp.mean(center * center, axis=-1, keepdims=True)
    return (center * lax.rsqrt(spread + EPSILON) * gain_row).astype(BF16)


def exp_capped(raw, scale):
    return jnp.exp2((CAP_LIMIT * LOG2E) * jnp.tanh(raw * (scale / CAP_LIMIT)))


def counts_of(index_rows, block_rows):
    rows = lax.broadcasted_iota(jnp.int32, (block_rows, index_rows.shape[1]), 0)
    total = jnp.zeros(rows.shape, F32)
    for j in range(index_rows.shape[0]):
        total = total + jnp.where(index_rows[j : j + 1, :] == rows, 1.0, 0.0)
    return total


def mm(a, b):
    return jnp.dot(a, b, preferred_element_type=F32)


def mm_nt(a, b):
    return lax.dot_general(a, b, (((1,), (1,)), ((), ())), preferred_element_type=F32)


def choose(mask_row, rows_ref, br):
    _, width = rows_ref.shape
    lanes = mask_row.shape[1]
    mask = jnp.broadcast_to(mask_row, (br, lanes))
    mask = jnp.concatenate([mask] * (width // lanes), axis=1)
    picked = rows_ref[:br, :].astype(F32)
    for block in range(1, rows_ref.shape[0] // br):
        other = rows_ref[block * br : (block + 1) * br, :].astype(F32)
        picked = jnp.where(mask == float(block), other, picked)
    return picked.astype(BF16)


def start_copies(pairs, sems):
    copies = [pltpu.make_async_copy(src, dst, sems.at[i]) for i, (src, dst) in enumerate(pairs)]
    for copy in copies:
        copy.start()
    return copies


def own_kernel(
    x_hbm, gain_hbm, win_hbm, vk_hbm, vid_hbm,
    normed_ref, k_ref, v_ref, gain_ref, pool_ref,
    x_ref, wk_ref, wv_ref, vk_ref, vid_ref, sems,
):
    rows, width = x_ref.shape
    virtual = vk_ref.shape[0]
    scale = (width // HEADS) ** (-0.5)
    copies = start_copies(
        [
            (x_hbm, x_ref), (gain_hbm, gain_ref),
            (win_hbm.at[:, width : 2 * width], wk_ref), (win_hbm.at[:, 2 * width :], wv_ref),
            (vk_hbm, vk_ref), (vid_hbm, vid_ref),
        ],
        sems,
    )
    copies[0].wait()
    copies[1].wait()
    normed = norm_rows(x_ref[...], gain_ref[...])
    normed_ref[...] = normed
    for copy in copies[2:]:
        copy.wait()
    k = mm(normed, wk_ref[...]).astype(BF16)
    v = mm(normed, wv_ref[...]).astype(BF16)
    k_ref[...] = k
    v_ref[...] = v

    head_of_lane = lax.broadcasted_iota(jnp.int32, (HEADS, width), 1) // (width // HEADS)
    own_head = head_of_lane == lax.broadcasted_iota(jnp.int32, (HEADS, width), 0)
    vkf = vk_ref[...].astype(F32)
    vkbd = jnp.concatenate(
        [
            jnp.where(own_head, jnp.broadcast_to(vkf[j : j + 1, :], (HEADS, width)), 0.0)
            for j in range(virtual)
        ],
        axis=0,
    ).astype(BF16)
    raw = mm_nt(vkbd, k)
    owner = lax.broadcasted_iota(jnp.int32, raw.shape, 0) // HEADS
    pool_w = jnp.where(vid_ref[...] == owner, exp_capped(raw, scale), 0.0).astype(BF16)
    pool_num = mm(pool_w, v)
    pool_den = mm(pool_w, jnp.ones((rows, width), BF16))
    parts = [
        jnp.sum(jnp.where(own_head, whole[j * HEADS : (j + 1) * HEADS], 0.0), axis=0, keepdims=True)
        for whole in (pool_num, pool_den)
        for j in range(virtual)
    ]
    pool_ref[...] = jnp.concatenate(parts, axis=0)


def attend(keys, values, counts, qbd, scale):
    p = (counts * exp_capped(mm(keys, qbd), scale)).astype(BF16)
    return mm(values, p)


def fold(o, num_ref, den_ref, b, t, add):
    wide = o.shape[0] - EXTRA
    head = wide // 2
    br = o.shape[1] // 2
    r0 = t * wide
    places = (
        (num_ref, slice(r0, r0 + head), o[:head, :br]),
        (num_ref, slice(r0 + head, r0 + wide), o[head:wide, br:]),
        (den_ref, slice(2 * t, 2 * t + 1), o[wide : wide + 1, :br]),
        (den_ref, slice(2 * t + 1, 2 * t + 2), o[wide : wide + 1, br:]),
    )
    for ref, part, value in places:
        if add:
            ref[b, part, :] += value
        else:
            ref[b, part, :] = value


def prep_kernel(
    normed_ref, k_ref, v_ref, win_hbm, lrows_hbm, srows_hbm, sblock_hbm, scount_hbm, vid_hbm, wo_hbm,
    qbd_ref, num_ref, den_ref, counts_ref, mask_ref, vcol_ref, wk_ref, wvt_ref, wo_ref,
    wq_ref, wv_ref, lrows_ref, srows_ref, vid_ref, sblock_ref, scount_ref, want_ref, sems,
):
    rows, width = normed_ref.shape
    blocks, pairs, wide, _ = qbd_ref.shape
    chips = mask_ref.shape[1]
    slots = sblock_ref.shape[1]
    br = rows // blocks
    head = width // HEADS
    scale = head ** (-0.5)
    copies = start_copies(
        [
            (sblock_hbm, sblock_ref), (scount_hbm, scount_ref),
            (win_hbm.at[:, :width], wq_ref), (lrows_hbm, lrows_ref), (srows_hbm, srows_ref),
            (vid_hbm, vid_ref), (win_hbm.at[:, width : 2 * width], wk_ref),
            (win_hbm.at[:, 2 * width :], wv_ref), (wo_hbm, wo_ref),
        ],
        sems,
    )
    counts_ref[...] = jnp.zeros(counts_ref.shape, F32)
    for copy in copies:
        copy.wait()
    me = lax.axis_index("node")
    place = ring_place(me // CORES, chips)
    core = me % CORES
    for d in range(chips * CORES):
        want_ref[d] = 0
    for b in range(blocks):
        for e in range(slots):
            entry = sblock_ref[b, e]
            want_ref[entry // blocks] = entry % blocks
    for d in range(chips * CORES):
        step = (place - ring_place(jnp.int32(d // CORES), chips) + chips) % chips
        far = jnp.where(core == d % CORES, 0, 1)
        mask_ref[far, step] = jnp.full(mask_ref.shape[2:], want_ref[d].astype(F32), F32)
    for b in range(blocks):
        for e in range(slots):
            device = sblock_ref[b, e] // blocks
            step = (place - ring_place(device // CORES, chips) + chips) % chips
            far = jnp.where(device % CORES == core, 0, 1)
            live = jnp.where(e < scount_ref[b], 1.0, 0.0).astype(F32)
            counts_ref[far, step, b] += counts_of(srows_ref[b, e], br) * live

    vcol_ref[...] = jnp.broadcast_to(vid_ref[...].astype(F32), (128, rows)).T
    wvt_ref[...] = wv_ref[...].T
    qt = mm(normed_ref[...], wq_ref[...]).astype(BF16).T
    vt = v_ref[...].T
    zero = jnp.zeros((head, br), BF16)
    ones = jnp.ones((EXTRA, br), BF16)
    for b in range(blocks):
        cols = slice(b * br, (b + 1) * br)
        counts = counts_of(lrows_ref[:, cols], br)
        counts2 = jnp.concatenate([counts, counts], axis=1)
        for t in range(pairs):
            r0 = t * wide
            mid = r0 + head
            end = r0 + wide
            bd = jnp.concatenate(
                [
                    jnp.concatenate([qt[r0:mid, cols], zero], axis=1),
                    jnp.concatenate([zero, qt[mid:end, cols]], axis=1),
                ],
                axis=0,
            )
            qbd_ref[b, t] = bd
            values = jnp.concatenate([vt[r0:end, cols], ones], axis=0)
            fold(attend(k_ref[cols, r0:end], values, counts2, bd, scale), num_ref, den_ref, b, t, False)


def project(xs, gain_ref, wk_ref, wvt_ref, k_ref, vt_ref):
    normed = norm_rows(jnp.concatenate(xs, axis=0), gain_ref[...])
    k_ref[...] = mm(normed, wk_ref[...]).astype(BF16)
    vt_ref[...] = mm_nt(wvt_ref[...], normed).astype(BF16)


def add_sources(names, b, counts_ref, qbd_ref, k_ref, vt_ref, num_ref, den_ref):
    _, pairs, wide, _ = qbd_ref.shape
    scale = (2 / wide) ** 0.5
    counts = jnp.concatenate([counts_ref[far, step, b] for far, step in names], axis=0)
    counts2 = jnp.concatenate([counts, counts], axis=1)
    ones = jnp.ones((EXTRA, counts.shape[0]), BF16)
    for t in range(pairs):
        cols = slice(t * wide, (t + 1) * wide)
        values = jnp.concatenate([vt_ref[cols, :], ones], axis=0)
        o = attend(k_ref[:, cols], values, counts2, qbd_ref[b, t], scale)
        fold(o, num_ref, den_ref, b, t, True)


def slots_kernel(
    names, mask_ref, gain_ref, wk_ref, wvt_ref, counts_ref, qbd_ref, num_in, den_in, *refs
):
    num_ref, den_ref, k_ref, vt_ref = refs[len(names) :]
    blocks, _, br = num_ref.shape
    num_ref[...] = num_in[...]
    den_ref[...] = den_in[...]
    xs = [choose(mask_ref[far, step, :1, :], ref, br) for (far, step), ref in zip(names, refs)]
    project(xs, gain_ref, wk_ref, wvt_ref, k_ref, vt_ref)
    for b in range(blocks):
        add_sources(names, b, counts_ref, qbd_ref, k_ref, vt_ref, num_ref, den_ref)


def finish_kernel(names, b, lead, *refs):
    if lead:
        (
            mask_ref, rows_ref, gain_ref, wk_ref, wvt_ref, counts_ref, qbd_ref, num_in, den_in,
            total_ref, vcol_ref, x_ref, wo_ref, out_ref, k_ref, vt_ref, num_ref, den_ref,
        ) = refs
    else:
        (
            k_ref, vt_ref, counts_ref, qbd_ref, num_in, den_in,
            total_ref, vcol_ref, x_ref, wo_ref, out_ref, num_ref, den_ref,
        ) = refs
    _, width, br = num_ref.shape
    head = width // HEADS
    num_ref[b] = num_in[b]
    den_ref[b] = den_in[b]
    if lead:
        xs = [choose(mask_ref[far, step, :1, :], rows_ref, br) for far, step in names]
        project(xs, gain_ref, wk_ref, wvt_ref, k_ref, vt_ref)
    add_sources(names, b, counts_ref, qbd_ref, k_ref, vt_ref, num_ref, den_ref)
    total = total_ref[...]
    virtual = total.shape[0] // 2
    pooled = total[:virtual] / total[virtual:]
    lanes = vcol_ref.shape[1]
    part = slice(b * br, (b + 1) * br)
    vid = vcol_ref[part, :]
    att = jnp.concatenate(
        [
            num_ref[b, h * head : (h + 1) * head, :] / den_ref[b, h : h + 1, :]
            for h in range(HEADS)
        ],
        axis=0,
    ).T
    pieces = []
    for c in range(0, width, lanes):
        own = jnp.broadcast_to(pooled[0:1, c : c + lanes], (br, lanes))
        for j in range(1, virtual):
            own = jnp.where(vid == float(j), pooled[j : j + 1, c : c + lanes], own)
        pieces.append((att[:, c : c + lanes] + own).astype(BF16))
    mixed = jnp.concatenate(pieces, axis=1)
    out_ref[...] = (x_ref[part, :].astype(F32) + mm(mixed, wo_ref[...])).astype(BF16)


def place_kernel(b, rows_ref, *refs):
    out_ref, sems = refs[-2:]
    br = rows_ref.shape[0]
    copy = pltpu.make_async_copy(rows_ref, out_ref.at[0, b * br : (b + 1) * br, :], sems.at[0])
    copy.start()
    copy.wait()


def params(mib):
    return pltpu.CompilerParams(vmem_limit_bytes=mib * 2**20)


def cost(flops):
    return pl.CostEstimate(flops=flops, bytes_accessed=1024, transcendentals=0)


def body(
    activations,
    norm_gain,
    project_in,
    project_out,
    virtual_keys,
    virtual_id,
    local_rows,
    slot_block,
    slot_count,
    slot_rows,
):
    _, rows, width = activations.shape
    br = slot_rows.shape[3]
    slots = slot_block.shape[1]
    blocks = rows // br
    devices = lax.axis_size("node")
    chips = devices // CORES
    virtual = virtual_keys.shape[1]
    pairs = HEADS // 2
    wide = width // pairs
    shape = jax.ShapeDtypeStruct
    after = lax.optimization_barrier
    x = activations[0]
    vid = virtual_id.reshape(1, rows)
    unit = 2**16

    near = {1: to_next_chip(x, devices, 1)}
    if chips > 2:
        near[chips - 1] = to_next_chip(x, devices, -1)
    far = {0: swapped(x, devices, 1)}
    normed, k, v, gain, pool = pl.pallas_call(
        own_kernel,
        out_shape=(
            shape((rows, width), BF16),
            shape((rows, width), BF16),
            shape((rows, width), BF16),
            shape((1, width), F32),
            shape((2 * virtual, width), F32),
        ),
        in_specs=[HBM] * 5,
        out_specs=[VMEM] * 5,
        scratch_shapes=[
            pltpu.VMEM((rows, width), BF16),
            pltpu.VMEM((width, width), BF16),
            pltpu.VMEM((width, width), BF16),
            pltpu.VMEM((virtual, width), BF16),
            pltpu.VMEM((1, rows), jnp.int32),
            pltpu.SemaphoreType.DMA((6,)),
        ],
        compiler_params=params(24),
        cost_estimate=cost(unit),
        name="own_rows",
    )(x, norm_gain, project_in[0], virtual_keys[0], vid)
    pool_in = swapped(pool, devices, 1)

    accumulators = (shape((blocks, width, br), F32), shape((blocks, HEADS, br), F32))
    qbd, num, den, counts, mask, vcol, wk, wvt, wo = pl.pallas_call(
        prep_kernel,
        out_shape=(
            (shape((blocks, pairs, wide, 2 * br), BF16),)
            + accumulators
            + (
                shape((CORES, chips, blocks, br, br), F32),
                shape((CORES, chips, 8, 128), F32),
                shape((rows, 128), F32),
                shape((width, width), BF16),
                shape((width, width), BF16),
                shape((width, width), BF16),
            )
        ),
        in_specs=[VMEM] * 3 + [HBM] * 7,
        out_specs=[VMEM] * 9,
        scratch_shapes=[
            pltpu.VMEM((width, width), BF16),
            pltpu.VMEM((width, width), BF16),
            pltpu.VMEM(local_rows.shape, jnp.int32),
            pltpu.VMEM(slot_rows.shape, jnp.int32),
            pltpu.VMEM((1, rows), jnp.int32),
            pltpu.SMEM((blocks, slots), jnp.int32),
            pltpu.SMEM((blocks,), jnp.int32),
            pltpu.SMEM((devices,), jnp.int32),
            pltpu.SemaphoreType.DMA((9,)),
        ],
        compiler_params=params(32),
        cost_estimate=cost(unit),
        name="prepare",
    )(
        normed, k, v, project_in[0], local_rows, slot_rows, slot_block, slot_count,
        vid, project_out[0],
    )

    def slots_call(names, num, den, name):
        return pl.pallas_call(
            functools.partial(slots_kernel, tuple(names)),
            out_shape=accumulators,
            in_specs=[VMEM] * (8 + len(names)),
            out_specs=[VMEM] * 2,
            scratch_shapes=[
                pltpu.VMEM((len(names) * br, width), BF16),
                pltpu.VMEM((width, len(names) * br), BF16),
            ],
            compiler_params=params(40),
            cost_estimate=cost(unit),
            name=name,
        )(
            mask, gain, wk, wvt, counts, qbd, num, den,
            *[(far if other else near)[step] for other, step in names],
        )

    ahead = chips // 2
    order = []
    for s in range(1, ahead + 1):
        order.append((s, 1))
        if s < chips - s:
            order.append((chips - s, -1))
    distance = 1
    for i, (step, way) in enumerate(order):
        last = i == len(order) - 1
        if distance < devices:
            pool_in, den = after((pool_in, den))
            pool = pool + pool_in
            distance *= 2
            if distance < devices:
                pool_in = swapped(pool, devices, distance)
        if i == 0 or last:
            near[step], den = after((near[step], den))
        nexts = step + way
        if nexts not in near and (nexts, way) in order:
            near[nexts] = to_next_chip(near[step], devices, way)
        far[step] = swapped(near[step], devices, 1)
        names = [(0, step)] if last else [(0, step), (1, step)]
        if i == 0:
            names = [(1, 0)] + names
        if i + 2 < len(order):
            ready = order[i + 1][0]
            near[ready], den = after((near[ready], den))
        num, den = slots_call(names, num, den, "slots_%d" % i)
    while distance < devices:
        pool = pool + pool_in
        distance *= 2
        if distance < devices:
            pool_in = swapped(pool, devices, distance)

    names = ((1, order[-1][0]),)
    out_shape = shape((br, width), BF16)
    shared = (counts, qbd, num, den, pool, vcol, x, wo)
    sums = [pltpu.VMEM((blocks, width, br), F32), pltpu.VMEM((blocks, HEADS, br), F32)]
    results = []
    for b in range(blocks):
        lead = b == 0
        kernel = functools.partial(finish_kernel, names, b, lead)
        if lead:
            result, far_k, far_vt = pl.pallas_call(
                kernel,
                out_shape=(out_shape, shape((br, width), BF16), shape((width, br), BF16)),
                in_specs=[VMEM] * 13,
                out_specs=[VMEM] * 3,
                scratch_shapes=sums,
                compiler_params=params(40),
                cost_estimate=cost(unit),
                name="finish_first",
            )(mask, far[names[0][1]], gain, wk, wvt, *shared)
        else:
            result = pl.pallas_call(
                kernel,
                out_shape=out_shape,
                in_specs=[VMEM] * 10,
                out_specs=VMEM,
                scratch_shapes=sums,
                compiler_params=params(40),
                cost_estimate=cost(unit),
                name="finish_rest",
            )(far_k, far_vt, *shared)
        results.append(result)
    results = [to_next_segment(result) for result in results]
    joined = None
    for b in range(blocks):
        earlier = [] if joined is None else [joined]
        joined = pl.pallas_call(
            functools.partial(place_kernel, b),
            out_shape=shape((1, rows, width), BF16),
            in_specs=[VMEM] + [HBM] * len(earlier),
            out_specs=HBM,
            scratch_shapes=[pltpu.SemaphoreType.DMA((1,))],
            input_output_aliases={1: 0} if earlier else {},
            compiler_params=params(24),
            cost_estimate=cost(unit),
            name="place_%d" % b,
        )(results[b], *earlier)
    return joined


def solution(mesh):
    placed = (
        P("segment", "node", None),
        P("segment", None),
        P("segment", None, None),
        P("segment", None, None),
        P("segment", None, None),
        P("node", None),
        P(None, "node"),
        P("node", None),
        P("node"),
        P("node", None, None, None),
    )
    return jax.shard_map(
        body, mesh=mesh, in_specs=placed, out_specs=P("segment", "node", None), check_vma=False
    )
```

```python
import functools

import jax
import jax.numpy as jnp
from jax import lax
from jax.experimental import pallas as pl
from jax.experimental.pallas import tpu as pltpu
from jax.sharding import PartitionSpec as P

HEADS = 8
CORES = 2
EPSILON = 1e-05
CAP_LIMIT = 10.0
LOG2E = 1.4426950408889634
EXTRA = 16
PACK_MIB = 60
PREP_MIB = 32
F32 = jnp.float32
BF16 = jnp.bfloat16
HBM = pl.BlockSpec(memory_space=pltpu.HBM)
VMEM = pl.BlockSpec(memory_space=pltpu.VMEM)


def ring_order(chips):
    return list(range(0, 1)) + list(range(1, chips, 2)) + list(range((chips - 1) // 2 * 2, 0, -2))


def ring_place(chip, chips):
    return jnp.where(chip % 2 == 1, (chip + 1) // 2, (chips - chip // 2) % chips)


def to_next_chip(value, devices, way):
    chips = devices // CORES
    order = ring_order(chips)
    pairs = [
        (order[i] * CORES + c, order[(i + way) % chips] * CORES + c)
        for i in range(chips)
        for c in range(CORES)
    ]
    return lax.ppermute(value, "node", pairs)


def swapped(value, devices, distance):
    return lax.ppermute(value, "node", [(d, d ^ distance) for d in range(devices)])


def to_next_segment(value):
    count = lax.axis_size("segment")
    return lax.ppermute(value, "segment", [(s, (s + 1) % count) for s in range(count)])


def norm_rows(rows_in, gain_row):
    widened = rows_in.astype(F32)
    center = widened - jnp.mean(widened, axis=-1, keepdims=True)
    spread = jnp.mean(center * center, axis=-1, keepdims=True)
    return (center * lax.rsqrt(spread + EPSILON) * gain_row).astype(BF16)


def exp_capped(raw, scale):
    return jnp.exp2((CAP_LIMIT * LOG2E) * jnp.tanh(raw * (scale / CAP_LIMIT)))


def counts_of(index_rows, block_rows):
    rows = lax.broadcasted_iota(jnp.int32, (block_rows, index_rows.shape[1]), 0)
    total = jnp.zeros(rows.shape, F32)
    for j in range(index_rows.shape[0]):
        total = total + jnp.where(index_rows[j : j + 1, :] == rows, 1.0, 0.0)
    return total


def mm(a, b):
    return jnp.dot(a, b, preferred_element_type=F32)


def mm_nt(a, b):
    return lax.dot_general(a, b, (((1,), (1,)), ((), ())), preferred_element_type=F32)


def choose(mask_row, rows):
    lanes = mask_row.shape[1]
    count, width = rows.shape
    br = count // 2
    mask = jnp.broadcast_to(mask_row, (br, lanes))
    mask = jnp.concatenate([mask] * (width // lanes), axis=1)
    first, second = rows[:br, :].astype(F32), rows[br:, :].astype(F32)
    return jnp.where(mask > 0.5, second, first).astype(rows.dtype)


def halves(value):
    high = value.astype(BF16)
    low = (value - high.astype(F32)).astype(BF16)
    return jnp.concatenate([high, low], axis=0)


def of_own_head(shape):
    head = lax.broadcasted_iota(jnp.int32, shape, 0) % HEADS
    return head == lax.broadcasted_iota(jnp.int32, shape, 1) // (shape[1] // HEADS)


def add_pool(normed, vid_row, vkw_ref, pool_ref, weight_ref, scale, first):
    count = pool_ref.shape[0]
    raw = mm_nt(vkw_ref[...], normed)
    raw = raw[:count] + raw[count:]
    owner = lax.broadcasted_iota(jnp.int32, raw.shape, 0) // HEADS
    w = jnp.where(vid_row == owner.astype(F32), exp_capped(raw, scale), 0.0).astype(BF16)
    sums = mm(w, normed)
    totals = jnp.broadcast_to(
        jnp.sum(w.astype(F32), axis=1, keepdims=True), weight_ref.shape
    )
    pool_ref[...] = sums if first else pool_ref[...] + sums
    weight_ref[...] = totals if first else weight_ref[...] + totals


def start_copies(pairs, sems):
    copies = [pltpu.make_async_copy(src, dst, sems.at[i]) for i, (src, dst) in enumerate(pairs)]
    for copy in copies:
        copy.start()
    return copies


def pack_kernel(x_hbm, vid_hbm, load_ref, vid_ref, sems):
    rows = vid_ref.shape[1]
    copies = start_copies([(x_hbm, load_ref.at[:rows, :]), (vid_hbm, vid_ref)], sems)
    copies[1].wait()
    tile = jnp.broadcast_to(vid_ref[...].astype(F32), (EXTRA, rows))
    rest = jnp.zeros((EXTRA, load_ref.shape[1] - rows), F32)
    load_ref[rows:, :] = jnp.concatenate([tile, rest], axis=1).astype(BF16)
    copies[0].wait()


def vid_row(load_ref, rows):
    return load_ref[rows:, :rows].astype(F32)[:1, :]


def attend(keys, values, counts, qbd, scale):
    p = (counts * exp_capped(mm(keys, qbd), scale)).astype(BF16)
    return mm(values, p)


def fold(o, num_ref, den_ref, b, t, add):
    wide = o.shape[0] - EXTRA
    head = wide // 2
    br = o.shape[1] // 2
    r0 = t * wide
    places = (
        (num_ref, slice(r0, r0 + head), o[:head, :br]),
        (num_ref, slice(r0 + head, r0 + wide), o[head:wide, br:]),
        (den_ref, slice(2 * t, 2 * t + 1), o[wide : wide + 1, :br]),
        (den_ref, slice(2 * t + 1, 2 * t + 2), o[wide : wide + 1, br:]),
    )
    for ref, part, value in places:
        if add:
            ref[b, part, :] += value
        else:
            ref[b, part, :] = value


def prep_kernel(
    load_ref, gain_hbm, win_hbm, vk_hbm, lrows_hbm, srows_hbm, sblock_hbm, scount_hbm, wo_hbm,
    qbd_ref, num_ref, den_ref, counts_ref, mask_ref, vcol_ref, wk_ref, wvt_ref, wo_ref, gain_ref,
    vkw_ref, pool_ref, weight_ref,
    wq_ref, wv_ref, vk_ref, lrows_ref, srows_ref, sblock_ref, scount_ref, want_ref, sems,
):
    width = load_ref.shape[1]
    rows = load_ref.shape[0] - EXTRA
    blocks, pairs, wide, _ = qbd_ref.shape
    chips = mask_ref.shape[1]
    slots = sblock_ref.shape[1]
    virtual = vk_ref.shape[0]
    br = rows // blocks
    head = width // HEADS
    scale = head ** (-0.5)
    copies = start_copies(
        [
            (gain_hbm, gain_ref), (sblock_hbm, sblock_ref), (scount_hbm, scount_ref),
            (srows_hbm, srows_ref), (lrows_hbm, lrows_ref), (vk_hbm, vk_ref),
            (win_hbm.at[:, width : 2 * width], wk_ref), (win_hbm.at[:, :width], wq_ref),
            (win_hbm.at[:, 2 * width :], wv_ref), (wo_hbm, wo_ref),
        ],
        sems,
    )
    counts_ref[...] = jnp.zeros(counts_ref.shape, F32)
    for copy in copies:
        copy.wait()
    normed = norm_rows(load_ref[:rows, :], gain_ref[...])
    k = mm(normed, wk_ref[...]).astype(BF16)
    v = mm(normed, wv_ref[...]).astype(BF16)
    qt = mm(normed, wq_ref[...]).astype(BF16).T
    vt = v.T
    wvt_ref[...] = wv_ref[...].T

    vkf = vk_ref[...].astype(F32)
    vkbd = jnp.concatenate(
        [jnp.broadcast_to(vkf[j : j + 1, :], (HEADS, width)) for j in range(virtual)], axis=0
    )
    vkbd = jnp.where(of_own_head(vkbd.shape), vkbd, 0.0).astype(BF16)
    vkw_ref[...] = halves(mm_nt(vkbd, wk_ref[...]))
    vid = vid_row(load_ref, rows)
    add_pool(normed, vid, vkw_ref, pool_ref, weight_ref, scale, True)
    vcol_ref[...] = jnp.broadcast_to(vid, (128, rows)).T

    me = lax.axis_index("node")
    place = ring_place(me // CORES, chips)
    core = me % CORES
    for d in range(chips * CORES):
        want_ref[d] = 0
    for b in range(blocks):
        for e in range(slots):
            entry = sblock_ref[b, e]
            want_ref[entry // blocks] = entry % blocks
    for d in range(chips * CORES):
        step = (place - ring_place(jnp.int32(d // CORES), chips) + chips) % chips
        far = jnp.where(core == d % CORES, 0, 1)
        mask_ref[far, step] = jnp.full(mask_ref.shape[2:], want_ref[d].astype(F32), F32)
    for b in range(blocks):
        for e in range(slots):
            device = sblock_ref[b, e] // blocks
            step = (place - ring_place(device // CORES, chips) + chips) % chips
            far = jnp.where(device % CORES == core, 0, 1)
            live = jnp.where(e < scount_ref[b], 1.0, 0.0).astype(F32)
            counts_ref[far, step, b] += counts_of(srows_ref[b, e], br) * live

    zero = jnp.zeros((head, br), BF16)
    ones = jnp.ones((EXTRA, br), BF16)
    for b in range(blocks):
        cols = slice(b * br, (b + 1) * br)
        counts = counts_of(lrows_ref[:, cols], br)
        counts2 = jnp.concatenate([counts, counts], axis=1)
        for t in range(pairs):
            r0 = t * wide
            mid = r0 + head
            end = r0 + wide
            bd = jnp.concatenate(
                [
                    jnp.concatenate([qt[r0:mid, cols], zero], axis=1),
                    jnp.concatenate([zero, qt[mid:end, cols]], axis=1),
                ],
                axis=0,
            )
            qbd_ref[b, t] = bd
            values = jnp.concatenate([vt[r0:end, cols], ones], axis=0)
            fold(attend(k[cols, r0:end], values, counts2, bd, scale), num_ref, den_ref, b, t, False)


def take_sources(
    names, loads, mask_ref, gain_ref, wk_ref, wvt_ref, vkw_ref,
    normed_ref, k_ref, vt_ref, pool_ref, weight_ref,
):
    rows = loads[0].shape[0] - EXTRA
    width = k_ref.shape[1]
    chosen = []
    vids = []
    for i, ((far, step), load_ref) in enumerate(zip(names, loads)):
        part = norm_rows(load_ref[:rows, :], gain_ref[...])
        normed_ref[i * rows : (i + 1) * rows, :] = part
        chosen.append(choose(mask_ref[far, step, :1, :], part))
        vids.append(vid_row(load_ref, rows))
    picked = jnp.concatenate(chosen, axis=0)
    k_ref[...] = mm(picked, wk_ref[...]).astype(BF16)
    vt_ref[...] = mm_nt(wvt_ref[...], picked).astype(BF16)
    scale = (width // HEADS) ** (-0.5)
    vid = jnp.concatenate(vids, axis=1)
    add_pool(normed_ref[...], vid, vkw_ref, pool_ref, weight_ref, scale, False)


def add_sources(names, b, counts_ref, qbd_ref, k_ref, vt_ref, num_ref, den_ref):
    _, pairs, wide, _ = qbd_ref.shape
    scale = (2 / wide) ** 0.5
    counts = jnp.concatenate([counts_ref[far, step, b] for far, step in names], axis=0)
    counts2 = jnp.concatenate([counts, counts], axis=1)
    ones = jnp.ones((EXTRA, counts.shape[0]), BF16)
    for t in range(pairs):
        cols = slice(t * wide, (t + 1) * wide)
        values = jnp.concatenate([vt_ref[cols, :], ones], axis=0)
        o = attend(k_ref[:, cols], values, counts2, qbd_ref[b, t], scale)
        fold(o, num_ref, den_ref, b, t, True)


def slots_kernel(
    names, mask_ref, gain_ref, wk_ref, wvt_ref, vkw_ref, counts_ref, qbd_ref,
    num_in, den_in, pool_in, weight_in, *refs
):
    loads = refs[: len(names)]
    num_ref, den_ref, pool_ref, weight_ref, normed_ref, k_ref, vt_ref = refs[len(names) :]
    num_ref[...] = num_in[...]
    den_ref[...] = den_in[...]
    pool_ref[...] = pool_in[...]
    weight_ref[...] = weight_in[...]
    take_sources(
        names, loads, mask_ref, gain_ref, wk_ref, wvt_ref, vkw_ref,
        normed_ref, k_ref, vt_ref, pool_ref, weight_ref,
    )
    for b in range(num_ref.shape[0]):
        add_sources(names, b, counts_ref, qbd_ref, k_ref, vt_ref, num_ref, den_ref)


def finish_kernel(
    names, mask_ref, gain_ref, wk_ref, wvt_ref, vkw_ref, counts_ref, qbd_ref,
    num_in, den_in, pool_in, weight_in, last_ref, vcol_ref, load_ref, wo_ref,
    out_ref, num_ref, den_ref, pool_ref, weight_ref, normed_ref, k_ref, vt_ref,
):
    slots_kernel(
        names, mask_ref, gain_ref, wk_ref, wvt_ref, vkw_ref, counts_ref, qbd_ref,
        num_in, den_in, pool_in, weight_in, last_ref,
        num_ref, den_ref, pool_ref, weight_ref, normed_ref, k_ref, vt_ref,
    )
    blocks, width, br = num_ref.shape
    head = width // HEADS
    lanes = vcol_ref.shape[1]
    count = pool_ref.shape[0]
    weight = jnp.concatenate([weight_ref[...]] * (width // lanes), axis=1)
    both = mm_nt(halves(pool_ref[...] / weight), wvt_ref[...])
    both = jnp.where(of_own_head((count, width)), both[:count] + both[count:], 0.0)
    pooled = [
        jnp.sum(both[j : j + HEADS], axis=0, keepdims=True) for j in range(0, count, HEADS)
    ]
    for b in range(blocks):
        part = slice(b * br, (b + 1) * br)
        vid = vcol_ref[part, :]
        att = jnp.concatenate(
            [
                num_ref[b, h * head : (h + 1) * head, :] / den_ref[b, h : h + 1, :]
                for h in range(HEADS)
            ],
            axis=0,
        ).T
        pieces = []
        for c in range(0, width, lanes):
            own = jnp.broadcast_to(pooled[0][:, c : c + lanes], (br, lanes))
            for j in range(1, len(pooled)):
                own = jnp.where(vid == float(j), pooled[j][:, c : c + lanes], own)
            pieces.append((att[:, c : c + lanes] + own).astype(BF16))
        mixed = jnp.concatenate(pieces, axis=1)
        out_ref[part, :] = (load_ref[part, :].astype(F32) + mm(mixed, wo_ref[...])).astype(BF16)


def params(mib):
    return pltpu.CompilerParams(vmem_limit_bytes=mib * 2**20)


def cost(flops):
    return pl.CostEstimate(flops=flops, bytes_accessed=1024, transcendentals=0)


def body(
    activations,
    norm_gain,
    project_in,
    project_out,
    virtual_keys,
    virtual_id,
    local_rows,
    slot_block,
    slot_count,
    slot_rows,
):
    _, rows, width = activations.shape
    br = slot_rows.shape[3]
    slots = slot_block.shape[1]
    blocks = rows // br
    devices = lax.axis_size("node")
    chips = devices // CORES
    virtual = virtual_keys.shape[1]
    pairs = HEADS // 2
    wide = width // pairs
    shape = jax.ShapeDtypeStruct
    after = lax.optimization_barrier
    unit = 2**16

    load = pl.pallas_call(
        pack_kernel,
        out_shape=shape((rows + EXTRA, width), BF16),
        in_specs=[HBM] * 2,
        out_specs=VMEM,
        scratch_shapes=[pltpu.VMEM((1, rows), jnp.int32), pltpu.SemaphoreType.DMA((2,))],
        compiler_params=params(PACK_MIB),
        cost_estimate=cost(unit),
        name="pack_rows",
    )(activations[0], virtual_id.reshape(1, rows))
    near = {1: to_next_chip(load, devices, 1)}
    if chips > 2:
        near[chips - 1] = to_next_chip(load, devices, -1)
    far = {0: swapped(load, devices, 1)}

    accumulators = (
        shape((blocks, width, br), F32),
        shape((blocks, HEADS, br), F32),
        shape((virtual * HEADS, width), F32),
        shape((virtual * HEADS, 128), F32),
    )
    square = shape((width, width), BF16)
    qbd, num, den, counts, mask, vcol, wk, wvt, wo, gain, vkw, pool, weight = pl.pallas_call(
        prep_kernel,
        out_shape=(
            (shape((blocks, pairs, wide, 2 * br), BF16),)
            + accumulators[:2]
            + (
                shape((CORES, chips, blocks, br, br), F32),
                shape((CORES, chips, 8, 128), F32),
                shape((rows, 128), F32),
                square,
                square,
                square,
                shape((1, width), F32),
                shape((2 * virtual * HEADS, width), BF16),
            )
            + accumulators[2:]
        ),
        in_specs=[VMEM] + [HBM] * 8,
        out_specs=[VMEM] * 13,
        scratch_shapes=[
            pltpu.VMEM((width, width), BF16),
            pltpu.VMEM((width, width), BF16),
            pltpu.VMEM((virtual, width), BF16),
            pltpu.VMEM(local_rows.shape, jnp.int32),
            pltpu.VMEM(slot_rows.shape, jnp.int32),
            pltpu.SMEM((blocks, slots), jnp.int32),
            pltpu.SMEM((blocks,), jnp.int32),
            pltpu.SMEM((devices,), jnp.int32),
            pltpu.SemaphoreType.DMA((10,)),
        ],
        compiler_params=params(PREP_MIB),
        cost_estimate=cost(unit),
        name="prepare",
    )(
        load, norm_gain, project_in[0], virtual_keys[0], local_rows, slot_rows, slot_block,
        slot_count, project_out[0],
    )

    def work(count):
        return [
            pltpu.VMEM((count * rows, width), BF16),
            pltpu.VMEM((count * br, width), BF16),
            pltpu.VMEM((width, count * br), BF16),
        ]

    sums = (num, den, pool, weight)

    def arrive(step, sums):
        near[step], first = after((near[step], sums[1]))
        return (sums[0], first) + sums[2:]

    def slots_call(names, sums, name):
        return pl.pallas_call(
            functools.partial(slots_kernel, tuple(names)),
            out_shape=accumulators,
            in_specs=[VMEM] * (11 + len(names)),
            out_specs=[VMEM] * 4,
            scratch_shapes=work(len(names)),
            compiler_params=params(40),
            cost_estimate=cost(unit),
            name=name,
        )(
            mask, gain, wk, wvt, vkw, counts, qbd, *sums,
            *[(far if other else near)[step] for other, step in names],
        )

    ahead = chips // 2
    order = []
    for s in range(1, ahead + 1):
        order.append((s, 1))
        if s < chips - s:
            order.append((chips - s, -1))
    waiting = [(1, 0)]
    for i, (step, way) in enumerate(order):
        if step not in far:
            sums = arrive(step, sums)
            nexts = step + way
            if nexts not in near and (nexts, way) in order:
                near[nexts] = to_next_chip(near[step], devices, way)
            far[step] = swapped(near[step], devices, 1)
        waiting.append((0, step))
        if i == len(order) - 1:
            break
        waiting.append((1, step))
        if i == len(order) - 2:
            continue
        sums = slots_call(waiting, sums, "slots_%d" % i)
        waiting = []
    sums = slots_call(waiting, sums, "slots_last")
    names = ((1, order[-1][0]),)
    updated = pl.pallas_call(
        functools.partial(finish_kernel, names),
        out_shape=shape((rows, width), BF16),
        in_specs=[VMEM] * 15,
        out_specs=VMEM,
        scratch_shapes=[pltpu.VMEM(leaf.shape, leaf.dtype) for leaf in accumulators] + work(1),
        compiler_params=params(40),
        cost_estimate=cost(unit),
        name="finish",
    )(
        mask, gain, wk, wvt, vkw, counts, qbd, *sums, far[names[0][1]], vcol, load, wo
    )
    return to_next_segment(updated[None])


def solution(mesh):
    placed = (
        P("segment", "node", None),
        P("segment", None),
        P("segment", None, None),
        P("segment", None, None),
        P("segment", None, None),
        P("node", None),
        P(None, "node"),
        P("node", None),
        P("node"),
        P("node", None, None, None),
    )
    return jax.shard_map(
        body, mesh=mesh, in_specs=placed, out_specs=P("segment", "node", None), check_vma=False
    )
```

```python
import functools

import jax
import jax.numpy as jnp
from jax import lax
from jax.experimental import pallas as pl
from jax.experimental.pallas import tpu as pltpu
from jax.sharding import PartitionSpec as P

HEADS = 8
CORES = 2
EPSILON = 1e-05
CAP_LIMIT = 10.0
LOG2E = 1.4426950408889634
EXTRA = 16
F32 = jnp.float32
BF16 = jnp.bfloat16
HBM = pl.BlockSpec(memory_space=pltpu.HBM)
VMEM = pl.BlockSpec(memory_space=pltpu.VMEM)


def ring_order(chips):
    return list(range(0, 1)) + list(range(1, chips, 2)) + list(range((chips - 1) // 2 * 2, 0, -2))


def ring_place(chip, chips):
    return jnp.where(chip % 2 == 1, (chip + 1) // 2, (chips - chip // 2) % chips)


def to_next_chip(value, devices, way):
    chips = devices // CORES
    order = ring_order(chips)
    pairs = [
        (order[i] * CORES + c, order[(i + way) % chips] * CORES + c)
        for i in range(chips)
        for c in range(CORES)
    ]
    return lax.ppermute(value, "node", pairs)


def swapped(value, devices, distance):
    return lax.ppermute(value, "node", [(d, d ^ distance) for d in range(devices)])


def to_next_segment(value):
    count = lax.axis_size("segment")
    return lax.ppermute(value, "segment", [(s, (s + 1) % count) for s in range(count)])


def norm_rows(rows_in, gain_row):
    widened = rows_in.astype(F32)
    center = widened - jnp.mean(widened, axis=-1, keepdims=True)
    spread = jnp.mean(center * center, axis=-1, keepdims=True)
    return (center * lax.rsqrt(spread + EPSILON) * gain_row).astype(BF16)


def exp_capped(raw, scale):
    return jnp.exp2((CAP_LIMIT * LOG2E) * jnp.tanh(raw * (scale / CAP_LIMIT)))


def counts_of(index_rows, block_rows):
    rows = lax.broadcasted_iota(jnp.int32, (block_rows, index_rows.shape[1]), 0)
    total = jnp.zeros(rows.shape, F32)
    for j in range(index_rows.shape[0]):
        total = total + jnp.where(index_rows[j : j + 1, :] == rows, 1.0, 0.0)
    return total


def mm(a, b):
    return jnp.dot(a, b, preferred_element_type=F32)


def mm_nt(a, b):
    return lax.dot_general(a, b, (((1,), (1,)), ((), ())), preferred_element_type=F32)


def choose(mask_row, rows):
    lanes = mask_row.shape[1]
    count, width = rows.shape
    br = count // 2
    mask = jnp.broadcast_to(mask_row, (br, lanes))
    mask = jnp.concatenate([mask] * (width // lanes), axis=1)
    first, second = rows[:br, :].astype(F32), rows[br:, :].astype(F32)
    return jnp.where(mask > 0.5, second, first).astype(rows.dtype)


def halves(value):
    high = value.astype(BF16)
    low = (value - high.astype(F32)).astype(BF16)
    return jnp.concatenate([high, low], axis=0)


def of_own_head(shape):
    head = lax.broadcasted_iota(jnp.int32, shape, 0) % HEADS
    return head == lax.broadcasted_iota(jnp.int32, shape, 1) // (shape[1] // HEADS)


def add_pool(normed, vid_row, vkw_ref, pool_ref, weight_ref, scale, first):
    count = pool_ref.shape[0]
    raw = mm_nt(vkw_ref[...], normed)
    raw = raw[:count] + raw[count:]
    owner = lax.broadcasted_iota(jnp.int32, raw.shape, 0) // HEADS
    w = jnp.where(vid_row == owner.astype(F32), exp_capped(raw, scale), 0.0).astype(BF16)
    sums = mm(w, normed)
    totals = jnp.broadcast_to(
        jnp.sum(w.astype(F32), axis=1, keepdims=True), weight_ref.shape
    )
    pool_ref[...] = sums if first else pool_ref[...] + sums
    weight_ref[...] = totals if first else weight_ref[...] + totals


def start_copies(pairs, sems):
    copies = [pltpu.make_async_copy(src, dst, sems.at[i]) for i, (src, dst) in enumerate(pairs)]
    for copy in copies:
        copy.start()
    return copies


def vid_row(load_ref, rows):
    return load_ref[rows:, :rows].astype(F32)[:1, :]


def attend(keys, values, counts, qbd, scale):
    p = (counts * exp_capped(mm(keys, qbd), scale)).astype(BF16)
    return mm(values, p)


def fold(o, num_ref, den_ref, b, t, add):
    wide = o.shape[0] - EXTRA
    head = wide // 2
    br = o.shape[1] // 2
    r0 = t * wide
    places = (
        (num_ref, slice(r0, r0 + head), o[:head, :br]),
        (num_ref, slice(r0 + head, r0 + wide), o[head:wide, br:]),
        (den_ref, slice(2 * t, 2 * t + 1), o[wide : wide + 1, :br]),
        (den_ref, slice(2 * t + 1, 2 * t + 2), o[wide : wide + 1, br:]),
    )
    for ref, part, value in places:
        if add:
            ref[b, part, :] += value
        else:
            ref[b, part, :] = value


def prep_kernel(
    load_ref, gain_hbm, win_hbm, vk_hbm, lrows_hbm, srows_hbm, sblock_hbm, scount_hbm, wo_hbm,
    qbd_ref, num_ref, den_ref, counts_ref, mask_ref, vcol_ref, wk_ref, wvt_ref, wo_ref, gain_ref,
    vkw_ref, pool_ref, weight_ref,
    wq_ref, wv_ref, vk_ref, lrows_ref, srows_ref, sblock_ref, scount_ref, want_ref, sems,
):
    width = load_ref.shape[1]
    rows = load_ref.shape[0] - EXTRA
    blocks, pairs, wide, _ = qbd_ref.shape
    chips = mask_ref.shape[1]
    slots = sblock_ref.shape[1]
    virtual = vk_ref.shape[0]
    br = rows // blocks
    head = width // HEADS
    scale = head ** (-0.5)
    copies = start_copies(
        [
            (gain_hbm, gain_ref), (sblock_hbm, sblock_ref), (scount_hbm, scount_ref),
            (srows_hbm, srows_ref), (lrows_hbm, lrows_ref), (vk_hbm, vk_ref),
            (win_hbm.at[:, width : 2 * width], wk_ref), (win_hbm.at[:, :width], wq_ref),
            (win_hbm.at[:, 2 * width :], wv_ref), (wo_hbm, wo_ref),
        ],
        sems,
    )
    counts_ref[...] = jnp.zeros(counts_ref.shape, F32)
    for copy in copies:
        copy.wait()
    normed = norm_rows(load_ref[:rows, :], gain_ref[...])
    k = mm(normed, wk_ref[...]).astype(BF16)
    v = mm(normed, wv_ref[...]).astype(BF16)
    qt = mm(normed, wq_ref[...]).astype(BF16).T
    vt = v.T
    wvt_ref[...] = wv_ref[...].T

    vkf = vk_ref[...].astype(F32)
    vkbd = jnp.concatenate(
        [jnp.broadcast_to(vkf[j : j + 1, :], (HEADS, width)) for j in range(virtual)], axis=0
    )
    vkbd = jnp.where(of_own_head(vkbd.shape), vkbd, 0.0).astype(BF16)
    vkw_ref[...] = halves(mm_nt(vkbd, wk_ref[...]))
    vid = vid_row(load_ref, rows)
    add_pool(normed, vid, vkw_ref, pool_ref, weight_ref, scale, True)
    vcol_ref[...] = jnp.broadcast_to(vid, (128, rows)).T

    me = lax.axis_index("node")
    place = ring_place(me // CORES, chips)
    core = me % CORES
    for d in range(chips * CORES):
        want_ref[d] = 0
    for b in range(blocks):
        for e in range(slots):
            entry = sblock_ref[b, e]
            want_ref[entry // blocks] = entry % blocks
    for d in range(chips * CORES):
        step = (place - ring_place(jnp.int32(d // CORES), chips) + chips) % chips
        far = jnp.where(core == d % CORES, 0, 1)
        mask_ref[far, step] = jnp.full(mask_ref.shape[2:], want_ref[d].astype(F32), F32)
    for b in range(blocks):
        for e in range(slots):
            device = sblock_ref[b, e] // blocks
            step = (place - ring_place(device // CORES, chips) + chips) % chips
            far = jnp.where(device % CORES == core, 0, 1)
            live = jnp.where(e < scount_ref[b], 1.0, 0.0).astype(F32)
            counts_ref[far, step, b] += counts_of(srows_ref[b, e], br) * live

    zero = jnp.zeros((head, br), BF16)
    ones = jnp.ones((EXTRA, br), BF16)
    for b in range(blocks):
        cols = slice(b * br, (b + 1) * br)
        counts = counts_of(lrows_ref[:, cols], br)
        counts2 = jnp.concatenate([counts, counts], axis=1)
        for t in range(pairs):
            r0 = t * wide
            mid = r0 + head
            end = r0 + wide
            bd = jnp.concatenate(
                [
                    jnp.concatenate([qt[r0:mid, cols], zero], axis=1),
                    jnp.concatenate([zero, qt[mid:end, cols]], axis=1),
                ],
                axis=0,
            )
            qbd_ref[b, t] = bd
            values = jnp.concatenate([vt[r0:end, cols], ones], axis=0)
            fold(attend(k[cols, r0:end], values, counts2, bd, scale), num_ref, den_ref, b, t, False)


def take_sources(
    names, loads, mask_ref, gain_ref, wk_ref, wvt_ref, vkw_ref,
    normed_ref, k_ref, vt_ref, pool_ref, weight_ref,
):
    rows = loads[0].shape[0] - EXTRA
    width = k_ref.shape[1]
    chosen = []
    vids = []
    for i, ((far, step), load_ref) in enumerate(zip(names, loads)):
        part = norm_rows(load_ref[:rows, :], gain_ref[...])
        normed_ref[i * rows : (i + 1) * rows, :] = part
        chosen.append(choose(mask_ref[far, step, :1, :], part))
        vids.append(vid_row(load_ref, rows))
    picked = jnp.concatenate(chosen, axis=0)
    k_ref[...] = mm(picked, wk_ref[...]).astype(BF16)
    vt_ref[...] = mm_nt(wvt_ref[...], picked).astype(BF16)
    scale = (width // HEADS) ** (-0.5)
    vid = jnp.concatenate(vids, axis=1)
    add_pool(normed_ref[...], vid, vkw_ref, pool_ref, weight_ref, scale, False)


def add_sources(names, b, counts_ref, qbd_ref, k_ref, vt_ref, num_ref, den_ref):
    _, pairs, wide, _ = qbd_ref.shape
    scale = (2 / wide) ** 0.5
    counts = jnp.concatenate([counts_ref[far, step, b] for far, step in names], axis=0)
    counts2 = jnp.concatenate([counts, counts], axis=1)
    ones = jnp.ones((EXTRA, counts.shape[0]), BF16)
    for t in range(pairs):
        cols = slice(t * wide, (t + 1) * wide)
        values = jnp.concatenate([vt_ref[cols, :], ones], axis=0)
        o = attend(k_ref[:, cols], values, counts2, qbd_ref[b, t], scale)
        fold(o, num_ref, den_ref, b, t, True)


def slots_kernel(
    names, mask_ref, gain_ref, wk_ref, wvt_ref, vkw_ref, counts_ref, qbd_ref,
    num_in, den_in, pool_in, weight_in, *refs
):
    loads = refs[: len(names)]
    num_ref, den_ref, pool_ref, weight_ref, normed_ref, k_ref, vt_ref = refs[len(names) :]
    num_ref[...] = num_in[...]
    den_ref[...] = den_in[...]
    pool_ref[...] = pool_in[...]
    weight_ref[...] = weight_in[...]
    take_sources(
        names, loads, mask_ref, gain_ref, wk_ref, wvt_ref, vkw_ref,
        normed_ref, k_ref, vt_ref, pool_ref, weight_ref,
    )
    for b in range(num_ref.shape[0]):
        add_sources(names, b, counts_ref, qbd_ref, k_ref, vt_ref, num_ref, den_ref)


def finish_kernel(
    names, mask_ref, gain_ref, wk_ref, wvt_ref, vkw_ref, counts_ref, qbd_ref,
    num_in, den_in, pool_in, weight_in, last_ref, vcol_ref, load_ref, wo_ref,
    out_ref, num_ref, den_ref, pool_ref, weight_ref, normed_ref, k_ref, vt_ref,
):
    slots_kernel(
        names, mask_ref, gain_ref, wk_ref, wvt_ref, vkw_ref, counts_ref, qbd_ref,
        num_in, den_in, pool_in, weight_in, last_ref,
        num_ref, den_ref, pool_ref, weight_ref, normed_ref, k_ref, vt_ref,
    )
    blocks, width, br = num_ref.shape
    head = width // HEADS
    lanes = vcol_ref.shape[1]
    count = pool_ref.shape[0]
    weight = jnp.concatenate([weight_ref[...]] * (width // lanes), axis=1)
    both = mm_nt(halves(pool_ref[...] / weight), wvt_ref[...])
    both = jnp.where(of_own_head((count, width)), both[:count] + both[count:], 0.0)
    pooled = [
        jnp.sum(both[j : j + HEADS], axis=0, keepdims=True) for j in range(0, count, HEADS)
    ]
    for b in range(blocks):
        part = slice(b * br, (b + 1) * br)
        vid = vcol_ref[part, :]
        att = jnp.concatenate(
            [
                num_ref[b, h * head : (h + 1) * head, :] / den_ref[b, h : h + 1, :]
                for h in range(HEADS)
            ],
            axis=0,
        ).T
        pieces = []
        for c in range(0, width, lanes):
            own = jnp.broadcast_to(pooled[0][:, c : c + lanes], (br, lanes))
            for j in range(1, len(pooled)):
                own = jnp.where(vid == float(j), pooled[j][:, c : c + lanes], own)
            pieces.append((att[:, c : c + lanes] + own).astype(BF16))
        mixed = jnp.concatenate(pieces, axis=1)
        out_ref[part, :] = (load_ref[part, :].astype(F32) + mm(mixed, wo_ref[...])).astype(BF16)


def params(mib):
    return pltpu.CompilerParams(vmem_limit_bytes=mib * 2**20)


def cost(flops):
    return pl.CostEstimate(flops=flops, bytes_accessed=1024, transcendentals=0)


def body(
    activations,
    norm_gain,
    project_in,
    project_out,
    virtual_keys,
    virtual_id,
    local_rows,
    slot_block,
    slot_count,
    slot_rows,
):
    _, rows, width = activations.shape
    br = slot_rows.shape[3]
    slots = slot_block.shape[1]
    blocks = rows // br
    devices = lax.axis_size("node")
    chips = devices // CORES
    virtual = virtual_keys.shape[1]
    pairs = HEADS // 2
    wide = width // pairs
    shape = jax.ShapeDtypeStruct
    after = lax.optimization_barrier
    unit = 2**16

    ids = jnp.pad(virtual_id.reshape(1, rows).astype(BF16), ((0, EXTRA - 1), (0, width - rows)))
    load = jnp.concatenate([activations[0], ids], axis=0)
    near = {1: to_next_chip(load, devices, 1)}
    if chips > 2:
        near[chips - 1] = to_next_chip(load, devices, -1)
    far = {0: swapped(load, devices, 1)}

    accumulators = (
        shape((blocks, width, br), F32),
        shape((blocks, HEADS, br), F32),
        shape((virtual * HEADS, width), F32),
        shape((virtual * HEADS, 128), F32),
    )
    square = shape((width, width), BF16)
    qbd, num, den, counts, mask, vcol, wk, wvt, wo, gain, vkw, pool, weight = pl.pallas_call(
        prep_kernel,
        out_shape=(
            (shape((blocks, pairs, wide, 2 * br), BF16),)
            + accumulators[:2]
            + (
                shape((CORES, chips, blocks, br, br), F32),
                shape((CORES, chips, 8, 128), F32),
                shape((rows, 128), F32),
                square,
                square,
                square,
                shape((1, width), F32),
                shape((2 * virtual * HEADS, width), BF16),
            )
            + accumulators[2:]
        ),
        in_specs=[VMEM] + [HBM] * 8,
        out_specs=[VMEM] * 13,
        scratch_shapes=[
            pltpu.VMEM((width, width), BF16),
            pltpu.VMEM((width, width), BF16),
            pltpu.VMEM((virtual, width), BF16),
            pltpu.VMEM(local_rows.shape, jnp.int32),
            pltpu.VMEM(slot_rows.shape, jnp.int32),
            pltpu.SMEM((blocks, slots), jnp.int32),
            pltpu.SMEM((blocks,), jnp.int32),
            pltpu.SMEM((devices,), jnp.int32),
            pltpu.SemaphoreType.DMA((10,)),
        ],
        compiler_params=params(32),
        cost_estimate=cost(unit),
        name="prepare",
    )(
        load,
        *[
            pltpu.with_memory_space_constraint(value, pltpu.HBM)
            for value in (
                norm_gain, project_in[0], virtual_keys[0], local_rows, slot_rows, slot_block,
                slot_count, project_out[0],
            )
        ],
    )

    def work(count):
        return [
            pltpu.VMEM((count * rows, width), BF16),
            pltpu.VMEM((count * br, width), BF16),
            pltpu.VMEM((width, count * br), BF16),
        ]

    sums = (num, den, pool, weight)

    def arrive(step, sums):
        near[step], first = after((near[step], sums[1]))
        return (sums[0], first) + sums[2:]

    def slots_call(names, sums, name):
        return pl.pallas_call(
            functools.partial(slots_kernel, tuple(names)),
            out_shape=accumulators,
            in_specs=[VMEM] * (11 + len(names)),
            out_specs=[VMEM] * 4,
            scratch_shapes=work(len(names)),
            compiler_params=params(40),
            cost_estimate=cost(unit),
            name=name,
        )(
            mask, gain, wk, wvt, vkw, counts, qbd, *sums,
            *[(far if other else near)[step] for other, step in names],
        )

    ahead = chips // 2
    order = []
    for s in range(1, ahead + 1):
        order.append((s, 1))
        if s < chips - s:
            order.append((chips - s, -1))
    waiting = [(1, 0)]
    for i, (step, way) in enumerate(order):
        if i == 0:
            ready = [near[other] for other, _ in order[:2]]
            *ready, first = after((*ready, sums[1]))
            near.update({other: value for (other, _), value in zip(order, ready)})
            sums = (sums[0], first) + sums[2:]
        elif i > 1:
            sums = arrive(step, sums)
        nexts = step + way
        if nexts not in near and (nexts, way) in order:
            near[nexts] = to_next_chip(near[step], devices, way)
        far[step] = swapped(near[step], devices, 1)
        waiting.append((0, step))
        if i == len(order) - 1:
            break
        waiting.append((1, step))
        if i > 0:
            sums = slots_call(waiting, sums, "slots_%d" % i)
            waiting = []
    sums = slots_call(waiting, sums, "slots_last")
    names = ((1, order[-1][0]),)
    updated = pl.pallas_call(
        functools.partial(finish_kernel, names),
        out_shape=shape((rows, width), BF16),
        in_specs=[VMEM] * 15,
        out_specs=VMEM,
        scratch_shapes=[pltpu.VMEM(leaf.shape, leaf.dtype) for leaf in accumulators] + work(1),
        compiler_params=params(40),
        cost_estimate=cost(unit),
        name="finish",
    )(
        mask, gain, wk, wvt, vkw, counts, qbd, *sums, far[names[0][1]], vcol, load, wo
    )
    return to_next_segment(updated[None])


def solution(mesh):
    placed = (
        P("segment", "node", None),
        P("segment", None),
        P("segment", None, None),
        P("segment", None, None),
        P("segment", None, None),
        P("node", None),
        P(None, "node"),
        P("node", None),
        P("node"),
        P("node", None, None, None),
    )
    return jax.shard_map(
        body, mesh=mesh, in_specs=placed, out_specs=P("segment", "node", None), check_vma=False
    )
```

```python
import functools

import jax
import jax.numpy as jnp
from jax import lax
from jax.experimental import pallas as pl
from jax.experimental.pallas import tpu as pltpu
from jax.sharding import PartitionSpec as P

HEADS = 8
CORES = 2
EPSILON = 1e-05
CAP_LIMIT = 10.0
LOG2E = 1.4426950408889634
EXTRA = 16
F32 = jnp.float32
BF16 = jnp.bfloat16
HBM = pl.BlockSpec(memory_space=pltpu.HBM)
VMEM = pl.BlockSpec(memory_space=pltpu.VMEM)


def ring_order(chips):
    return list(range(0, 1)) + list(range(1, chips, 2)) + list(range((chips - 1) // 2 * 2, 0, -2))


def ring_place(chip, chips):
    return jnp.where(chip % 2 == 1, (chip + 1) // 2, (chips - chip // 2) % chips)


def to_next_chip(value, devices, way):
    chips = devices // CORES
    order = ring_order(chips)
    pairs = [
        (order[i] * CORES + c, order[(i + way) % chips] * CORES + c)
        for i in range(chips)
        for c in range(CORES)
    ]
    return lax.ppermute(value, "node", pairs)


def swapped(value, devices, distance):
    return lax.ppermute(value, "node", [(d, d ^ distance) for d in range(devices)])


def swapped_parts(value, devices, cut):
    return [swapped(value[:cut], devices, 1), swapped(value[cut:], devices, 1)]


def to_next_segment(value):
    count = lax.axis_size("segment")
    return lax.ppermute(value, "segment", [(s, (s + 1) % count) for s in range(count)])


def norm_rows(rows_in, gain_row):
    widened = rows_in.astype(F32)
    center = widened - jnp.mean(widened, axis=-1, keepdims=True)
    spread = jnp.mean(center * center, axis=-1, keepdims=True)
    return (center * lax.rsqrt(spread + EPSILON) * gain_row).astype(BF16)


def exp_capped(raw, scale):
    return jnp.exp2((CAP_LIMIT * LOG2E) * jnp.tanh(raw * (scale / CAP_LIMIT)))


def counts_of(index_rows, block_rows):
    rows = lax.broadcasted_iota(jnp.int32, (block_rows, index_rows.shape[1]), 0)
    total = jnp.zeros(rows.shape, F32)
    for j in range(index_rows.shape[0]):
        total = total + jnp.where(index_rows[j : j + 1, :] == rows, 1.0, 0.0)
    return total


def mm(a, b):
    return jnp.dot(a, b, preferred_element_type=F32)


def mm_nt(a, b):
    return lax.dot_general(a, b, (((1,), (1,)), ((), ())), preferred_element_type=F32)


def choose(mask_row, rows):
    lanes = mask_row.shape[1]
    count, width = rows.shape
    br = count // 2
    mask = jnp.broadcast_to(mask_row, (br, lanes))
    mask = jnp.concatenate([mask] * (width // lanes), axis=1)
    first, second = rows[:br, :].astype(F32), rows[br:, :].astype(F32)
    return jnp.where(mask > 0.5, second, first).astype(rows.dtype)


def halves(value):
    high = value.astype(BF16)
    low = (value - high.astype(F32)).astype(BF16)
    return jnp.concatenate([high, low], axis=0)


def of_own_head(shape):
    head = lax.broadcasted_iota(jnp.int32, shape, 0) % HEADS
    return head == lax.broadcasted_iota(jnp.int32, shape, 1) // (shape[1] // HEADS)


def add_pool(normed, vid_row, vkw_ref, pool_ref, weight_ref, scale, first):
    count = pool_ref.shape[0]
    raw = mm_nt(vkw_ref[...], normed)
    raw = raw[:count] + raw[count:]
    owner = lax.broadcasted_iota(jnp.int32, raw.shape, 0) // HEADS
    w = jnp.where(vid_row == owner.astype(F32), exp_capped(raw, scale), 0.0).astype(BF16)
    sums = mm(w, normed)
    totals = jnp.broadcast_to(
        jnp.sum(w.astype(F32), axis=1, keepdims=True), weight_ref.shape
    )
    pool_ref[...] = sums if first else pool_ref[...] + sums
    weight_ref[...] = totals if first else weight_ref[...] + totals


def start_copies(pairs, sems):
    copies = [pltpu.make_async_copy(src, dst, sems.at[i]) for i, (src, dst) in enumerate(pairs)]
    for copy in copies:
        copy.start()
    return copies


def vid_row(load_ref, rows):
    last = load_ref.shape[0]
    return load_ref[last - EXTRA :, :rows].astype(F32)[:1, :]


def load_rows(refs):
    last = refs[-1].shape[0] - EXTRA
    return jnp.concatenate([ref[...] for ref in refs[:-1]] + [refs[-1][:last, :]], axis=0)


def grouped(refs, sizes):
    groups = []
    for size in sizes:
        groups.append(refs[:size])
        refs = refs[size:]
    return groups


def attend(keys, values, counts, qbd, scale):
    p = (counts * exp_capped(mm(keys, qbd), scale)).astype(BF16)
    return mm(values, p)


def fold(o, num_ref, den_ref, b, t, add):
    wide = o.shape[0] - EXTRA
    head = wide // 2
    br = o.shape[1] // 2
    r0 = t * wide
    places = (
        (num_ref, slice(r0, r0 + head), o[:head, :br]),
        (num_ref, slice(r0 + head, r0 + wide), o[head:wide, br:]),
        (den_ref, slice(2 * t, 2 * t + 1), o[wide : wide + 1, :br]),
        (den_ref, slice(2 * t + 1, 2 * t + 2), o[wide : wide + 1, br:]),
    )
    for ref, part, value in places:
        if add:
            ref[b, part, :] += value
        else:
            ref[b, part, :] = value


def prep_kernel(
    load_ref, gain_hbm, win_hbm, vk_hbm, lrows_hbm, srows_hbm, sblock_hbm, scount_hbm, wo_hbm,
    qbd_ref, num_ref, den_ref, counts_ref, mask_ref, vcol_ref, wk_ref, wvt_ref, wo_ref, gain_ref,
    vkw_ref, pool_ref, weight_ref,
    wq_ref, wv_ref, vk_ref, lrows_ref, srows_ref, sblock_ref, scount_ref, want_ref, sems,
):
    width = load_ref.shape[1]
    rows = load_ref.shape[0] - EXTRA
    blocks, pairs, wide, _ = qbd_ref.shape
    chips = mask_ref.shape[1]
    slots = sblock_ref.shape[1]
    virtual = vk_ref.shape[0]
    br = rows // blocks
    head = width // HEADS
    scale = head ** (-0.5)
    copies = start_copies(
        [
            (gain_hbm, gain_ref), (sblock_hbm, sblock_ref), (scount_hbm, scount_ref),
            (srows_hbm, srows_ref), (lrows_hbm, lrows_ref), (vk_hbm, vk_ref),
            (win_hbm.at[:, width : 2 * width], wk_ref), (win_hbm.at[:, :width], wq_ref),
            (win_hbm.at[:, 2 * width :], wv_ref), (wo_hbm, wo_ref),
        ],
        sems,
    )
    counts_ref[...] = jnp.zeros(counts_ref.shape, F32)
    for copy in copies:
        copy.wait()
    normed = norm_rows(load_ref[:rows, :], gain_ref[...])
    k = mm(normed, wk_ref[...]).astype(BF16)
    v = mm(normed, wv_ref[...]).astype(BF16)
    qt = mm(normed, wq_ref[...]).astype(BF16).T
    vt = v.T
    wvt_ref[...] = wv_ref[...].T

    vkf = vk_ref[...].astype(F32)
    vkbd = jnp.concatenate(
        [jnp.broadcast_to(vkf[j : j + 1, :], (HEADS, width)) for j in range(virtual)], axis=0
    )
    vkbd = jnp.where(of_own_head(vkbd.shape), vkbd, 0.0).astype(BF16)
    vkw_ref[...] = halves(mm_nt(vkbd, wk_ref[...]))
    vid = vid_row(load_ref, rows)
    add_pool(normed, vid, vkw_ref, pool_ref, weight_ref, scale, True)
    vcol_ref[...] = jnp.broadcast_to(vid, (128, rows)).T

    me = lax.axis_index("node")
    place = ring_place(me // CORES, chips)
    core = me % CORES
    for d in range(chips * CORES):
        want_ref[d] = 0
    for b in range(blocks):
        for e in range(slots):
            entry = sblock_ref[b, e]
            want_ref[entry // blocks] = entry % blocks
    for d in range(chips * CORES):
        step = (place - ring_place(jnp.int32(d // CORES), chips) + chips) % chips
        far = jnp.where(core == d % CORES, 0, 1)
        mask_ref[far, step] = jnp.full(mask_ref.shape[2:], want_ref[d].astype(F32), F32)
    for b in range(blocks):
        for e in range(slots):
            device = sblock_ref[b, e] // blocks
            step = (place - ring_place(device // CORES, chips) + chips) % chips
            far = jnp.where(device % CORES == core, 0, 1)
            live = jnp.where(e < scount_ref[b], 1.0, 0.0).astype(F32)
            counts_ref[far, step, b] += counts_of(srows_ref[b, e], br) * live

    zero = jnp.zeros((head, br), BF16)
    ones = jnp.ones((EXTRA, br), BF16)
    for b in range(blocks):
        cols = slice(b * br, (b + 1) * br)
        counts = counts_of(lrows_ref[:, cols], br)
        counts2 = jnp.concatenate([counts, counts], axis=1)
        for t in range(pairs):
            r0 = t * wide
            mid = r0 + head
            end = r0 + wide
            bd = jnp.concatenate(
                [
                    jnp.concatenate([qt[r0:mid, cols], zero], axis=1),
                    jnp.concatenate([zero, qt[mid:end, cols]], axis=1),
                ],
                axis=0,
            )
            qbd_ref[b, t] = bd
            values = jnp.concatenate([vt[r0:end, cols], ones], axis=0)
            fold(attend(k[cols, r0:end], values, counts2, bd, scale), num_ref, den_ref, b, t, False)


def take_sources(
    names, loads, mask_ref, gain_ref, wk_ref, wvt_ref, vkw_ref,
    normed_ref, k_ref, vt_ref, pool_ref, weight_ref,
):
    width = k_ref.shape[1]
    chosen = []
    vids = []
    for i, ((far, step), pieces) in enumerate(zip(names, loads)):
        part = norm_rows(load_rows(pieces), gain_ref[...])
        rows = part.shape[0]
        normed_ref[i * rows : (i + 1) * rows, :] = part
        chosen.append(choose(mask_ref[far, step, :1, :], part))
        vids.append(vid_row(pieces[-1], rows))
    picked = jnp.concatenate(chosen, axis=0)
    k_ref[...] = mm(picked, wk_ref[...]).astype(BF16)
    vt_ref[...] = mm_nt(wvt_ref[...], picked).astype(BF16)
    scale = (width // HEADS) ** (-0.5)
    vid = jnp.concatenate(vids, axis=1)
    add_pool(normed_ref[...], vid, vkw_ref, pool_ref, weight_ref, scale, False)


def add_sources(names, b, counts_ref, qbd_ref, k_ref, vt_ref, num_ref, den_ref):
    _, pairs, wide, _ = qbd_ref.shape
    scale = (2 / wide) ** 0.5
    counts = jnp.concatenate([counts_ref[far, step, b] for far, step in names], axis=0)
    counts2 = jnp.concatenate([counts, counts], axis=1)
    ones = jnp.ones((EXTRA, counts.shape[0]), BF16)
    for t in range(pairs):
        cols = slice(t * wide, (t + 1) * wide)
        values = jnp.concatenate([vt_ref[cols, :], ones], axis=0)
        o = attend(k_ref[:, cols], values, counts2, qbd_ref[b, t], scale)
        fold(o, num_ref, den_ref, b, t, True)


def slots_kernel(
    names, sizes, mask_ref, gain_ref, wk_ref, wvt_ref, vkw_ref, counts_ref, qbd_ref,
    num_in, den_in, pool_in, weight_in, *refs
):
    loads = grouped(refs, sizes)
    num_ref, den_ref, pool_ref, weight_ref, normed_ref, k_ref, vt_ref = refs[sum(sizes) :]
    num_ref[...] = num_in[...]
    den_ref[...] = den_in[...]
    pool_ref[...] = pool_in[...]
    weight_ref[...] = weight_in[...]
    take_sources(
        names, loads, mask_ref, gain_ref, wk_ref, wvt_ref, vkw_ref,
        normed_ref, k_ref, vt_ref, pool_ref, weight_ref,
    )
    for b in range(num_ref.shape[0]):
        add_sources(names, b, counts_ref, qbd_ref, k_ref, vt_ref, num_ref, den_ref)


def finish_kernel(
    names, mask_ref, gain_ref, wk_ref, wvt_ref, vkw_ref, counts_ref, qbd_ref,
    num_in, den_in, pool_in, weight_in, last_ref, vcol_ref, load_ref, wo_ref,
    out_ref, num_ref, den_ref, pool_ref, weight_ref, normed_ref, k_ref, vt_ref,
):
    slots_kernel(
        names, (1,), mask_ref, gain_ref, wk_ref, wvt_ref, vkw_ref, counts_ref, qbd_ref,
        num_in, den_in, pool_in, weight_in, last_ref,
        num_ref, den_ref, pool_ref, weight_ref, normed_ref, k_ref, vt_ref,
    )
    blocks, width, br = num_ref.shape
    head = width // HEADS
    lanes = vcol_ref.shape[1]
    count = pool_ref.shape[0]
    weight = jnp.concatenate([weight_ref[...]] * (width // lanes), axis=1)
    both = mm_nt(halves(pool_ref[...] / weight), wvt_ref[...])
    both = jnp.where(of_own_head((count, width)), both[:count] + both[count:], 0.0)
    pooled = [
        jnp.sum(both[j : j + HEADS], axis=0, keepdims=True) for j in range(0, count, HEADS)
    ]
    for b in range(blocks):
        part = slice(b * br, (b + 1) * br)
        vid = vcol_ref[part, :]
        att = jnp.concatenate(
            [
                num_ref[b, h * head : (h + 1) * head, :] / den_ref[b, h : h + 1, :]
                for h in range(HEADS)
            ],
            axis=0,
        ).T
        pieces = []
        for c in range(0, width, lanes):
            own = jnp.broadcast_to(pooled[0][:, c : c + lanes], (br, lanes))
            for j in range(1, len(pooled)):
                own = jnp.where(vid == float(j), pooled[j][:, c : c + lanes], own)
            pieces.append((att[:, c : c + lanes] + own).astype(BF16))
        mixed = jnp.concatenate(pieces, axis=1)
        out_ref[part, :] = (load_ref[part, :].astype(F32) + mm(mixed, wo_ref[...])).astype(BF16)


def params(mib):
    return pltpu.CompilerParams(vmem_limit_bytes=mib * 2**20)


def cost(flops):
    return pl.CostEstimate(flops=flops, bytes_accessed=1024, transcendentals=0)


def body(
    activations,
    norm_gain,
    project_in,
    project_out,
    virtual_keys,
    virtual_id,
    local_rows,
    slot_block,
    slot_count,
    slot_rows,
):
    _, rows, width = activations.shape
    br = slot_rows.shape[3]
    slots = slot_block.shape[1]
    blocks = rows // br
    devices = lax.axis_size("node")
    chips = devices // CORES
    virtual = virtual_keys.shape[1]
    pairs = HEADS // 2
    wide = width // pairs
    shape = jax.ShapeDtypeStruct
    after = lax.optimization_barrier
    unit = 2**16

    ids = after(virtual_id.reshape(1, rows))
    ids = jnp.pad(ids.astype(BF16), ((0, EXTRA - 1), (0, width - rows)))
    load = jnp.concatenate([activations[0], ids], axis=0)
    near = {1: to_next_chip(load, devices, 1)}
    if chips > 2:
        near[chips - 1] = to_next_chip(load, devices, -1)
    far = {0: swapped_parts(load, devices, br)}

    accumulators = (
        shape((blocks, width, br), F32),
        shape((blocks, HEADS, br), F32),
        shape((virtual * HEADS, width), F32),
        shape((virtual * HEADS, 128), F32),
    )
    square = shape((width, width), BF16)
    qbd, num, den, counts, mask, vcol, wk, wvt, wo, gain, vkw, pool, weight = pl.pallas_call(
        prep_kernel,
        out_shape=(
            (shape((blocks, pairs, wide, 2 * br), BF16),)
            + accumulators[:2]
            + (
                shape((CORES, chips, blocks, br, br), F32),
                shape((CORES, chips, 8, 128), F32),
                shape((rows, 128), F32),
                square,
                square,
                square,
                shape((1, width), F32),
                shape((2 * virtual * HEADS, width), BF16),
            )
            + accumulators[2:]
        ),
        in_specs=[VMEM] + [HBM] * 8,
        out_specs=[VMEM] * 13,
        scratch_shapes=[
            pltpu.VMEM((width, width), BF16),
            pltpu.VMEM((width, width), BF16),
            pltpu.VMEM((virtual, width), BF16),
            pltpu.VMEM(local_rows.shape, jnp.int32),
            pltpu.VMEM(slot_rows.shape, jnp.int32),
            pltpu.SMEM((blocks, slots), jnp.int32),
            pltpu.SMEM((blocks,), jnp.int32),
            pltpu.SMEM((devices,), jnp.int32),
            pltpu.SemaphoreType.DMA((10,)),
        ],
        compiler_params=params(32),
        cost_estimate=cost(unit),
        name="prepare",
    )(
        load,
        *[
            pltpu.with_memory_space_constraint(value, pltpu.HBM)
            for value in (
                norm_gain, project_in[0], virtual_keys[0], local_rows, slot_rows, slot_block,
                slot_count, project_out[0],
            )
        ],
    )

    def work(count):
        return [
            pltpu.VMEM((count * rows, width), BF16),
            pltpu.VMEM((count * br, width), BF16),
            pltpu.VMEM((width, count * br), BF16),
        ]

    sums = (num, den, pool, weight)

    def arrive(step, sums):
        near[step], first = after((near[step], sums[1]))
        return (sums[0], first) + sums[2:]

    def slots_call(names, sums, name):
        loads = [(far if other else near)[step] for other, step in names]
        loads = [load if isinstance(load, list) else [load] for load in loads]
        sizes = tuple(len(load) for load in loads)
        return pl.pallas_call(
            functools.partial(slots_kernel, tuple(names), sizes),
            out_shape=accumulators,
            in_specs=[VMEM] * (11 + sum(sizes)),
            out_specs=[VMEM] * 4,
            scratch_shapes=work(len(names)),
            compiler_params=params(40),
            cost_estimate=cost(unit),
            name=name,
        )(
            mask, gain, wk, wvt, vkw, counts, qbd, *sums,
            *[piece for load in loads for piece in load],
        )

    ahead = chips // 2
    order = []
    for s in range(1, ahead + 1):
        order.append((s, 1))
        if s < chips - s:
            order.append((chips - s, -1))
    waiting = [(1, 0)]
    for i, (step, way) in enumerate(order):
        sums = arrive(step, sums)
        nexts = step + way
        if nexts not in near and (nexts, way) in order:
            near[nexts] = to_next_chip(near[step], devices, way)
        if i == len(order) - 1:
            far[step] = swapped(near[step], devices, 1)
        else:
            far[step] = swapped_parts(near[step], devices, br)
        waiting.append((0, step))
        if i == len(order) - 1:
            break
        waiting.append((1, step))
        if i < len(order) - 1:
            sums = slots_call(waiting, sums, "slots_%d" % i)
            waiting = []
    sums = slots_call(waiting, sums, "slots_last")
    names = ((1, order[-1][0]),)
    updated = pl.pallas_call(
        functools.partial(finish_kernel, names),
        out_shape=shape((rows, width), BF16),
        in_specs=[VMEM] * 15,
        out_specs=VMEM,
        scratch_shapes=[pltpu.VMEM(leaf.shape, leaf.dtype) for leaf in accumulators] + work(1),
        compiler_params=params(40),
        cost_estimate=cost(unit),
        name="finish",
    )(
        mask, gain, wk, wvt, vkw, counts, qbd, *sums, far[names[0][1]], vcol, load, wo
    )
    return to_next_segment(updated[None])


def solution(mesh):
    placed = (
        P("segment", "node", None),
        P("segment", None),
        P("segment", None, None),
        P("segment", None, None),
        P("segment", None, None),
        P("node", None),
        P(None, "node"),
        P("node", None),
        P("node"),
        P("node", None, None, None),
    )
    return jax.shard_map(
        body, mesh=mesh, in_specs=placed, out_specs=P("segment", "node", None), check_vma=False
    )
```

```python
import functools

import jax
import jax.numpy as jnp
from jax import lax
from jax.experimental import pallas as pl
from jax.experimental.pallas import tpu as pltpu
from jax.sharding import PartitionSpec as P

HEADS = 8
CORES = 2
EPSILON = 1e-05
CAP_LIMIT = 10.0
LOG2E = 1.4426950408889634
EXTRA = 16
F32 = jnp.float32
BF16 = jnp.bfloat16
HBM = pl.BlockSpec(memory_space=pltpu.HBM)
VMEM = pl.BlockSpec(memory_space=pltpu.VMEM)


def ring_order(chips):
    return list(range(0, 1)) + list(range(1, chips, 2)) + list(range((chips - 1) // 2 * 2, 0, -2))


def ring_place(chip, chips):
    return jnp.where(chip % 2 == 1, (chip + 1) // 2, (chips - chip // 2) % chips)


def to_next_chip(value, devices, way):
    chips = devices // CORES
    order = ring_order(chips)
    pairs = [
        (order[i] * CORES + c, order[(i + way) % chips] * CORES + c)
        for i in range(chips)
        for c in range(CORES)
    ]
    return lax.ppermute(value, "node", pairs)


def swapped(value, devices, distance):
    return lax.ppermute(value, "node", [(d, d ^ distance) for d in range(devices)])


def swapped_parts(value, devices, parts):
    tiles = value.shape[0] // 16
    cuts = [0] + [16 * (-(-tiles * (i + 1) // parts)) for i in range(parts)]
    return [swapped(value[a:b], devices, 1) for a, b in zip(cuts, cuts[1:])]


def to_next_segment(value):
    count = lax.axis_size("segment")
    return lax.ppermute(value, "segment", [(s, (s + 1) % count) for s in range(count)])


def norm_rows(rows_in, gain_row):
    widened = rows_in.astype(F32)
    center = widened - jnp.mean(widened, axis=-1, keepdims=True)
    spread = jnp.mean(center * center, axis=-1, keepdims=True)
    return (center * lax.rsqrt(spread + EPSILON) * gain_row).astype(BF16)


def exp_capped(raw, scale):
    return jnp.exp2((CAP_LIMIT * LOG2E) * jnp.tanh(raw * (scale / CAP_LIMIT)))


def counts_of(index_rows, block_rows):
    rows = lax.broadcasted_iota(jnp.int32, (block_rows, index_rows.shape[1]), 0)
    total = jnp.zeros(rows.shape, F32)
    for j in range(index_rows.shape[0]):
        total = total + jnp.where(index_rows[j : j + 1, :] == rows, 1.0, 0.0)
    return total


def mm(a, b):
    return jnp.dot(a, b, preferred_element_type=F32)


def mm_nt(a, b):
    return lax.dot_general(a, b, (((1,), (1,)), ((), ())), preferred_element_type=F32)


def choose(mask_row, rows):
    lanes = mask_row.shape[1]
    count, width = rows.shape
    br = count // 2
    mask = jnp.broadcast_to(mask_row, (br, lanes))
    mask = jnp.concatenate([mask] * (width // lanes), axis=1)
    first, second = rows[:br, :].astype(F32), rows[br:, :].astype(F32)
    return jnp.where(mask > 0.5, second, first).astype(rows.dtype)


def halves(value):
    high = value.astype(BF16)
    low = (value - high.astype(F32)).astype(BF16)
    return jnp.concatenate([high, low], axis=0)


def of_own_head(shape):
    head = lax.broadcasted_iota(jnp.int32, shape, 0) % HEADS
    return head == lax.broadcasted_iota(jnp.int32, shape, 1) // (shape[1] // HEADS)


def add_pool(normed, vid_row, vkw_ref, pool_ref, weight_ref, scale, first):
    count = pool_ref.shape[0]
    raw = mm_nt(vkw_ref[...], normed)
    raw = raw[:count] + raw[count:]
    owner = lax.broadcasted_iota(jnp.int32, raw.shape, 0) // HEADS
    w = jnp.where(vid_row == owner.astype(F32), exp_capped(raw, scale), 0.0).astype(BF16)
    sums = mm(w, normed)
    totals = jnp.broadcast_to(
        jnp.sum(w.astype(F32), axis=1, keepdims=True), weight_ref.shape
    )
    pool_ref[...] = sums if first else pool_ref[...] + sums
    weight_ref[...] = totals if first else weight_ref[...] + totals


def start_copies(pairs, sems):
    copies = [pltpu.make_async_copy(src, dst, sems.at[i]) for i, (src, dst) in enumerate(pairs)]
    for copy in copies:
        copy.start()
    return copies


def pack_kernel(x_hbm, vid_hbm, load_ref, vid_ref, sems):
    rows = vid_ref.shape[1]
    copies = start_copies([(x_hbm, load_ref.at[:rows, :]), (vid_hbm, vid_ref)], sems)
    copies[1].wait()
    tile = jnp.broadcast_to(vid_ref[...].astype(F32), (EXTRA, rows))
    rest = jnp.zeros((EXTRA, load_ref.shape[1] - rows), F32)
    load_ref[rows:, :] = jnp.concatenate([tile, rest], axis=1).astype(BF16)
    copies[0].wait()


def vid_row(load_ref, rows):
    last = load_ref.shape[0]
    return load_ref[last - EXTRA :, :rows].astype(F32)[:1, :]


def load_rows(refs):
    last = refs[-1].shape[0] - EXTRA
    return jnp.concatenate([ref[...] for ref in refs[:-1]] + [refs[-1][:last, :]], axis=0)


def grouped(refs, sizes):
    groups = []
    for size in sizes:
        groups.append(refs[:size])
        refs = refs[size:]
    return groups


def attend(keys, values, counts, qbd, scale):
    p = (counts * exp_capped(mm(keys, qbd), scale)).astype(BF16)
    return mm(values, p)


def fold(o, num_ref, den_ref, b, t, add):
    wide = o.shape[0] - EXTRA
    head = wide // 2
    br = o.shape[1] // 2
    r0 = t * wide
    places = (
        (num_ref, slice(r0, r0 + head), o[:head, :br]),
        (num_ref, slice(r0 + head, r0 + wide), o[head:wide, br:]),
        (den_ref, slice(2 * t, 2 * t + 1), o[wide : wide + 1, :br]),
        (den_ref, slice(2 * t + 1, 2 * t + 2), o[wide : wide + 1, br:]),
    )
    for ref, part, value in places:
        if add:
            ref[b, part, :] += value
        else:
            ref[b, part, :] = value


def prep_kernel(
    load_ref, gain_hbm, win_hbm, vk_hbm, lrows_hbm, srows_hbm, sblock_hbm, scount_hbm, wo_hbm,
    qbd_ref, num_ref, den_ref, counts_ref, mask_ref, vcol_ref, wk_ref, wvt_ref, wo_ref, gain_ref,
    vkw_ref, pool_ref, weight_ref,
    wq_ref, wv_ref, vk_ref, lrows_ref, srows_ref, sblock_ref, scount_ref, want_ref, sems,
):
    width = load_ref.shape[1]
    rows = load_ref.shape[0] - EXTRA
    blocks, pairs, wide, _ = qbd_ref.shape
    chips = mask_ref.shape[1]
    slots = sblock_ref.shape[1]
    virtual = vk_ref.shape[0]
    br = rows // blocks
    head = width // HEADS
    scale = head ** (-0.5)
    copies = start_copies(
        [
            (gain_hbm, gain_ref), (sblock_hbm, sblock_ref), (scount_hbm, scount_ref),
            (srows_hbm, srows_ref), (lrows_hbm, lrows_ref), (vk_hbm, vk_ref),
            (win_hbm.at[:, width : 2 * width], wk_ref), (win_hbm.at[:, :width], wq_ref),
            (win_hbm.at[:, 2 * width :], wv_ref), (wo_hbm, wo_ref),
        ],
        sems,
    )
    counts_ref[...] = jnp.zeros(counts_ref.shape, F32)
    for copy in copies:
        copy.wait()
    normed = norm_rows(load_ref[:rows, :], gain_ref[...])
    k = mm(normed, wk_ref[...]).astype(BF16)
    v = mm(normed, wv_ref[...]).astype(BF16)
    qt = mm(normed, wq_ref[...]).astype(BF16).T
    vt = v.T
    wvt_ref[...] = wv_ref[...].T

    vkf = vk_ref[...].astype(F32)
    vkbd = jnp.concatenate(
        [jnp.broadcast_to(vkf[j : j + 1, :], (HEADS, width)) for j in range(virtual)], axis=0
    )
    vkbd = jnp.where(of_own_head(vkbd.shape), vkbd, 0.0).astype(BF16)
    vkw_ref[...] = halves(mm_nt(vkbd, wk_ref[...]))
    vid = vid_row(load_ref, rows)
    add_pool(normed, vid, vkw_ref, pool_ref, weight_ref, scale, True)
    vcol_ref[...] = jnp.broadcast_to(vid, (128, rows)).T

    me = lax.axis_index("node")
    place = ring_place(me // CORES, chips)
    core = me % CORES
    for d in range(chips * CORES):
        want_ref[d] = 0
    for b in range(blocks):
        for e in range(slots):
            entry = sblock_ref[b, e]
            want_ref[entry // blocks] = entry % blocks
    for d in range(chips * CORES):
        step = (place - ring_place(jnp.int32(d // CORES), chips) + chips) % chips
        far = jnp.where(core == d % CORES, 0, 1)
        mask_ref[far, step] = jnp.full(mask_ref.shape[2:], want_ref[d].astype(F32), F32)
    for b in range(blocks):
        for e in range(slots):
            device = sblock_ref[b, e] // blocks
            step = (place - ring_place(device // CORES, chips) + chips) % chips
            far = jnp.where(device % CORES == core, 0, 1)
            live = jnp.where(e < scount_ref[b], 1.0, 0.0).astype(F32)
            counts_ref[far, step, b] += counts_of(srows_ref[b, e], br) * live

    zero = jnp.zeros((head, br), BF16)
    ones = jnp.ones((EXTRA, br), BF16)
    for b in range(blocks):
        cols = slice(b * br, (b + 1) * br)
        counts = counts_of(lrows_ref[:, cols], br)
        counts2 = jnp.concatenate([counts, counts], axis=1)
        for t in range(pairs):
            r0 = t * wide
            mid = r0 + head
            end = r0 + wide
            bd = jnp.concatenate(
                [
                    jnp.concatenate([qt[r0:mid, cols], zero], axis=1),
                    jnp.concatenate([zero, qt[mid:end, cols]], axis=1),
                ],
                axis=0,
            )
            qbd_ref[b, t] = bd
            values = jnp.concatenate([vt[r0:end, cols], ones], axis=0)
            fold(attend(k[cols, r0:end], values, counts2, bd, scale), num_ref, den_ref, b, t, False)


def take_sources(
    names, loads, mask_ref, gain_ref, wk_ref, wvt_ref, vkw_ref,
    normed_ref, k_ref, vt_ref, pool_ref, weight_ref,
):
    width = k_ref.shape[1]
    chosen = []
    vids = []
    for i, ((far, step), pieces) in enumerate(zip(names, loads)):
        part = norm_rows(load_rows(pieces), gain_ref[...])
        rows = part.shape[0]
        normed_ref[i * rows : (i + 1) * rows, :] = part
        chosen.append(choose(mask_ref[far, step, :1, :], part))
        vids.append(vid_row(pieces[-1], rows))
    picked = jnp.concatenate(chosen, axis=0)
    k_ref[...] = mm(picked, wk_ref[...]).astype(BF16)
    vt_ref[...] = mm_nt(wvt_ref[...], picked).astype(BF16)
    scale = (width // HEADS) ** (-0.5)
    vid = jnp.concatenate(vids, axis=1)
    add_pool(normed_ref[...], vid, vkw_ref, pool_ref, weight_ref, scale, False)


def add_sources(names, b, counts_ref, qbd_ref, k_ref, vt_ref, num_ref, den_ref):
    _, pairs, wide, _ = qbd_ref.shape
    scale = (2 / wide) ** 0.5
    counts = jnp.concatenate([counts_ref[far, step, b] for far, step in names], axis=0)
    counts2 = jnp.concatenate([counts, counts], axis=1)
    ones = jnp.ones((EXTRA, counts.shape[0]), BF16)
    for t in range(pairs):
        cols = slice(t * wide, (t + 1) * wide)
        values = jnp.concatenate([vt_ref[cols, :], ones], axis=0)
        o = attend(k_ref[:, cols], values, counts2, qbd_ref[b, t], scale)
        fold(o, num_ref, den_ref, b, t, True)


def slots_kernel(
    names, sizes, mask_ref, gain_ref, wk_ref, wvt_ref, vkw_ref, counts_ref, qbd_ref,
    num_in, den_in, pool_in, weight_in, *refs
):
    loads = grouped(refs, sizes)
    num_ref, den_ref, pool_ref, weight_ref, normed_ref, k_ref, vt_ref = refs[sum(sizes) :]
    num_ref[...] = num_in[...]
    den_ref[...] = den_in[...]
    pool_ref[...] = pool_in[...]
    weight_ref[...] = weight_in[...]
    take_sources(
        names, loads, mask_ref, gain_ref, wk_ref, wvt_ref, vkw_ref,
        normed_ref, k_ref, vt_ref, pool_ref, weight_ref,
    )
    for b in range(num_ref.shape[0]):
        add_sources(names, b, counts_ref, qbd_ref, k_ref, vt_ref, num_ref, den_ref)


def finish_kernel(
    names, mask_ref, gain_ref, wk_ref, wvt_ref, vkw_ref, counts_ref, qbd_ref,
    num_in, den_in, pool_in, weight_in, last_ref, vcol_ref, load_ref, wo_ref,
    out_ref, num_ref, den_ref, pool_ref, weight_ref, normed_ref, k_ref, vt_ref,
):
    slots_kernel(
        names, (1,), mask_ref, gain_ref, wk_ref, wvt_ref, vkw_ref, counts_ref, qbd_ref,
        num_in, den_in, pool_in, weight_in, last_ref,
        num_ref, den_ref, pool_ref, weight_ref, normed_ref, k_ref, vt_ref,
    )
    blocks, width, br = num_ref.shape
    head = width // HEADS
    lanes = vcol_ref.shape[1]
    count = pool_ref.shape[0]
    weight = jnp.concatenate([weight_ref[...]] * (width // lanes), axis=1)
    both = mm_nt(halves(pool_ref[...] / weight), wvt_ref[...])
    both = jnp.where(of_own_head((count, width)), both[:count] + both[count:], 0.0)
    pooled = [
        jnp.sum(both[j : j + HEADS], axis=0, keepdims=True) for j in range(0, count, HEADS)
    ]
    for b in range(blocks):
        part = slice(b * br, (b + 1) * br)
        vid = vcol_ref[part, :]
        att = jnp.concatenate(
            [
                num_ref[b, h * head : (h + 1) * head, :] / den_ref[b, h : h + 1, :]
                for h in range(HEADS)
            ],
            axis=0,
        ).T
        pieces = []
        for c in range(0, width, lanes):
            own = jnp.broadcast_to(pooled[0][:, c : c + lanes], (br, lanes))
            for j in range(1, len(pooled)):
                own = jnp.where(vid == float(j), pooled[j][:, c : c + lanes], own)
            pieces.append((att[:, c : c + lanes] + own).astype(BF16))
        mixed = jnp.concatenate(pieces, axis=1)
        out_ref[part, :] = (load_ref[part, :].astype(F32) + mm(mixed, wo_ref[...])).astype(BF16)


def params(mib):
    return pltpu.CompilerParams(vmem_limit_bytes=mib * 2**20)


def cost(flops):
    return pl.CostEstimate(flops=flops, bytes_accessed=1024, transcendentals=0)


def body(
    activations,
    norm_gain,
    project_in,
    project_out,
    virtual_keys,
    virtual_id,
    local_rows,
    slot_block,
    slot_count,
    slot_rows,
):
    _, rows, width = activations.shape
    br = slot_rows.shape[3]
    slots = slot_block.shape[1]
    blocks = rows // br
    devices = lax.axis_size("node")
    chips = devices // CORES
    virtual = virtual_keys.shape[1]
    pairs = HEADS // 2
    wide = width // pairs
    shape = jax.ShapeDtypeStruct
    after = lax.optimization_barrier
    unit = 2**16

    load = pl.pallas_call(
        pack_kernel,
        out_shape=shape((rows + EXTRA, width), BF16),
        in_specs=[HBM] * 2,
        out_specs=VMEM,
        scratch_shapes=[pltpu.VMEM((1, rows), jnp.int32), pltpu.SemaphoreType.DMA((2,))],
        compiler_params=params(24),
        cost_estimate=cost(unit),
        name="pack_rows",
    )(
        pltpu.with_memory_space_constraint(activations[0], pltpu.HBM),
        pltpu.with_memory_space_constraint(virtual_id.reshape(1, rows), pltpu.HBM),
    )
    near = {1: to_next_chip(load, devices, 1)}
    if chips > 2:
        near[chips - 1] = to_next_chip(load, devices, -1)
    far = {0: swapped(load, devices, 1)}

    accumulators = (
        shape((blocks, width, br), F32),
        shape((blocks, HEADS, br), F32),
        shape((virtual * HEADS, width), F32),
        shape((virtual * HEADS, 128), F32),
    )
    square = shape((width, width), BF16)
    qbd, num, den, counts, mask, vcol, wk, wvt, wo, gain, vkw, pool, weight = pl.pallas_call(
        prep_kernel,
        out_shape=(
            (shape((blocks, pairs, wide, 2 * br), BF16),)
            + accumulators[:2]
            + (
                shape((CORES, chips, blocks, br, br), F32),
                shape((CORES, chips, 8, 128), F32),
                shape((rows, 128), F32),
                square,
                square,
                square,
                shape((1, width), F32),
                shape((2 * virtual * HEADS, width), BF16),
            )
            + accumulators[2:]
        ),
        in_specs=[VMEM] + [HBM] * 8,
        out_specs=[VMEM] * 13,
        scratch_shapes=[
            pltpu.VMEM((width, width), BF16),
            pltpu.VMEM((width, width), BF16),
            pltpu.VMEM((virtual, width), BF16),
            pltpu.VMEM(local_rows.shape, jnp.int32),
            pltpu.VMEM(slot_rows.shape, jnp.int32),
            pltpu.SMEM((blocks, slots), jnp.int32),
            pltpu.SMEM((blocks,), jnp.int32),
            pltpu.SMEM((devices,), jnp.int32),
            pltpu.SemaphoreType.DMA((10,)),
        ],
        compiler_params=params(32),
        cost_estimate=cost(unit),
        name="prepare",
    )(
        load,
        *[
            pltpu.with_memory_space_constraint(value, pltpu.HBM)
            for value in (
                norm_gain, project_in[0], virtual_keys[0], local_rows, slot_rows, slot_block,
                slot_count, project_out[0],
            )
        ],
    )

    def work(count):
        return [
            pltpu.VMEM((count * rows, width), BF16),
            pltpu.VMEM((count * br, width), BF16),
            pltpu.VMEM((width, count * br), BF16),
        ]

    sums = (num, den, pool, weight)

    def arrive(step, sums):
        near[step], first = after((near[step], sums[1]))
        return (sums[0], first) + sums[2:]

    def slots_call(names, sums, name):
        loads = [(far if other else near)[step] for other, step in names]
        loads = [load if isinstance(load, list) else [load] for load in loads]
        sizes = tuple(len(load) for load in loads)
        return pl.pallas_call(
            functools.partial(slots_kernel, tuple(names), sizes),
            out_shape=accumulators,
            in_specs=[VMEM] * (11 + sum(sizes)),
            out_specs=[VMEM] * 4,
            scratch_shapes=work(len(names)),
            compiler_params=params(40),
            cost_estimate=cost(unit),
            name=name,
        )(
            mask, gain, wk, wvt, vkw, counts, qbd, *sums,
            *[piece for load in loads for piece in load],
        )

    ahead = chips // 2
    order = []
    for s in range(1, ahead + 1):
        order.append((s, 1))
        if s < chips - s:
            order.append((chips - s, -1))
    waiting = [(1, 0)]
    for i, (step, way) in enumerate(order):
        last = i == len(order) - 1
        sums = arrive(step, sums)
        if not last:
            far[step] = swapped_parts(near[step], devices, 3 if i == 0 else 2)
        else:
            far[step] = swapped(near[step], devices, 1)
        waiting.append((0, step))
        if not last:
            waiting.append((1, step))
        sums = slots_call(waiting, sums, "slots_%d" % i)
        waiting = []
        nexts = step + way
        if nexts not in near and (nexts, way) in order:
            sums = arrive(step, sums)
            near[nexts] = to_next_chip(near[step], devices, way)
    names = ((1, order[-1][0]),)
    updated = pl.pallas_call(
        functools.partial(finish_kernel, names),
        out_shape=shape((rows, width), BF16),
        in_specs=[VMEM] * 15,
        out_specs=VMEM,
        scratch_shapes=[pltpu.VMEM(leaf.shape, leaf.dtype) for leaf in accumulators] + work(1),
        compiler_params=params(40),
        cost_estimate=cost(unit),
        name="finish",
    )(
        mask, gain, wk, wvt, vkw, counts, qbd, *sums, far[names[0][1]], vcol, load, wo
    )
    return to_next_segment(updated[None])


def solution(mesh):
    placed = (
        P("segment", "node", None),
        P("segment", None),
        P("segment", None, None),
        P("segment", None, None),
        P("segment", None, None),
        P("node", None),
        P(None, "node"),
        P("node", None),
        P("node"),
        P("node", None, None, None),
    )
    return jax.shard_map(
        body, mesh=mesh, in_specs=placed, out_specs=P("segment", "node", None), check_vma=False
    )
```

```python
import functools

import jax
import jax.numpy as jnp
from jax import lax
from jax.experimental import pallas as pl
from jax.experimental.pallas import tpu as pltpu
from jax.sharding import PartitionSpec as P

HEADS = 8
CORES = 2
EPSILON = 1e-05
CAP_LIMIT = 10.0
LOG2E = 1.4426950408889634
EXTRA = 16
PARTS = 2
F32 = jnp.float32
BF16 = jnp.bfloat16
HBM = pl.BlockSpec(memory_space=pltpu.HBM)
VMEM = pl.BlockSpec(memory_space=pltpu.VMEM)


def ring_order(chips):
    return list(range(0, 1)) + list(range(1, chips, 2)) + list(range((chips - 1) // 2 * 2, 0, -2))


def ring_place(chip, chips):
    return jnp.where(chip % 2 == 1, (chip + 1) // 2, (chips - chip // 2) % chips)


def to_next_chip(value, devices, way):
    chips = devices // CORES
    order = ring_order(chips)
    pairs = [
        (order[i] * CORES + c, order[(i + way) % chips] * CORES + c)
        for i in range(chips)
        for c in range(CORES)
    ]
    return lax.ppermute(value, "node", pairs)


def swapped(value, devices, distance):
    return lax.ppermute(value, "node", [(d, d ^ distance) for d in range(devices)])


def swapped_parts(value, devices, parts):
    tiles = value.shape[0] // 16
    cuts = [0] + [16 * (-(-tiles * (i + 1) // parts)) for i in range(parts)]
    return [swapped(value[a:b], devices, 1) for a, b in zip(cuts, cuts[1:])]


def to_next_segment(value):
    count = lax.axis_size("segment")
    return lax.ppermute(value, "segment", [(s, (s + 1) % count) for s in range(count)])


def norm_rows(rows_in, gain_row):
    widened = rows_in.astype(F32)
    center = widened - jnp.mean(widened, axis=-1, keepdims=True)
    spread = jnp.mean(center * center, axis=-1, keepdims=True)
    return (center * lax.rsqrt(spread + EPSILON) * gain_row).astype(BF16)


def exp_capped(raw, scale):
    return jnp.exp2((CAP_LIMIT * LOG2E) * jnp.tanh(raw * (scale / CAP_LIMIT)))


def counts_of(index_rows, block_rows):
    rows = lax.broadcasted_iota(jnp.int32, (block_rows, index_rows.shape[1]), 0)
    total = jnp.zeros(rows.shape, F32)
    for j in range(index_rows.shape[0]):
        total = total + jnp.where(index_rows[j : j + 1, :] == rows, 1.0, 0.0)
    return total


def mm(a, b):
    return jnp.dot(a, b, preferred_element_type=F32)


def mm_nt(a, b):
    return lax.dot_general(a, b, (((1,), (1,)), ((), ())), preferred_element_type=F32)


def choose(mask_row, rows):
    lanes = mask_row.shape[1]
    count, width = rows.shape
    br = count // 2
    mask = jnp.broadcast_to(mask_row, (br, lanes))
    mask = jnp.concatenate([mask] * (width // lanes), axis=1)
    first, second = rows[:br, :].astype(F32), rows[br:, :].astype(F32)
    return jnp.where(mask > 0.5, second, first).astype(rows.dtype)


def halves(value):
    high = value.astype(BF16)
    low = (value - high.astype(F32)).astype(BF16)
    return jnp.concatenate([high, low], axis=0)


def of_own_head(shape):
    head = lax.broadcasted_iota(jnp.int32, shape, 0) % HEADS
    return head == lax.broadcasted_iota(jnp.int32, shape, 1) // (shape[1] // HEADS)


def add_pool(normed, vid_row, vkw_ref, pool_ref, weight_ref, scale, first):
    count = pool_ref.shape[0]
    raw = mm_nt(vkw_ref[...], normed)
    raw = raw[:count] + raw[count:]
    owner = lax.broadcasted_iota(jnp.int32, raw.shape, 0) // HEADS
    w = jnp.where(vid_row == owner.astype(F32), exp_capped(raw, scale), 0.0).astype(BF16)
    sums = mm(w, normed)
    totals = jnp.broadcast_to(
        jnp.sum(w.astype(F32), axis=1, keepdims=True), weight_ref.shape
    )
    pool_ref[...] = sums if first else pool_ref[...] + sums
    weight_ref[...] = totals if first else weight_ref[...] + totals


def start_copies(pairs, sems):
    copies = [pltpu.make_async_copy(src, dst, sems.at[i]) for i, (src, dst) in enumerate(pairs)]
    for copy in copies:
        copy.start()
    return copies


def pack_kernel(x_hbm, vid_hbm, load_ref, vid_ref, sems):
    rows = vid_ref.shape[1]
    copies = start_copies([(x_hbm, load_ref.at[:rows, :]), (vid_hbm, vid_ref)], sems)
    copies[1].wait()
    tile = jnp.broadcast_to(vid_ref[...].astype(F32), (EXTRA, rows))
    rest = jnp.zeros((EXTRA, load_ref.shape[1] - rows), F32)
    load_ref[rows:, :] = jnp.concatenate([tile, rest], axis=1).astype(BF16)
    copies[0].wait()


def vid_row(load_ref, rows):
    last = load_ref.shape[0]
    return load_ref[last - EXTRA :, :rows].astype(F32)[:1, :]


def load_rows(refs):
    last = refs[-1].shape[0] - EXTRA
    return jnp.concatenate([ref[...] for ref in refs[:-1]] + [refs[-1][:last, :]], axis=0)


def grouped(refs, sizes):
    groups = []
    for size in sizes:
        groups.append(refs[:size])
        refs = refs[size:]
    return groups


def attend(keys, values, counts, qbd, scale):
    p = (counts * exp_capped(mm(keys, qbd), scale)).astype(BF16)
    return mm(values, p)


def fold(o, num_ref, den_ref, b, t, add):
    wide = o.shape[0] - EXTRA
    head = wide // 2
    br = o.shape[1] // 2
    r0 = t * wide
    places = (
        (num_ref, slice(r0, r0 + head), o[:head, :br]),
        (num_ref, slice(r0 + head, r0 + wide), o[head:wide, br:]),
        (den_ref, slice(2 * t, 2 * t + 1), o[wide : wide + 1, :br]),
        (den_ref, slice(2 * t + 1, 2 * t + 2), o[wide : wide + 1, br:]),
    )
    for ref, part, value in places:
        if add:
            ref[b, part, :] += value
        else:
            ref[b, part, :] = value


def prep_kernel(
    load_ref, gain_hbm, win_hbm, vk_hbm, lrows_hbm, srows_hbm, sblock_hbm, scount_hbm, wo_hbm,
    qbd_ref, num_ref, den_ref, counts_ref, mask_ref, vcol_ref, wk_ref, wvt_ref, wo_ref, gain_ref,
    vkw_ref, pool_ref, weight_ref,
    wq_ref, wv_ref, vk_ref, lrows_ref, srows_ref, sblock_ref, scount_ref, want_ref, sems,
):
    width = load_ref.shape[1]
    rows = load_ref.shape[0] - EXTRA
    blocks, pairs, wide, _ = qbd_ref.shape
    chips = mask_ref.shape[1]
    slots = sblock_ref.shape[1]
    virtual = vk_ref.shape[0]
    br = rows // blocks
    head = width // HEADS
    scale = head ** (-0.5)
    copies = start_copies(
        [
            (gain_hbm, gain_ref), (sblock_hbm, sblock_ref), (scount_hbm, scount_ref),
            (srows_hbm, srows_ref), (lrows_hbm, lrows_ref), (vk_hbm, vk_ref),
            (win_hbm.at[:, width : 2 * width], wk_ref), (win_hbm.at[:, :width], wq_ref),
            (win_hbm.at[:, 2 * width :], wv_ref), (wo_hbm, wo_ref),
        ],
        sems,
    )
    counts_ref[...] = jnp.zeros(counts_ref.shape, F32)
    for copy in copies:
        copy.wait()
    normed = norm_rows(load_ref[:rows, :], gain_ref[...])
    k = mm(normed, wk_ref[...]).astype(BF16)
    v = mm(normed, wv_ref[...]).astype(BF16)
    qt = mm(normed, wq_ref[...]).astype(BF16).T
    vt = v.T
    wvt_ref[...] = wv_ref[...].T

    vkf = vk_ref[...].astype(F32)
    vkbd = jnp.concatenate(
        [jnp.broadcast_to(vkf[j : j + 1, :], (HEADS, width)) for j in range(virtual)], axis=0
    )
    vkbd = jnp.where(of_own_head(vkbd.shape), vkbd, 0.0).astype(BF16)
    vkw_ref[...] = halves(mm_nt(vkbd, wk_ref[...]))
    vid = vid_row(load_ref, rows)
    add_pool(normed, vid, vkw_ref, pool_ref, weight_ref, scale, True)
    vcol_ref[...] = jnp.broadcast_to(vid, (128, rows)).T

    me = lax.axis_index("node")
    place = ring_place(me // CORES, chips)
    core = me % CORES
    for d in range(chips * CORES):
        want_ref[d] = 0
    for b in range(blocks):
        for e in range(slots):
            entry = sblock_ref[b, e]
            want_ref[entry // blocks] = entry % blocks
    for d in range(chips * CORES):
        step = (place - ring_place(jnp.int32(d // CORES), chips) + chips) % chips
        far = jnp.where(core == d % CORES, 0, 1)
        mask_ref[far, step] = jnp.full(mask_ref.shape[2:], want_ref[d].astype(F32), F32)
    for b in range(blocks):
        for e in range(slots):
            device = sblock_ref[b, e] // blocks
            step = (place - ring_place(device // CORES, chips) + chips) % chips
            far = jnp.where(device % CORES == core, 0, 1)
            live = jnp.where(e < scount_ref[b], 1.0, 0.0).astype(F32)
            counts_ref[far, step, b] += counts_of(srows_ref[b, e], br) * live

    zero = jnp.zeros((head, br), BF16)
    ones = jnp.ones((EXTRA, br), BF16)
    for b in range(blocks):
        cols = slice(b * br, (b + 1) * br)
        counts = counts_of(lrows_ref[:, cols], br)
        counts2 = jnp.concatenate([counts, counts], axis=1)
        for t in range(pairs):
            r0 = t * wide
            mid = r0 + head
            end = r0 + wide
            bd = jnp.concatenate(
                [
                    jnp.concatenate([qt[r0:mid, cols], zero], axis=1),
                    jnp.concatenate([zero, qt[mid:end, cols]], axis=1),
                ],
                axis=0,
            )
            qbd_ref[b, t] = bd
            values = jnp.concatenate([vt[r0:end, cols], ones], axis=0)
            fold(attend(k[cols, r0:end], values, counts2, bd, scale), num_ref, den_ref, b, t, False)


def take_sources(
    names, loads, mask_ref, gain_ref, wk_ref, wvt_ref, vkw_ref,
    normed_ref, k_ref, vt_ref, pool_ref, weight_ref,
):
    width = k_ref.shape[1]
    chosen = []
    vids = []
    for i, ((far, step), pieces) in enumerate(zip(names, loads)):
        part = norm_rows(load_rows(pieces), gain_ref[...])
        rows = part.shape[0]
        normed_ref[i * rows : (i + 1) * rows, :] = part
        chosen.append(choose(mask_ref[far, step, :1, :], part))
        vids.append(vid_row(pieces[-1], rows))
    picked = jnp.concatenate(chosen, axis=0)
    k_ref[...] = mm(picked, wk_ref[...]).astype(BF16)
    vt_ref[...] = mm_nt(wvt_ref[...], picked).astype(BF16)
    scale = (width // HEADS) ** (-0.5)
    vid = jnp.concatenate(vids, axis=1)
    add_pool(normed_ref[...], vid, vkw_ref, pool_ref, weight_ref, scale, False)


def add_sources(names, b, counts_ref, qbd_ref, k_ref, vt_ref, num_ref, den_ref):
    _, pairs, wide, _ = qbd_ref.shape
    scale = (2 / wide) ** 0.5
    counts = jnp.concatenate([counts_ref[far, step, b] for far, step in names], axis=0)
    counts2 = jnp.concatenate([counts, counts], axis=1)
    ones = jnp.ones((EXTRA, counts.shape[0]), BF16)
    for t in range(pairs):
        cols = slice(t * wide, (t + 1) * wide)
        values = jnp.concatenate([vt_ref[cols, :], ones], axis=0)
        o = attend(k_ref[:, cols], values, counts2, qbd_ref[b, t], scale)
        fold(o, num_ref, den_ref, b, t, True)


def slots_kernel(
    names, sizes, mask_ref, gain_ref, wk_ref, wvt_ref, vkw_ref, counts_ref, qbd_ref,
    num_in, den_in, pool_in, weight_in, *refs
):
    loads = grouped(refs, sizes)
    num_ref, den_ref, pool_ref, weight_ref, normed_ref, k_ref, vt_ref = refs[sum(sizes) :]
    num_ref[...] = num_in[...]
    den_ref[...] = den_in[...]
    pool_ref[...] = pool_in[...]
    weight_ref[...] = weight_in[...]
    take_sources(
        names, loads, mask_ref, gain_ref, wk_ref, wvt_ref, vkw_ref,
        normed_ref, k_ref, vt_ref, pool_ref, weight_ref,
    )
    for b in range(num_ref.shape[0]):
        add_sources(names, b, counts_ref, qbd_ref, k_ref, vt_ref, num_ref, den_ref)


def finish_kernel(
    names, mask_ref, gain_ref, wk_ref, wvt_ref, vkw_ref, counts_ref, qbd_ref,
    num_in, den_in, pool_in, weight_in, last_ref, vcol_ref, load_ref, wo_ref,
    out_ref, num_ref, den_ref, pool_ref, weight_ref, normed_ref, k_ref, vt_ref,
):
    slots_kernel(
        names, (1,), mask_ref, gain_ref, wk_ref, wvt_ref, vkw_ref, counts_ref, qbd_ref,
        num_in, den_in, pool_in, weight_in, last_ref,
        num_ref, den_ref, pool_ref, weight_ref, normed_ref, k_ref, vt_ref,
    )
    blocks, width, br = num_ref.shape
    head = width // HEADS
    lanes = vcol_ref.shape[1]
    count = pool_ref.shape[0]
    weight = jnp.concatenate([weight_ref[...]] * (width // lanes), axis=1)
    both = mm_nt(halves(pool_ref[...] / weight), wvt_ref[...])
    both = jnp.where(of_own_head((count, width)), both[:count] + both[count:], 0.0)
    pooled = [
        jnp.sum(both[j : j + HEADS], axis=0, keepdims=True) for j in range(0, count, HEADS)
    ]
    for b in range(blocks):
        part = slice(b * br, (b + 1) * br)
        vid = vcol_ref[part, :]
        att = jnp.concatenate(
            [
                num_ref[b, h * head : (h + 1) * head, :] / den_ref[b, h : h + 1, :]
                for h in range(HEADS)
            ],
            axis=0,
        ).T
        pieces = []
        for c in range(0, width, lanes):
            own = jnp.broadcast_to(pooled[0][:, c : c + lanes], (br, lanes))
            for j in range(1, len(pooled)):
                own = jnp.where(vid == float(j), pooled[j][:, c : c + lanes], own)
            pieces.append((att[:, c : c + lanes] + own).astype(BF16))
        mixed = jnp.concatenate(pieces, axis=1)
        out_ref[part, :] = (load_ref[part, :].astype(F32) + mm(mixed, wo_ref[...])).astype(BF16)


def params(mib):
    return pltpu.CompilerParams(vmem_limit_bytes=mib * 2**20)


def cost(flops):
    return pl.CostEstimate(flops=flops, bytes_accessed=1024, transcendentals=0)


def body(
    activations,
    norm_gain,
    project_in,
    project_out,
    virtual_keys,
    virtual_id,
    local_rows,
    slot_block,
    slot_count,
    slot_rows,
):
    _, rows, width = activations.shape
    br = slot_rows.shape[3]
    slots = slot_block.shape[1]
    blocks = rows // br
    devices = lax.axis_size("node")
    chips = devices // CORES
    virtual = virtual_keys.shape[1]
    pairs = HEADS // 2
    wide = width // pairs
    shape = jax.ShapeDtypeStruct
    after = lax.optimization_barrier
    unit = 2**16

    load = pl.pallas_call(
        pack_kernel,
        out_shape=shape((rows + EXTRA, width), BF16),
        in_specs=[HBM] * 2,
        out_specs=VMEM,
        scratch_shapes=[pltpu.VMEM((1, rows), jnp.int32), pltpu.SemaphoreType.DMA((2,))],
        compiler_params=params(24),
        cost_estimate=cost(unit),
        name="pack_rows",
    )(
        pltpu.with_memory_space_constraint(activations[0], pltpu.HBM),
        pltpu.with_memory_space_constraint(virtual_id.reshape(1, rows), pltpu.HBM),
    )
    near = {1: to_next_chip(load, devices, 1)}
    far = {0: swapped(load, devices, 1)}

    accumulators = (
        shape((blocks, width, br), F32),
        shape((blocks, HEADS, br), F32),
        shape((virtual * HEADS, width), F32),
        shape((virtual * HEADS, 128), F32),
    )
    square = shape((width, width), BF16)
    qbd, num, den, counts, mask, vcol, wk, wvt, wo, gain, vkw, pool, weight = pl.pallas_call(
        prep_kernel,
        out_shape=(
            (shape((blocks, pairs, wide, 2 * br), BF16),)
            + accumulators[:2]
            + (
                shape((CORES, chips, blocks, br, br), F32),
                shape((CORES, chips, 8, 128), F32),
                shape((rows, 128), F32),
                square,
                square,
                square,
                shape((1, width), F32),
                shape((2 * virtual * HEADS, width), BF16),
            )
            + accumulators[2:]
        ),
        in_specs=[VMEM] + [HBM] * 8,
        out_specs=[VMEM] * 13,
        scratch_shapes=[
            pltpu.VMEM((width, width), BF16),
            pltpu.VMEM((width, width), BF16),
            pltpu.VMEM((virtual, width), BF16),
            pltpu.VMEM(local_rows.shape, jnp.int32),
            pltpu.VMEM(slot_rows.shape, jnp.int32),
            pltpu.SMEM((blocks, slots), jnp.int32),
            pltpu.SMEM((blocks,), jnp.int32),
            pltpu.SMEM((devices,), jnp.int32),
            pltpu.SemaphoreType.DMA((10,)),
        ],
        compiler_params=params(32),
        cost_estimate=cost(unit),
        name="prepare",
    )(
        load,
        *[
            pltpu.with_memory_space_constraint(value, pltpu.HBM)
            for value in (
                norm_gain, project_in[0], virtual_keys[0], local_rows, slot_rows, slot_block,
                slot_count, project_out[0],
            )
        ],
    )

    def work(count):
        return [
            pltpu.VMEM((count * rows, width), BF16),
            pltpu.VMEM((count * br, width), BF16),
            pltpu.VMEM((width, count * br), BF16),
        ]

    if chips > 2:
        back, den = after((load, den))
        near[chips - 1] = to_next_chip(back, devices, -1)
    sums = (num, den, pool, weight)

    def arrive(step, sums):
        near[step], first = after((near[step], sums[1]))
        return (sums[0], first) + sums[2:]

    def slots_call(names, sums, name):
        loads = [(far if other else near)[step] for other, step in names]
        loads = [load if isinstance(load, list) else [load] for load in loads]
        sizes = tuple(len(load) for load in loads)
        return pl.pallas_call(
            functools.partial(slots_kernel, tuple(names), sizes),
            out_shape=accumulators,
            in_specs=[VMEM] * (11 + sum(sizes)),
            out_specs=[VMEM] * 4,
            scratch_shapes=work(len(names)),
            compiler_params=params(40),
            cost_estimate=cost(unit),
            name=name,
        )(
            mask, gain, wk, wvt, vkw, counts, qbd, *sums,
            *[piece for load in loads for piece in load],
        )

    ahead = chips // 2
    order = []
    for s in range(1, ahead + 1):
        order.append((s, 1))
        if s < chips - s:
            order.append((chips - s, -1))
    waiting = [(1, 0)]
    for i, (step, way) in enumerate(order):
        last = i == len(order) - 1
        sums = arrive(step, sums)
        if not last:
            far[step] = swapped_parts(near[step], devices, PARTS)
        else:
            far[step] = swapped(near[step], devices, 1)
        nexts = step + way
        if nexts not in near and (nexts, way) in order:
            near[nexts] = to_next_chip(near[step], devices, way)
        waiting.append((0, step))
        if not last:
            waiting.append((1, step))
        sums = slots_call(waiting, sums, "slots_%d" % i)
        waiting = []
    names = ((1, order[-1][0]),)
    updated = pl.pallas_call(
        functools.partial(finish_kernel, names),
        out_shape=shape((rows, width), BF16),
        in_specs=[VMEM] * 15,
        out_specs=VMEM,
        scratch_shapes=[pltpu.VMEM(leaf.shape, leaf.dtype) for leaf in accumulators] + work(1),
        compiler_params=params(40),
        cost_estimate=cost(unit),
        name="finish",
    )(
        mask, gain, wk, wvt, vkw, counts, qbd, *sums, far[names[0][1]], vcol, load, wo
    )
    return to_next_segment(updated[None])


def solution(mesh):
    placed = (
        P("segment", "node", None),
        P("segment", None),
        P("segment", None, None),
        P("segment", None, None),
        P("segment", None, None),
        P("node", None),
        P(None, "node"),
        P("node", None),
        P("node"),
        P("node", None, None, None),
    )
    return jax.shard_map(
        body, mesh=mesh, in_specs=placed, out_specs=P("segment", "node", None), check_vma=False
    )
```

```python
import functools

import jax
import jax.numpy as jnp
from jax import lax
from jax.experimental import pallas as pl
from jax.experimental.pallas import tpu as pltpu
from jax.sharding import PartitionSpec as P

HEADS = 8
CORES = 2
EPSILON = 1e-05
CAP_LIMIT = 10.0
LOG2E = 1.4426950408889634
EXTRA = 16
PARTS = 2
F32 = jnp.float32
BF16 = jnp.bfloat16
HBM = pl.BlockSpec(memory_space=pltpu.HBM)
VMEM = pl.BlockSpec(memory_space=pltpu.VMEM)


def ring_order(chips):
    return list(range(0, 1)) + list(range(1, chips, 2)) + list(range((chips - 1) // 2 * 2, 0, -2))


def ring_place(chip, chips):
    return jnp.where(chip % 2 == 1, (chip + 1) // 2, (chips - chip // 2) % chips)


def to_next_chip(value, devices, way):
    chips = devices // CORES
    order = ring_order(chips)
    pairs = [
        (order[i] * CORES + c, order[(i + way) % chips] * CORES + c)
        for i in range(chips)
        for c in range(CORES)
    ]
    return lax.ppermute(value, "node", pairs)


def swapped(value, devices, distance):
    return lax.ppermute(value, "node", [(d, d ^ distance) for d in range(devices)])


def swapped_parts(value, devices, parts):
    tiles = value.shape[0] // 16
    cuts = [0] + [16 * (-(-tiles * (i + 1) // parts)) for i in range(parts)]
    return [swapped(value[a:b], devices, 1) for a, b in zip(cuts, cuts[1:])]


def to_next_segment(value):
    count = lax.axis_size("segment")
    return lax.ppermute(value, "segment", [(s, (s + 1) % count) for s in range(count)])


def norm_rows(rows_in, gain_row):
    widened = rows_in.astype(F32)
    center = widened - jnp.mean(widened, axis=-1, keepdims=True)
    spread = jnp.mean(center * center, axis=-1, keepdims=True)
    return (center * lax.rsqrt(spread + EPSILON) * gain_row).astype(BF16)


def exp_capped(raw, scale):
    return jnp.exp2((CAP_LIMIT * LOG2E) * jnp.tanh(raw * (scale / CAP_LIMIT)))


def counts_of(index_rows, block_rows):
    rows = lax.broadcasted_iota(jnp.int32, (block_rows, index_rows.shape[1]), 0)
    total = jnp.zeros(rows.shape, F32)
    for j in range(index_rows.shape[0]):
        total = total + jnp.where(index_rows[j : j + 1, :] == rows, 1.0, 0.0)
    return total


def mm(a, b):
    return jnp.dot(a, b, preferred_element_type=F32)


def mm_nt(a, b):
    return lax.dot_general(a, b, (((1,), (1,)), ((), ())), preferred_element_type=F32)


def choose(mask_row, rows):
    lanes = mask_row.shape[1]
    count, width = rows.shape
    br = count // 2
    mask = jnp.broadcast_to(mask_row, (br, lanes))
    mask = jnp.concatenate([mask] * (width // lanes), axis=1)
    first, second = rows[:br, :].astype(F32), rows[br:, :].astype(F32)
    return jnp.where(mask > 0.5, second, first).astype(rows.dtype)


def halves(value):
    high = value.astype(BF16)
    low = (value - high.astype(F32)).astype(BF16)
    return jnp.concatenate([high, low], axis=0)


def of_own_head(shape):
    head = lax.broadcasted_iota(jnp.int32, shape, 0) % HEADS
    return head == lax.broadcasted_iota(jnp.int32, shape, 1) // (shape[1] // HEADS)


def add_pool(normed, vid_row, vkw_ref, pool_ref, weight_ref, scale, first):
    count = pool_ref.shape[0]
    raw = mm_nt(vkw_ref[...], normed)
    raw = raw[:count] + raw[count:]
    owner = lax.broadcasted_iota(jnp.int32, raw.shape, 0) // HEADS
    w = jnp.where(vid_row == owner.astype(F32), exp_capped(raw, scale), 0.0).astype(BF16)
    sums = mm(w, normed)
    totals = jnp.broadcast_to(
        jnp.sum(w.astype(F32), axis=1, keepdims=True), weight_ref.shape
    )
    pool_ref[...] = sums if first else pool_ref[...] + sums
    weight_ref[...] = totals if first else weight_ref[...] + totals


def start_copies(pairs, sems):
    copies = [pltpu.make_async_copy(src, dst, sems.at[i]) for i, (src, dst) in enumerate(pairs)]
    for copy in copies:
        copy.start()
    return copies


def pack_kernel(x_hbm, vid_hbm, load_ref, vid_ref, sems):
    rows = vid_ref.shape[1]
    copies = start_copies([(x_hbm, load_ref.at[:rows, :]), (vid_hbm, vid_ref)], sems)
    copies[1].wait()
    tile = jnp.broadcast_to(vid_ref[...].astype(F32), (EXTRA, rows))
    rest = jnp.zeros((EXTRA, load_ref.shape[1] - rows), F32)
    load_ref[rows:, :] = jnp.concatenate([tile, rest], axis=1).astype(BF16)
    copies[0].wait()


def vid_row(load_ref, rows):
    last = load_ref.shape[0]
    return load_ref[last - EXTRA :, :rows].astype(F32)[:1, :]


def load_rows(refs):
    last = refs[-1].shape[0] - EXTRA
    return jnp.concatenate([ref[...] for ref in refs[:-1]] + [refs[-1][:last, :]], axis=0)


def grouped(refs, sizes):
    groups = []
    for size in sizes:
        groups.append(refs[:size])
        refs = refs[size:]
    return groups


def attend(keys, values, counts, qbd, scale):
    p = (counts * exp_capped(mm(keys, qbd), scale)).astype(BF16)
    return mm(values, p)


def fold(o, num_ref, den_ref, b, t, add):
    wide = o.shape[0] - EXTRA
    head = wide // 2
    br = o.shape[1] // 2
    r0 = t * wide
    places = (
        (num_ref, slice(r0, r0 + head), o[:head, :br]),
        (num_ref, slice(r0 + head, r0 + wide), o[head:wide, br:]),
        (den_ref, slice(2 * t, 2 * t + 1), o[wide : wide + 1, :br]),
        (den_ref, slice(2 * t + 1, 2 * t + 2), o[wide : wide + 1, br:]),
    )
    for ref, part, value in places:
        if add:
            ref[b, part, :] += value
        else:
            ref[b, part, :] = value


def prep_kernel(
    load_ref, gain_hbm, win_hbm, vk_hbm, lrows_hbm, srows_hbm, sblock_hbm, scount_hbm, wo_hbm,
    qbd_ref, num_ref, den_ref, counts_ref, mask_ref, vcol_ref, wk_ref, wvt_ref, wo_ref, gain_ref,
    vkw_ref, pool_ref, weight_ref,
    wq_ref, wv_ref, vk_ref, lrows_ref, srows_ref, sblock_ref, scount_ref, want_ref, sems,
):
    width = load_ref.shape[1]
    rows = load_ref.shape[0] - EXTRA
    blocks, pairs, wide, _ = qbd_ref.shape
    chips = mask_ref.shape[1]
    slots = sblock_ref.shape[1]
    virtual = vk_ref.shape[0]
    br = rows // blocks
    head = width // HEADS
    scale = head ** (-0.5)
    copies = start_copies(
        [
            (gain_hbm, gain_ref), (sblock_hbm, sblock_ref), (scount_hbm, scount_ref),
            (srows_hbm, srows_ref), (lrows_hbm, lrows_ref), (vk_hbm, vk_ref),
            (win_hbm.at[:, width : 2 * width], wk_ref), (win_hbm.at[:, :width], wq_ref),
            (win_hbm.at[:, 2 * width :], wv_ref), (wo_hbm, wo_ref),
        ],
        sems,
    )
    counts_ref[...] = jnp.zeros(counts_ref.shape, F32)
    for copy in copies:
        copy.wait()
    normed = norm_rows(load_ref[:rows, :], gain_ref[...])
    k = mm(normed, wk_ref[...]).astype(BF16)
    v = mm(normed, wv_ref[...]).astype(BF16)
    qt = mm(normed, wq_ref[...]).astype(BF16).T
    vt = v.T
    wvt_ref[...] = wv_ref[...].T

    vkf = vk_ref[...].astype(F32)
    vkbd = jnp.concatenate(
        [jnp.broadcast_to(vkf[j : j + 1, :], (HEADS, width)) for j in range(virtual)], axis=0
    )
    vkbd = jnp.where(of_own_head(vkbd.shape), vkbd, 0.0).astype(BF16)
    vkw_ref[...] = halves(mm_nt(vkbd, wk_ref[...]))
    vid = vid_row(load_ref, rows)
    add_pool(normed, vid, vkw_ref, pool_ref, weight_ref, scale, True)
    vcol_ref[...] = jnp.broadcast_to(vid, (128, rows)).T

    me = lax.axis_index("node")
    place = ring_place(me // CORES, chips)
    core = me % CORES
    for d in range(chips * CORES):
        want_ref[d] = 0
    for b in range(blocks):
        for e in range(slots):
            entry = sblock_ref[b, e]
            want_ref[entry // blocks] = entry % blocks
    for d in range(chips * CORES):
        step = (place - ring_place(jnp.int32(d // CORES), chips) + chips) % chips
        far = jnp.where(core == d % CORES, 0, 1)
        mask_ref[far, step] = jnp.full(mask_ref.shape[2:], want_ref[d].astype(F32), F32)
    for b in range(blocks):
        for e in range(slots):
            device = sblock_ref[b, e] // blocks
            step = (place - ring_place(device // CORES, chips) + chips) % chips
            far = jnp.where(device % CORES == core, 0, 1)
            live = jnp.where(e < scount_ref[b], 1.0, 0.0).astype(F32)
            counts_ref[far, step, b] += counts_of(srows_ref[b, e], br) * live

    zero = jnp.zeros((head, br), BF16)
    ones = jnp.ones((EXTRA, br), BF16)
    for b in range(blocks):
        cols = slice(b * br, (b + 1) * br)
        counts = counts_of(lrows_ref[:, cols], br)
        counts2 = jnp.concatenate([counts, counts], axis=1)
        for t in range(pairs):
            r0 = t * wide
            mid = r0 + head
            end = r0 + wide
            bd = jnp.concatenate(
                [
                    jnp.concatenate([qt[r0:mid, cols], zero], axis=1),
                    jnp.concatenate([zero, qt[mid:end, cols]], axis=1),
                ],
                axis=0,
            )
            qbd_ref[b, t] = bd
            values = jnp.concatenate([vt[r0:end, cols], ones], axis=0)
            fold(attend(k[cols, r0:end], values, counts2, bd, scale), num_ref, den_ref, b, t, False)


def take_sources(
    names, loads, mask_ref, gain_ref, wk_ref, wvt_ref, vkw_ref,
    normed_ref, k_ref, vt_ref, pool_ref, weight_ref,
):
    width = k_ref.shape[1]
    chosen = []
    vids = []
    for i, ((far, step), pieces) in enumerate(zip(names, loads)):
        part = norm_rows(load_rows(pieces), gain_ref[...])
        rows = part.shape[0]
        normed_ref[i * rows : (i + 1) * rows, :] = part
        chosen.append(choose(mask_ref[far, step, :1, :], part))
        vids.append(vid_row(pieces[-1], rows))
    picked = jnp.concatenate(chosen, axis=0)
    k_ref[...] = mm(picked, wk_ref[...]).astype(BF16)
    vt_ref[...] = mm_nt(wvt_ref[...], picked).astype(BF16)
    scale = (width // HEADS) ** (-0.5)
    vid = jnp.concatenate(vids, axis=1)
    add_pool(normed_ref[...], vid, vkw_ref, pool_ref, weight_ref, scale, False)


def add_sources(names, b, counts_ref, qbd_ref, k_ref, vt_ref, num_ref, den_ref):
    _, pairs, wide, _ = qbd_ref.shape
    scale = (2 / wide) ** 0.5
    counts = jnp.concatenate([counts_ref[far, step, b] for far, step in names], axis=0)
    counts2 = jnp.concatenate([counts, counts], axis=1)
    ones = jnp.ones((EXTRA, counts.shape[0]), BF16)
    for t in range(pairs):
        cols = slice(t * wide, (t + 1) * wide)
        values = jnp.concatenate([vt_ref[cols, :], ones], axis=0)
        o = attend(k_ref[:, cols], values, counts2, qbd_ref[b, t], scale)
        fold(o, num_ref, den_ref, b, t, True)


def slots_kernel(
    names, sizes, mask_ref, gain_ref, wk_ref, wvt_ref, vkw_ref, counts_ref, qbd_ref,
    num_in, den_in, pool_in, weight_in, *refs
):
    loads = grouped(refs, sizes)
    num_ref, den_ref, pool_ref, weight_ref, normed_ref, k_ref, vt_ref = refs[sum(sizes) :]
    num_ref[...] = num_in[...]
    den_ref[...] = den_in[...]
    pool_ref[...] = pool_in[...]
    weight_ref[...] = weight_in[...]
    take_sources(
        names, loads, mask_ref, gain_ref, wk_ref, wvt_ref, vkw_ref,
        normed_ref, k_ref, vt_ref, pool_ref, weight_ref,
    )
    for b in range(num_ref.shape[0]):
        add_sources(names, b, counts_ref, qbd_ref, k_ref, vt_ref, num_ref, den_ref)


def finish_kernel(
    names, mask_ref, gain_ref, wk_ref, wvt_ref, vkw_ref, counts_ref, qbd_ref,
    num_in, den_in, pool_in, weight_in, last_ref, vcol_ref, load_ref, wo_ref,
    out_ref, num_ref, den_ref, pool_ref, weight_ref, normed_ref, k_ref, vt_ref,
):
    slots_kernel(
        names, (1,), mask_ref, gain_ref, wk_ref, wvt_ref, vkw_ref, counts_ref, qbd_ref,
        num_in, den_in, pool_in, weight_in, last_ref,
        num_ref, den_ref, pool_ref, weight_ref, normed_ref, k_ref, vt_ref,
    )
    blocks, width, br = num_ref.shape
    head = width // HEADS
    lanes = vcol_ref.shape[1]
    count = pool_ref.shape[0]
    weight = jnp.concatenate([weight_ref[...]] * (width // lanes), axis=1)
    both = mm_nt(halves(pool_ref[...] / weight), wvt_ref[...])
    both = jnp.where(of_own_head((count, width)), both[:count] + both[count:], 0.0)
    pooled = [
        jnp.sum(both[j : j + HEADS], axis=0, keepdims=True) for j in range(0, count, HEADS)
    ]
    for b in range(blocks):
        part = slice(b * br, (b + 1) * br)
        vid = vcol_ref[part, :]
        att = jnp.concatenate(
            [
                num_ref[b, h * head : (h + 1) * head, :] / den_ref[b, h : h + 1, :]
                for h in range(HEADS)
            ],
            axis=0,
        ).T
        pieces = []
        for c in range(0, width, lanes):
            own = jnp.broadcast_to(pooled[0][:, c : c + lanes], (br, lanes))
            for j in range(1, len(pooled)):
                own = jnp.where(vid == float(j), pooled[j][:, c : c + lanes], own)
            pieces.append((att[:, c : c + lanes] + own).astype(BF16))
        mixed = jnp.concatenate(pieces, axis=1)
        out_ref[part, :] = (load_ref[part, :].astype(F32) + mm(mixed, wo_ref[...])).astype(BF16)


def params(mib):
    return pltpu.CompilerParams(vmem_limit_bytes=mib * 2**20)


def cost(flops):
    return pl.CostEstimate(flops=flops, bytes_accessed=1024, transcendentals=0)


def body(
    activations,
    norm_gain,
    project_in,
    project_out,
    virtual_keys,
    virtual_id,
    local_rows,
    slot_block,
    slot_count,
    slot_rows,
):
    _, rows, width = activations.shape
    br = slot_rows.shape[3]
    slots = slot_block.shape[1]
    blocks = rows // br
    devices = lax.axis_size("node")
    chips = devices // CORES
    virtual = virtual_keys.shape[1]
    pairs = HEADS // 2
    wide = width // pairs
    shape = jax.ShapeDtypeStruct
    after = lax.optimization_barrier
    unit = 2**16

    load = pl.pallas_call(
        pack_kernel,
        out_shape=shape((rows + EXTRA, width), BF16),
        in_specs=[HBM] * 2,
        out_specs=VMEM,
        scratch_shapes=[pltpu.VMEM((1, rows), jnp.int32), pltpu.SemaphoreType.DMA((2,))],
        compiler_params=params(24),
        cost_estimate=cost(unit),
        name="pack_rows",
    )(
        pltpu.with_memory_space_constraint(activations[0], pltpu.HBM),
        pltpu.with_memory_space_constraint(virtual_id.reshape(1, rows), pltpu.HBM),
    )
    near = {1: to_next_chip(load, devices, 1)}
    far = {0: swapped(load, devices, 1)}

    accumulators = (
        shape((blocks, width, br), F32),
        shape((blocks, HEADS, br), F32),
        shape((virtual * HEADS, width), F32),
        shape((virtual * HEADS, 128), F32),
    )
    square = shape((width, width), BF16)
    qbd, num, den, counts, mask, vcol, wk, wvt, wo, gain, vkw, pool, weight = pl.pallas_call(
        prep_kernel,
        out_shape=(
            (shape((blocks, pairs, wide, 2 * br), BF16),)
            + accumulators[:2]
            + (
                shape((CORES, chips, blocks, br, br), F32),
                shape((CORES, chips, 8, 128), F32),
                shape((rows, 128), F32),
                square,
                square,
                square,
                shape((1, width), F32),
                shape((2 * virtual * HEADS, width), BF16),
            )
            + accumulators[2:]
        ),
        in_specs=[VMEM] + [HBM] * 8,
        out_specs=[VMEM] * 13,
        scratch_shapes=[
            pltpu.VMEM((width, width), BF16),
            pltpu.VMEM((width, width), BF16),
            pltpu.VMEM((virtual, width), BF16),
            pltpu.VMEM(local_rows.shape, jnp.int32),
            pltpu.VMEM(slot_rows.shape, jnp.int32),
            pltpu.SMEM((blocks, slots), jnp.int32),
            pltpu.SMEM((blocks,), jnp.int32),
            pltpu.SMEM((devices,), jnp.int32),
            pltpu.SemaphoreType.DMA((10,)),
        ],
        compiler_params=params(32),
        cost_estimate=cost(unit),
        name="prepare",
    )(
        load,
        *[
            pltpu.with_memory_space_constraint(value, pltpu.HBM)
            for value in (
                norm_gain, project_in[0], virtual_keys[0], local_rows, slot_rows, slot_block,
                slot_count, project_out[0],
            )
        ],
    )

    def work(count):
        return [
            pltpu.VMEM((count * rows, width), BF16),
            pltpu.VMEM((count * br, width), BF16),
            pltpu.VMEM((width, count * br), BF16),
        ]

    if chips > 2:
        back, den = after((load, den))
        near[chips - 1] = to_next_chip(back, devices, -1)
    sums = (num, den, pool, weight)

    def arrive(step, sums):
        near[step], first = after((near[step], sums[1]))
        return (sums[0], first) + sums[2:]

    def slots_call(names, sums, name):
        loads = [(far if other else near)[step] for other, step in names]
        loads = [load if isinstance(load, list) else [load] for load in loads]
        sizes = tuple(len(load) for load in loads)
        return pl.pallas_call(
            functools.partial(slots_kernel, tuple(names), sizes),
            out_shape=accumulators,
            in_specs=[VMEM] * (11 + sum(sizes)),
            out_specs=[VMEM] * 4,
            scratch_shapes=work(len(names)),
            compiler_params=params(40),
            cost_estimate=cost(unit),
            name=name,
        )(
            mask, gain, wk, wvt, vkw, counts, qbd, *sums,
            *[piece for load in loads for piece in load],
        )

    ahead = chips // 2
    order = []
    for s in range(1, ahead + 1):
        order.append((s, 1))
        if s < chips - s:
            order.append((chips - s, -1))
    sums = slots_call([(1, 0)], sums, "slots_own")

    def hop_on(step, way):
        nexts = step + way
        if nexts not in near and (nexts, way) in order:
            near[nexts] = to_next_chip(near[step], devices, way)

    firsts = order[:-1][:2]
    for step, way in firsts:
        sums = arrive(step, sums)
        hop_on(step, way)
    for step, _ in firsts:
        far[step] = swapped_parts(near[step], devices, PARTS)
    if firsts:
        sums = slots_call([(0, step) for step, _ in firsts], sums, "slots_near")
        sums = slots_call([(1, step) for step, _ in firsts], sums, "slots_far")
    for i, (step, way) in enumerate(order[len(firsts) :]):
        sums = arrive(step, sums)
        hop_on(step, way)
        far[step] = swapped(near[step], devices, 1)
        names = [(0, step), (1, step)]
        if step == order[-1][0]:
            names = names[:1]
        sums = slots_call(names, sums, "slots_%d" % i)
    names = ((1, order[-1][0]),)
    updated = pl.pallas_call(
        functools.partial(finish_kernel, names),
        out_shape=shape((rows, width), BF16),
        in_specs=[VMEM] * 15,
        out_specs=VMEM,
        scratch_shapes=[pltpu.VMEM(leaf.shape, leaf.dtype) for leaf in accumulators] + work(1),
        compiler_params=params(40),
        cost_estimate=cost(unit),
        name="finish",
    )(
        mask, gain, wk, wvt, vkw, counts, qbd, *sums, far[names[0][1]], vcol, load, wo
    )
    return to_next_segment(updated[None])


def solution(mesh):
    placed = (
        P("segment", "node", None),
        P("segment", None),
        P("segment", None, None),
        P("segment", None, None),
        P("segment", None, None),
        P("node", None),
        P(None, "node"),
        P("node", None),
        P("node"),
        P("node", None, None, None),
    )
    return jax.shard_map(
        body, mesh=mesh, in_specs=placed, out_specs=P("segment", "node", None), check_vma=False
    )
```

```python
import functools

import jax
import jax.numpy as jnp
from jax import lax
from jax.experimental import pallas as pl
from jax.experimental.pallas import tpu as pltpu
from jax.sharding import PartitionSpec as P

HEADS = 8
CORES = 2
EPSILON = 1e-05
CAP_LIMIT = 10.0
LOG2E = 1.4426950408889634
EXTRA = 16
PARTS = 2
F32 = jnp.float32
BF16 = jnp.bfloat16
HBM = pl.BlockSpec(memory_space=pltpu.HBM)
VMEM = pl.BlockSpec(memory_space=pltpu.VMEM)


def ring_order(chips):
    return list(range(0, 1)) + list(range(1, chips, 2)) + list(range((chips - 1) // 2 * 2, 0, -2))


def ring_place(chip, chips):
    return jnp.where(chip % 2 == 1, (chip + 1) // 2, (chips - chip // 2) % chips)


def to_next_chip(value, devices, way):
    chips = devices // CORES
    order = ring_order(chips)
    pairs = [
        (order[i] * CORES + c, order[(i + way) % chips] * CORES + c)
        for i in range(chips)
        for c in range(CORES)
    ]
    return lax.ppermute(value, "node", pairs)


def swapped(value, devices, distance):
    return lax.ppermute(value, "node", [(d, d ^ distance) for d in range(devices)])


def swapped_parts(value, devices, parts):
    tiles = value.shape[0] // 16
    cuts = [0] + [16 * (-(-tiles * (i + 1) // parts)) for i in range(parts)]
    return [swapped(value[a:b], devices, 1) for a, b in zip(cuts, cuts[1:])]


def to_next_segment(value):
    count = lax.axis_size("segment")
    return lax.ppermute(value, "segment", [(s, (s + 1) % count) for s in range(count)])


def norm_rows(rows_in, gain_row):
    widened = rows_in.astype(F32)
    center = widened - jnp.mean(widened, axis=-1, keepdims=True)
    spread = jnp.mean(center * center, axis=-1, keepdims=True)
    return (center * lax.rsqrt(spread + EPSILON) * gain_row).astype(BF16)


def exp_capped(raw, scale):
    return jnp.exp2((CAP_LIMIT * LOG2E) * jnp.tanh(raw * (scale / CAP_LIMIT)))


def counts_of(index_rows, block_rows):
    rows = lax.broadcasted_iota(jnp.int32, (block_rows, index_rows.shape[1]), 0)
    total = jnp.zeros(rows.shape, F32)
    for j in range(index_rows.shape[0]):
        total = total + jnp.where(index_rows[j : j + 1, :] == rows, 1.0, 0.0)
    return total


def mm(a, b):
    return jnp.dot(a, b, preferred_element_type=F32)


def mm_nt(a, b):
    return lax.dot_general(a, b, (((1,), (1,)), ((), ())), preferred_element_type=F32)


def choose(mask_row, rows):
    lanes = mask_row.shape[1]
    count, width = rows.shape
    br = count // 2
    mask = jnp.broadcast_to(mask_row, (br, lanes))
    mask = jnp.concatenate([mask] * (width // lanes), axis=1)
    first, second = rows[:br, :].astype(F32), rows[br:, :].astype(F32)
    return jnp.where(mask > 0.5, second, first).astype(rows.dtype)


def halves(value):
    high = value.astype(BF16)
    low = (value - high.astype(F32)).astype(BF16)
    return jnp.concatenate([high, low], axis=0)


def of_own_head(shape):
    head = lax.broadcasted_iota(jnp.int32, shape, 0) % HEADS
    return head == lax.broadcasted_iota(jnp.int32, shape, 1) // (shape[1] // HEADS)


def add_pool(normed, vid_row, vkw_ref, pool_ref, weight_ref, scale, first):
    count = pool_ref.shape[0]
    raw = mm_nt(vkw_ref[...], normed)
    raw = raw[:count] + raw[count:]
    owner = lax.broadcasted_iota(jnp.int32, raw.shape, 0) // HEADS
    w = jnp.where(vid_row == owner.astype(F32), exp_capped(raw, scale), 0.0).astype(BF16)
    sums = mm(w, normed)
    totals = jnp.broadcast_to(
        jnp.sum(w.astype(F32), axis=1, keepdims=True), weight_ref.shape
    )
    pool_ref[...] = sums if first else pool_ref[...] + sums
    weight_ref[...] = totals if first else weight_ref[...] + totals


def start_copies(pairs, sems):
    copies = [pltpu.make_async_copy(src, dst, sems.at[i]) for i, (src, dst) in enumerate(pairs)]
    for copy in copies:
        copy.start()
    return copies


def pack_kernel(x_hbm, vid_hbm, load_ref, vid_ref, sems):
    rows = vid_ref.shape[1]
    copies = start_copies([(x_hbm, load_ref.at[:rows, :]), (vid_hbm, vid_ref)], sems)
    copies[1].wait()
    tile = jnp.broadcast_to(vid_ref[...].astype(F32), (EXTRA, rows))
    rest = jnp.zeros((EXTRA, load_ref.shape[1] - rows), F32)
    load_ref[rows:, :] = jnp.concatenate([tile, rest], axis=1).astype(BF16)
    copies[0].wait()


def vid_row(load_ref, rows):
    last = load_ref.shape[0]
    return load_ref[last - EXTRA :, :rows].astype(F32)[:1, :]


def load_rows(refs):
    last = refs[-1].shape[0] - EXTRA
    return jnp.concatenate([ref[...] for ref in refs[:-1]] + [refs[-1][:last, :]], axis=0)


def grouped(refs, sizes):
    groups = []
    for size in sizes:
        groups.append(refs[:size])
        refs = refs[size:]
    return groups


def attend(keys, values, counts, qbd, scale):
    p = (counts * exp_capped(mm(keys, qbd), scale)).astype(BF16)
    return mm(values, p)


def fold(o, num_ref, den_ref, b, t, add):
    wide = o.shape[0] - EXTRA
    head = wide // 2
    br = o.shape[1] // 2
    r0 = t * wide
    places = (
        (num_ref, slice(r0, r0 + head), o[:head, :br]),
        (num_ref, slice(r0 + head, r0 + wide), o[head:wide, br:]),
        (den_ref, slice(2 * t, 2 * t + 1), o[wide : wide + 1, :br]),
        (den_ref, slice(2 * t + 1, 2 * t + 2), o[wide : wide + 1, br:]),
    )
    for ref, part, value in places:
        if add:
            ref[b, part, :] += value
        else:
            ref[b, part, :] = value


def prep_kernel(
    load_ref, gain_hbm, win_hbm, vk_hbm, lrows_hbm, srows_hbm, sblock_hbm, scount_hbm, wo_hbm,
    qbd_ref, num_ref, den_ref, counts_ref, mask_ref, vcol_ref, wk_ref, wvt_ref, wo_ref, gain_ref,
    vkw_ref, pool_ref, weight_ref,
    wq_ref, wv_ref, vk_ref, lrows_ref, srows_ref, sblock_ref, scount_ref, want_ref, sems,
):
    width = load_ref.shape[1]
    rows = load_ref.shape[0] - EXTRA
    blocks, pairs, wide, _ = qbd_ref.shape
    chips = mask_ref.shape[1]
    slots = sblock_ref.shape[1]
    virtual = vk_ref.shape[0]
    br = rows // blocks
    head = width // HEADS
    scale = head ** (-0.5)
    copies = start_copies(
        [
            (gain_hbm, gain_ref), (sblock_hbm, sblock_ref), (scount_hbm, scount_ref),
            (srows_hbm, srows_ref), (lrows_hbm, lrows_ref), (vk_hbm, vk_ref),
            (win_hbm.at[:, width : 2 * width], wk_ref), (win_hbm.at[:, :width], wq_ref),
            (win_hbm.at[:, 2 * width :], wv_ref), (wo_hbm, wo_ref),
        ],
        sems,
    )
    counts_ref[...] = jnp.zeros(counts_ref.shape, F32)
    for copy in copies:
        copy.wait()
    normed = norm_rows(load_ref[:rows, :], gain_ref[...])
    k = mm(normed, wk_ref[...]).astype(BF16)
    v = mm(normed, wv_ref[...]).astype(BF16)
    qt = mm(normed, wq_ref[...]).astype(BF16).T
    vt = v.T
    wvt_ref[...] = wv_ref[...].T

    vkf = vk_ref[...].astype(F32)
    vkbd = jnp.concatenate(
        [jnp.broadcast_to(vkf[j : j + 1, :], (HEADS, width)) for j in range(virtual)], axis=0
    )
    vkbd = jnp.where(of_own_head(vkbd.shape), vkbd, 0.0).astype(BF16)
    vkw_ref[...] = halves(mm_nt(vkbd, wk_ref[...]))
    vid = vid_row(load_ref, rows)
    add_pool(normed, vid, vkw_ref, pool_ref, weight_ref, scale, True)
    vcol_ref[...] = jnp.broadcast_to(vid, (128, rows)).T

    me = lax.axis_index("node")
    place = ring_place(me // CORES, chips)
    core = me % CORES
    for d in range(chips * CORES):
        want_ref[d] = 0
    for b in range(blocks):
        for e in range(slots):
            entry = sblock_ref[b, e]
            want_ref[entry // blocks] = entry % blocks
    for d in range(chips * CORES):
        step = (place - ring_place(jnp.int32(d // CORES), chips) + chips) % chips
        far = jnp.where(core == d % CORES, 0, 1)
        mask_ref[far, step] = jnp.full(mask_ref.shape[2:], want_ref[d].astype(F32), F32)
    for b in range(blocks):
        for e in range(slots):
            device = sblock_ref[b, e] // blocks
            step = (place - ring_place(device // CORES, chips) + chips) % chips
            far = jnp.where(device % CORES == core, 0, 1)
            live = jnp.where(e < scount_ref[b], 1.0, 0.0).astype(F32)
            counts_ref[far, step, b] += counts_of(srows_ref[b, e], br) * live

    zero = jnp.zeros((head, br), BF16)
    ones = jnp.ones((EXTRA, br), BF16)
    for b in range(blocks):
        cols = slice(b * br, (b + 1) * br)
        counts = counts_of(lrows_ref[:, cols], br)
        counts2 = jnp.concatenate([counts, counts], axis=1)
        for t in range(pairs):
            r0 = t * wide
            mid = r0 + head
            end = r0 + wide
            bd = jnp.concatenate(
                [
                    jnp.concatenate([qt[r0:mid, cols], zero], axis=1),
                    jnp.concatenate([zero, qt[mid:end, cols]], axis=1),
                ],
                axis=0,
            )
            qbd_ref[b, t] = bd
            values = jnp.concatenate([vt[r0:end, cols], ones], axis=0)
            fold(attend(k[cols, r0:end], values, counts2, bd, scale), num_ref, den_ref, b, t, False)


def take_sources(
    names, loads, mask_ref, gain_ref, wk_ref, wvt_ref, vkw_ref,
    normed_ref, k_ref, vt_ref, pool_ref, weight_ref,
):
    width = k_ref.shape[1]
    chosen = []
    vids = []
    for i, ((far, step), pieces) in enumerate(zip(names, loads)):
        part = norm_rows(load_rows(pieces), gain_ref[...])
        rows = part.shape[0]
        normed_ref[i * rows : (i + 1) * rows, :] = part
        chosen.append(choose(mask_ref[far, step, :1, :], part))
        vids.append(vid_row(pieces[-1], rows))
    picked = jnp.concatenate(chosen, axis=0)
    k_ref[...] = mm(picked, wk_ref[...]).astype(BF16)
    vt_ref[...] = mm_nt(wvt_ref[...], picked).astype(BF16)
    scale = (width // HEADS) ** (-0.5)
    vid = jnp.concatenate(vids, axis=1)
    add_pool(normed_ref[...], vid, vkw_ref, pool_ref, weight_ref, scale, False)


def add_sources(names, b, counts_ref, qbd_ref, k_ref, vt_ref, num_ref, den_ref):
    _, pairs, wide, _ = qbd_ref.shape
    scale = (2 / wide) ** 0.5
    counts = jnp.concatenate([counts_ref[far, step, b] for far, step in names], axis=0)
    counts2 = jnp.concatenate([counts, counts], axis=1)
    ones = jnp.ones((EXTRA, counts.shape[0]), BF16)
    for t in range(pairs):
        cols = slice(t * wide, (t + 1) * wide)
        values = jnp.concatenate([vt_ref[cols, :], ones], axis=0)
        o = attend(k_ref[:, cols], values, counts2, qbd_ref[b, t], scale)
        fold(o, num_ref, den_ref, b, t, True)


def slots_kernel(
    names, sizes, mask_ref, gain_ref, wk_ref, wvt_ref, vkw_ref, counts_ref, qbd_ref,
    num_in, den_in, pool_in, weight_in, *refs
):
    loads = grouped(refs, sizes)
    num_ref, den_ref, pool_ref, weight_ref, normed_ref, k_ref, vt_ref = refs[sum(sizes) :]
    num_ref[...] = num_in[...]
    den_ref[...] = den_in[...]
    pool_ref[...] = pool_in[...]
    weight_ref[...] = weight_in[...]
    take_sources(
        names, loads, mask_ref, gain_ref, wk_ref, wvt_ref, vkw_ref,
        normed_ref, k_ref, vt_ref, pool_ref, weight_ref,
    )
    for b in range(num_ref.shape[0]):
        add_sources(names, b, counts_ref, qbd_ref, k_ref, vt_ref, num_ref, den_ref)


def finish_kernel(
    names, mask_ref, gain_ref, wk_ref, wvt_ref, vkw_ref, counts_ref, qbd_ref,
    num_in, den_in, pool_in, weight_in, last_ref, vcol_ref, load_ref, wo_ref,
    out_ref, num_ref, den_ref, pool_ref, weight_ref, normed_ref, k_ref, vt_ref,
):
    slots_kernel(
        names, (1,), mask_ref, gain_ref, wk_ref, wvt_ref, vkw_ref, counts_ref, qbd_ref,
        num_in, den_in, pool_in, weight_in, last_ref,
        num_ref, den_ref, pool_ref, weight_ref, normed_ref, k_ref, vt_ref,
    )
    blocks, width, br = num_ref.shape
    head = width // HEADS
    lanes = vcol_ref.shape[1]
    count = pool_ref.shape[0]
    weight = jnp.concatenate([weight_ref[...]] * (width // lanes), axis=1)
    both = mm_nt(halves(pool_ref[...] / weight), wvt_ref[...])
    both = jnp.where(of_own_head((count, width)), both[:count] + both[count:], 0.0)
    pooled = [
        jnp.sum(both[j : j + HEADS], axis=0, keepdims=True) for j in range(0, count, HEADS)
    ]
    for b in range(blocks):
        part = slice(b * br, (b + 1) * br)
        vid = vcol_ref[part, :]
        att = jnp.concatenate(
            [
                num_ref[b, h * head : (h + 1) * head, :] / den_ref[b, h : h + 1, :]
                for h in range(HEADS)
            ],
            axis=0,
        ).T
        pieces = []
        for c in range(0, width, lanes):
            own = jnp.broadcast_to(pooled[0][:, c : c + lanes], (br, lanes))
            for j in range(1, len(pooled)):
                own = jnp.where(vid == float(j), pooled[j][:, c : c + lanes], own)
            pieces.append((att[:, c : c + lanes] + own).astype(BF16))
        mixed = jnp.concatenate(pieces, axis=1)
        out_ref[part, :] = (load_ref[part, :].astype(F32) + mm(mixed, wo_ref[...])).astype(BF16)


def params(mib):
    return pltpu.CompilerParams(vmem_limit_bytes=mib * 2**20)


def cost(flops):
    return pl.CostEstimate(flops=flops, bytes_accessed=1024, transcendentals=0)


def body(
    activations,
    norm_gain,
    project_in,
    project_out,
    virtual_keys,
    virtual_id,
    local_rows,
    slot_block,
    slot_count,
    slot_rows,
):
    _, rows, width = activations.shape
    br = slot_rows.shape[3]
    slots = slot_block.shape[1]
    blocks = rows // br
    devices = lax.axis_size("node")
    chips = devices // CORES
    virtual = virtual_keys.shape[1]
    pairs = HEADS // 2
    wide = width // pairs
    shape = jax.ShapeDtypeStruct
    after = lax.optimization_barrier
    unit = 2**16

    load = pl.pallas_call(
        pack_kernel,
        out_shape=shape((rows + EXTRA, width), BF16),
        in_specs=[HBM] * 2,
        out_specs=VMEM,
        scratch_shapes=[pltpu.VMEM((1, rows), jnp.int32), pltpu.SemaphoreType.DMA((2,))],
        compiler_params=params(24),
        cost_estimate=cost(unit),
        name="pack_rows",
    )(
        pltpu.with_memory_space_constraint(activations[0], pltpu.HBM),
        pltpu.with_memory_space_constraint(virtual_id.reshape(1, rows), pltpu.HBM),
    )
    near = {1: [to_next_chip(load, devices, 1)]}
    far = {0: [swapped(load, devices, 1)]}

    accumulators = (
        shape((blocks, width, br), F32),
        shape((blocks, HEADS, br), F32),
        shape((virtual * HEADS, width), F32),
        shape((virtual * HEADS, 128), F32),
    )
    square = shape((width, width), BF16)
    qbd, num, den, counts, mask, vcol, wk, wvt, wo, gain, vkw, pool, weight = pl.pallas_call(
        prep_kernel,
        out_shape=(
            (shape((blocks, pairs, wide, 2 * br), BF16),)
            + accumulators[:2]
            + (
                shape((CORES, chips, blocks, br, br), F32),
                shape((CORES, chips, 8, 128), F32),
                shape((rows, 128), F32),
                square,
                square,
                square,
                shape((1, width), F32),
                shape((2 * virtual * HEADS, width), BF16),
            )
            + accumulators[2:]
        ),
        in_specs=[VMEM] + [HBM] * 8,
        out_specs=[VMEM] * 13,
        scratch_shapes=[
            pltpu.VMEM((width, width), BF16),
            pltpu.VMEM((width, width), BF16),
            pltpu.VMEM((virtual, width), BF16),
            pltpu.VMEM(local_rows.shape, jnp.int32),
            pltpu.VMEM(slot_rows.shape, jnp.int32),
            pltpu.SMEM((blocks, slots), jnp.int32),
            pltpu.SMEM((blocks,), jnp.int32),
            pltpu.SMEM((devices,), jnp.int32),
            pltpu.SemaphoreType.DMA((10,)),
        ],
        compiler_params=params(32),
        cost_estimate=cost(unit),
        name="prepare",
    )(
        load,
        *[
            pltpu.with_memory_space_constraint(value, pltpu.HBM)
            for value in (
                norm_gain, project_in[0], virtual_keys[0], local_rows, slot_rows, slot_block,
                slot_count, project_out[0],
            )
        ],
    )

    def work(count):
        return [
            pltpu.VMEM((count * rows, width), BF16),
            pltpu.VMEM((count * br, width), BF16),
            pltpu.VMEM((width, count * br), BF16),
        ]

    sums = (num, den, pool, weight)

    def tie(values, sums):
        *values, first = after((*values, sums[1]))
        return values, (sums[0], first) + sums[2:]

    cut = 16 * ((rows + EXTRA) // 32)
    if chips > 2:
        (early,), sums = tie([load[:cut]], sums)
        early = to_next_chip(early, devices, -1)

    def slots_call(names, sums, name):
        loads = [(far if other else near)[step] for other, step in names]
        sizes = tuple(len(load) for load in loads)
        return pl.pallas_call(
            functools.partial(slots_kernel, tuple(names), sizes),
            out_shape=accumulators,
            in_specs=[VMEM] * (11 + sum(sizes)),
            out_specs=[VMEM] * 4,
            scratch_shapes=work(len(names)),
            compiler_params=params(40),
            cost_estimate=cost(unit),
            name=name,
        )(
            mask, gain, wk, wvt, vkw, counts, qbd, *sums,
            *[piece for load in loads for piece in load],
        )

    ahead = chips // 2
    order = []
    for s in range(1, ahead + 1):
        order.append((s, 1))
        if s < chips - s:
            order.append((chips - s, -1))
    sums = slots_call([(1, 0)], sums, "slots_own")

    for i, (step, way) in enumerate(order):
        last = i == len(order) - 1
        tied = list(near[step])
        if i == 0 and chips > 2:
            (late, early, *tied), sums = tie([load[cut:], early] + tied, sums)
            near[chips - 1] = [early, to_next_chip(late, devices, -1)]
        else:
            tied, sums = tie(tied, sums)
        near[step] = tied
        if step + way not in near and (step + way, way) in order:
            near[step + way] = [to_next_chip(piece, devices, way) for piece in tied]
        if last:
            far[step] = [swapped(piece, devices, 1) for piece in tied]
        elif len(tied) == 1:
            far[step] = swapped_parts(tied[0], devices, PARTS)
        else:
            far[step] = [swapped(piece, devices, 1) for piece in tied]
        names = [(0, step)] if last else [(0, step), (1, step)]
        sums = slots_call(names, sums, "slots_%d" % i)
    names = ((1, order[-1][0]),)
    updated = pl.pallas_call(
        functools.partial(finish_kernel, names),
        out_shape=shape((rows, width), BF16),
        in_specs=[VMEM] * 15,
        out_specs=VMEM,
        scratch_shapes=[pltpu.VMEM(leaf.shape, leaf.dtype) for leaf in accumulators] + work(1),
        compiler_params=params(40),
        cost_estimate=cost(unit),
        name="finish",
    )(
        mask, gain, wk, wvt, vkw, counts, qbd, *sums, *far[names[0][1]], vcol, load, wo
    )
    return to_next_segment(updated[None])


def solution(mesh):
    placed = (
        P("segment", "node", None),
        P("segment", None),
        P("segment", None, None),
        P("segment", None, None),
        P("segment", None, None),
        P("node", None),
        P(None, "node"),
        P("node", None),
        P("node"),
        P("node", None, None, None),
    )
    return jax.shard_map(
        body, mesh=mesh, in_specs=placed, out_specs=P("segment", "node", None), check_vma=False
    )
```

```python
import functools

import jax
import jax.numpy as jnp
from jax import lax
from jax.experimental import pallas as pl
from jax.experimental.pallas import tpu as pltpu
from jax.sharding import PartitionSpec as P

HEADS = 8
CORES = 2
EPSILON = 1e-05
CAP_LIMIT = 10.0
LOG2E = 1.4426950408889634
EXTRA = 16
PARTS = 3
F32 = jnp.float32
BF16 = jnp.bfloat16
HBM = pl.BlockSpec(memory_space=pltpu.HBM)
VMEM = pl.BlockSpec(memory_space=pltpu.VMEM)


def ring_order(chips):
    return list(range(0, 1)) + list(range(1, chips, 2)) + list(range((chips - 1) // 2 * 2, 0, -2))


def ring_place(chip, chips):
    return jnp.where(chip % 2 == 1, (chip + 1) // 2, (chips - chip // 2) % chips)


def to_next_chip(value, devices, way):
    chips = devices // CORES
    order = ring_order(chips)
    pairs = [
        (order[i] * CORES + c, order[(i + way) % chips] * CORES + c)
        for i in range(chips)
        for c in range(CORES)
    ]
    return lax.ppermute(value, "node", pairs)


def swapped(value, devices, distance):
    return lax.ppermute(value, "node", [(d, d ^ distance) for d in range(devices)])


def swapped_parts(value, devices, parts):
    tiles = value.shape[0] // 16
    cuts = [0] + [16 * (-(-tiles * (i + 1) // parts)) for i in range(parts)]
    return [swapped(value[a:b], devices, 1) for a, b in zip(cuts, cuts[1:])]


def to_next_segment(value):
    count = lax.axis_size("segment")
    return lax.ppermute(value, "segment", [(s, (s + 1) % count) for s in range(count)])


def norm_rows(rows_in, gain_row):
    widened = rows_in.astype(F32)
    center = widened - jnp.mean(widened, axis=-1, keepdims=True)
    spread = jnp.mean(center * center, axis=-1, keepdims=True)
    return (center * lax.rsqrt(spread + EPSILON) * gain_row).astype(BF16)


def exp_capped(raw, scale):
    return jnp.exp2((CAP_LIMIT * LOG2E) * jnp.tanh(raw * (scale / CAP_LIMIT)))


def counts_of(index_rows, block_rows):
    rows = lax.broadcasted_iota(jnp.int32, (block_rows, index_rows.shape[1]), 0)
    total = jnp.zeros(rows.shape, F32)
    for j in range(index_rows.shape[0]):
        total = total + jnp.where(index_rows[j : j + 1, :] == rows, 1.0, 0.0)
    return total


def mm(a, b):
    return jnp.dot(a, b, preferred_element_type=F32)


def mm_nt(a, b):
    return lax.dot_general(a, b, (((1,), (1,)), ((), ())), preferred_element_type=F32)


def choose(mask_row, rows):
    lanes = mask_row.shape[1]
    count, width = rows.shape
    br = count // 2
    mask = jnp.broadcast_to(mask_row, (br, lanes))
    mask = jnp.concatenate([mask] * (width // lanes), axis=1)
    first, second = rows[:br, :].astype(F32), rows[br:, :].astype(F32)
    return jnp.where(mask > 0.5, second, first).astype(rows.dtype)


def halves(value):
    high = value.astype(BF16)
    low = (value - high.astype(F32)).astype(BF16)
    return jnp.concatenate([high, low], axis=0)


def of_own_head(shape):
    head = lax.broadcasted_iota(jnp.int32, shape, 0) % HEADS
    return head == lax.broadcasted_iota(jnp.int32, shape, 1) // (shape[1] // HEADS)


def add_pool(normed, vid_row, vkw_ref, pool_ref, weight_ref, scale, first):
    count = pool_ref.shape[0]
    raw = mm_nt(vkw_ref[...], normed)
    raw = raw[:count] + raw[count:]
    owner = lax.broadcasted_iota(jnp.int32, raw.shape, 0) // HEADS
    w = jnp.where(vid_row == owner.astype(F32), exp_capped(raw, scale), 0.0).astype(BF16)
    sums = mm(w, normed)
    totals = jnp.broadcast_to(
        jnp.sum(w.astype(F32), axis=1, keepdims=True), weight_ref.shape
    )
    pool_ref[...] = sums if first else pool_ref[...] + sums
    weight_ref[...] = totals if first else weight_ref[...] + totals


def start_copies(pairs, sems):
    copies = [pltpu.make_async_copy(src, dst, sems.at[i]) for i, (src, dst) in enumerate(pairs)]
    for copy in copies:
        copy.start()
    return copies


def load_rows(refs):
    return jnp.concatenate([ref[...] for ref in refs], axis=0)


def vid_row(table_ref, far, step, chips):
    me = lax.axis_index("node")
    at = (ring_place(me // CORES, chips) - step + chips) % chips
    chip = jnp.where(at <= chips // 2, jnp.maximum(2 * at - 1, 0), 2 * (chips - at))
    row = chip * CORES + ((me % CORES) ^ far)
    return table_ref[pl.ds(row, 1), :].astype(F32)


def grouped(refs, sizes):
    groups = []
    for size in sizes:
        groups.append(refs[:size])
        refs = refs[size:]
    return groups


def attend(keys, values, counts, qbd, scale):
    p = (counts * exp_capped(mm(keys, qbd), scale)).astype(BF16)
    return mm(values, p)


def fold(o, num_ref, den_ref, b, t, add):
    wide = o.shape[0] - EXTRA
    head = wide // 2
    br = o.shape[1] // 2
    r0 = t * wide
    places = (
        (num_ref, slice(r0, r0 + head), o[:head, :br]),
        (num_ref, slice(r0 + head, r0 + wide), o[head:wide, br:]),
        (den_ref, slice(2 * t, 2 * t + 1), o[wide : wide + 1, :br]),
        (den_ref, slice(2 * t + 1, 2 * t + 2), o[wide : wide + 1, br:]),
    )
    for ref, part, value in places:
        if add:
            ref[b, part, :] += value
        else:
            ref[b, part, :] = value


def prep_kernel(
    x_hbm, vid_hbm, gain_hbm, win_hbm, vk_hbm, lrows_hbm, srows_hbm, sblock_hbm, scount_hbm,
    wo_hbm,
    qbd_ref, num_ref, den_ref, counts_ref, mask_ref, vcol_ref, wk_ref, wvt_ref, wo_ref, gain_ref,
    vkw_ref, pool_ref, weight_ref,
    x_ref, vid_ref, wq_ref, wv_ref, vk_ref, lrows_ref, srows_ref, sblock_ref, scount_ref,
    want_ref, sems,
):
    rows, width = x_ref.shape
    blocks, pairs, wide, _ = qbd_ref.shape
    chips = mask_ref.shape[1]
    slots = sblock_ref.shape[1]
    virtual = vk_ref.shape[0]
    br = rows // blocks
    head = width // HEADS
    scale = head ** (-0.5)
    copies = start_copies(
        [
            (x_hbm, x_ref), (vid_hbm, vid_ref),
            (gain_hbm, gain_ref), (sblock_hbm, sblock_ref), (scount_hbm, scount_ref),
            (srows_hbm, srows_ref), (lrows_hbm, lrows_ref), (vk_hbm, vk_ref),
            (win_hbm.at[:, width : 2 * width], wk_ref), (win_hbm.at[:, :width], wq_ref),
            (win_hbm.at[:, 2 * width :], wv_ref), (wo_hbm, wo_ref),
        ],
        sems,
    )
    counts_ref[...] = jnp.zeros(counts_ref.shape, F32)
    for copy in copies:
        copy.wait()
    normed = norm_rows(x_ref[...], gain_ref[...])
    k = mm(normed, wk_ref[...]).astype(BF16)
    v = mm(normed, wv_ref[...]).astype(BF16)
    qt = mm(normed, wq_ref[...]).astype(BF16).T
    vt = v.T
    wvt_ref[...] = wv_ref[...].T

    vkf = vk_ref[...].astype(F32)
    vkbd = jnp.concatenate(
        [jnp.broadcast_to(vkf[j : j + 1, :], (HEADS, width)) for j in range(virtual)], axis=0
    )
    vkbd = jnp.where(of_own_head(vkbd.shape), vkbd, 0.0).astype(BF16)
    vkw_ref[...] = halves(mm_nt(vkbd, wk_ref[...]))
    vid = vid_ref[...].astype(F32)
    add_pool(normed, vid, vkw_ref, pool_ref, weight_ref, scale, True)
    vcol_ref[...] = jnp.broadcast_to(vid, (128, rows)).T

    me = lax.axis_index("node")
    place = ring_place(me // CORES, chips)
    core = me % CORES
    for d in range(chips * CORES):
        want_ref[d] = 0
    for b in range(blocks):
        for e in range(slots):
            entry = sblock_ref[b, e]
            want_ref[entry // blocks] = entry % blocks
    for d in range(chips * CORES):
        step = (place - ring_place(jnp.int32(d // CORES), chips) + chips) % chips
        far = jnp.where(core == d % CORES, 0, 1)
        mask_ref[far, step] = jnp.full(mask_ref.shape[2:], want_ref[d].astype(F32), F32)
    for b in range(blocks):
        for e in range(slots):
            device = sblock_ref[b, e] // blocks
            step = (place - ring_place(device // CORES, chips) + chips) % chips
            far = jnp.where(device % CORES == core, 0, 1)
            live = jnp.where(e < scount_ref[b], 1.0, 0.0).astype(F32)
            counts_ref[far, step, b] += counts_of(srows_ref[b, e], br) * live

    zero = jnp.zeros((head, br), BF16)
    ones = jnp.ones((EXTRA, br), BF16)
    for b in range(blocks):
        cols = slice(b * br, (b + 1) * br)
        counts = counts_of(lrows_ref[:, cols], br)
        counts2 = jnp.concatenate([counts, counts], axis=1)
        for t in range(pairs):
            r0 = t * wide
            mid = r0 + head
            end = r0 + wide
            bd = jnp.concatenate(
                [
                    jnp.concatenate([qt[r0:mid, cols], zero], axis=1),
                    jnp.concatenate([zero, qt[mid:end, cols]], axis=1),
                ],
                axis=0,
            )
            qbd_ref[b, t] = bd
            values = jnp.concatenate([vt[r0:end, cols], ones], axis=0)
            fold(attend(k[cols, r0:end], values, counts2, bd, scale), num_ref, den_ref, b, t, False)


def take_sources(
    names, loads, table_ref, mask_ref, gain_ref, wk_ref, wvt_ref, vkw_ref,
    normed_ref, k_ref, vt_ref, pool_ref, weight_ref,
):
    width = k_ref.shape[1]
    chosen = []
    vids = []
    for i, ((far, step), pieces) in enumerate(zip(names, loads)):
        part = norm_rows(load_rows(pieces), gain_ref[...])
        rows = part.shape[0]
        normed_ref[i * rows : (i + 1) * rows, :] = part
        chosen.append(choose(mask_ref[far, step, :1, :], part))
        vids.append(vid_row(table_ref, far, step, mask_ref.shape[1]))
    picked = jnp.concatenate(chosen, axis=0)
    k_ref[...] = mm(picked, wk_ref[...]).astype(BF16)
    vt_ref[...] = mm_nt(wvt_ref[...], picked).astype(BF16)
    scale = (width // HEADS) ** (-0.5)
    vid = jnp.concatenate(vids, axis=1)
    add_pool(normed_ref[...], vid, vkw_ref, pool_ref, weight_ref, scale, False)


def add_sources(names, b, counts_ref, qbd_ref, k_ref, vt_ref, num_ref, den_ref):
    _, pairs, wide, _ = qbd_ref.shape
    scale = (2 / wide) ** 0.5
    counts = jnp.concatenate([counts_ref[far, step, b] for far, step in names], axis=0)
    counts2 = jnp.concatenate([counts, counts], axis=1)
    ones = jnp.ones((EXTRA, counts.shape[0]), BF16)
    for t in range(pairs):
        cols = slice(t * wide, (t + 1) * wide)
        values = jnp.concatenate([vt_ref[cols, :], ones], axis=0)
        o = attend(k_ref[:, cols], values, counts2, qbd_ref[b, t], scale)
        fold(o, num_ref, den_ref, b, t, True)


def slots_kernel(
    names, sizes, table_ref, mask_ref, gain_ref, wk_ref, wvt_ref, vkw_ref, counts_ref, qbd_ref,
    num_in, den_in, pool_in, weight_in, *refs
):
    loads = grouped(refs, sizes)
    num_ref, den_ref, pool_ref, weight_ref, normed_ref, k_ref, vt_ref = refs[sum(sizes) :]
    num_ref[...] = num_in[...]
    den_ref[...] = den_in[...]
    pool_ref[...] = pool_in[...]
    weight_ref[...] = weight_in[...]
    take_sources(
        names, loads, table_ref, mask_ref, gain_ref, wk_ref, wvt_ref, vkw_ref,
        normed_ref, k_ref, vt_ref, pool_ref, weight_ref,
    )
    for b in range(num_ref.shape[0]):
        add_sources(names, b, counts_ref, qbd_ref, k_ref, vt_ref, num_ref, den_ref)


def finish_kernel(
    names, table_ref, mask_ref, gain_ref, wk_ref, wvt_ref, vkw_ref, counts_ref, qbd_ref,
    num_in, den_in, pool_in, weight_in, last_ref, vcol_ref, x_ref, wo_ref,
    out_ref, num_ref, den_ref, pool_ref, weight_ref, normed_ref, k_ref, vt_ref,
):
    slots_kernel(
        names, (1,), table_ref, mask_ref, gain_ref, wk_ref, wvt_ref, vkw_ref, counts_ref, qbd_ref,
        num_in, den_in, pool_in, weight_in, last_ref,
        num_ref, den_ref, pool_ref, weight_ref, normed_ref, k_ref, vt_ref,
    )
    blocks, width, br = num_ref.shape
    head = width // HEADS
    lanes = vcol_ref.shape[1]
    count = pool_ref.shape[0]
    weight = jnp.concatenate([weight_ref[...]] * (width // lanes), axis=1)
    both = mm_nt(halves(pool_ref[...] / weight), wvt_ref[...])
    both = jnp.where(of_own_head((count, width)), both[:count] + both[count:], 0.0)
    pooled = [
        jnp.sum(both[j : j + HEADS], axis=0, keepdims=True) for j in range(0, count, HEADS)
    ]
    for b in range(blocks):
        part = slice(b * br, (b + 1) * br)
        vid = vcol_ref[part, :]
        att = jnp.concatenate(
            [
                num_ref[b, h * head : (h + 1) * head, :] / den_ref[b, h : h + 1, :]
                for h in range(HEADS)
            ],
            axis=0,
        ).T
        pieces = []
        for c in range(0, width, lanes):
            own = jnp.broadcast_to(pooled[0][:, c : c + lanes], (br, lanes))
            for j in range(1, len(pooled)):
                own = jnp.where(vid == float(j), pooled[j][:, c : c + lanes], own)
            pieces.append((att[:, c : c + lanes] + own).astype(BF16))
        mixed = jnp.concatenate(pieces, axis=1)
        out_ref[part, :] = (x_ref[part, :].astype(F32) + mm(mixed, wo_ref[...])).astype(BF16)


def params(mib):
    return pltpu.CompilerParams(vmem_limit_bytes=mib * 2**20)


def cost(flops):
    return pl.CostEstimate(flops=flops, bytes_accessed=1024, transcendentals=0)


def body(
    activations,
    norm_gain,
    project_in,
    project_out,
    virtual_keys,
    virtual_id,
    local_rows,
    slot_block,
    slot_count,
    slot_rows,
):
    _, rows, width = activations.shape
    br = slot_rows.shape[3]
    slots = slot_block.shape[1]
    blocks = rows // br
    devices = lax.axis_size("node")
    chips = devices // CORES
    virtual = virtual_keys.shape[1]
    pairs = HEADS // 2
    wide = width // pairs
    shape = jax.ShapeDtypeStruct
    after = lax.optimization_barrier
    unit = 2**16

    load = activations[0]
    vid = virtual_id.reshape(1, rows)
    near = {1: to_next_chip(load, devices, 1)}
    far = {0: swapped(load, devices, 1)}

    accumulators = (
        shape((blocks, width, br), F32),
        shape((blocks, HEADS, br), F32),
        shape((virtual * HEADS, width), F32),
        shape((virtual * HEADS, 128), F32),
    )
    square = shape((width, width), BF16)
    qbd, num, den, counts, mask, vcol, wk, wvt, wo, gain, vkw, pool, weight = pl.pallas_call(
        prep_kernel,
        out_shape=(
            (shape((blocks, pairs, wide, 2 * br), BF16),)
            + accumulators[:2]
            + (
                shape((CORES, chips, blocks, br, br), F32),
                shape((CORES, chips, 8, 128), F32),
                shape((rows, 128), F32),
                square,
                square,
                square,
                shape((1, width), F32),
                shape((2 * virtual * HEADS, width), BF16),
            )
            + accumulators[2:]
        ),
        in_specs=[HBM] * 10,
        out_specs=[VMEM] * 13,
        scratch_shapes=[
            pltpu.VMEM((rows, width), BF16),
            pltpu.VMEM((1, rows), jnp.int32),
            pltpu.VMEM((width, width), BF16),
            pltpu.VMEM((width, width), BF16),
            pltpu.VMEM((virtual, width), BF16),
            pltpu.VMEM(local_rows.shape, jnp.int32),
            pltpu.VMEM(slot_rows.shape, jnp.int32),
            pltpu.SMEM((blocks, slots), jnp.int32),
            pltpu.SMEM((blocks,), jnp.int32),
            pltpu.SMEM((devices,), jnp.int32),
            pltpu.SemaphoreType.DMA((12,)),
        ],
        compiler_params=params(32),
        cost_estimate=cost(unit),
        name="prepare",
    )(
        *[
            pltpu.with_memory_space_constraint(value, pltpu.HBM)
            for value in (
                load, vid, norm_gain, project_in[0], virtual_keys[0], local_rows, slot_rows, slot_block,
                slot_count, project_out[0],
            )
        ],
    )

    def work(count):
        return [
            pltpu.VMEM((count * rows, width), BF16),
            pltpu.VMEM((count * br, width), BF16),
            pltpu.VMEM((width, count * br), BF16),
        ]

    tied, den = after((vid, den))
    table = lax.all_to_all(
        jnp.broadcast_to(tied, (devices, rows)), "node", split_axis=0, concat_axis=0, tiled=True
    )
    if chips > 2:
        back, den = after((load, den))
        near[chips - 1] = to_next_chip(back, devices, -1)
    sums = (num, den, pool, weight)

    def arrive(step, sums):
        near[step], first = after((near[step], sums[1]))
        return (sums[0], first) + sums[2:]

    def slots_call(names, sums, name):
        loads = [(far if other else near)[step] for other, step in names]
        loads = [load if isinstance(load, list) else [load] for load in loads]
        sizes = tuple(len(load) for load in loads)
        return pl.pallas_call(
            functools.partial(slots_kernel, tuple(names), sizes),
            out_shape=accumulators,
            in_specs=[VMEM] * (12 + sum(sizes)),
            out_specs=[VMEM] * 4,
            scratch_shapes=work(len(names)),
            compiler_params=params(40),
            cost_estimate=cost(unit),
            name=name,
        )(
            table, mask, gain, wk, wvt, vkw, counts, qbd, *sums,
            *[piece for load in loads for piece in load],
        )

    ahead = chips // 2
    order = []
    for s in range(1, ahead + 1):
        order.append((s, 1))
        if s < chips - s:
            order.append((chips - s, -1))
    sums = slots_call([(1, 0)], sums, "slots_own")

    def hop_on(step, way):
        nexts = step + way
        if nexts not in near and (nexts, way) in order:
            near[nexts] = to_next_chip(near[step], devices, way)

    firsts = order[:-1][:2]
    for step, way in firsts:
        sums = arrive(step, sums)
        hop_on(step, way)
    for step, _ in firsts:
        far[step] = swapped_parts(near[step], devices, PARTS)
    if firsts:
        sums = slots_call([(0, step) for step, _ in firsts], sums, "slots_near")
        sums = slots_call([(1, step) for step, _ in firsts], sums, "slots_far")
    for i, (step, way) in enumerate(order[len(firsts) :]):
        sums = arrive(step, sums)
        hop_on(step, way)
        far[step] = swapped(near[step], devices, 1)
        names = [(0, step), (1, step)]
        if step == order[-1][0]:
            names = names[:1]
        sums = slots_call(names, sums, "slots_%d" % i)
    names = ((1, order[-1][0]),)
    updated = pl.pallas_call(
        functools.partial(finish_kernel, names),
        out_shape=shape((rows, width), BF16),
        in_specs=[VMEM] * 16,
        out_specs=VMEM,
        scratch_shapes=[pltpu.VMEM(leaf.shape, leaf.dtype) for leaf in accumulators] + work(1),
        compiler_params=params(40),
        cost_estimate=cost(unit),
        name="finish",
    )(
        table, mask, gain, wk, wvt, vkw, counts, qbd, *sums, far[names[0][1]], vcol, load, wo
    )
    return to_next_segment(updated[None])


def solution(mesh):
    placed = (
        P("segment", "node", None),
        P("segment", None),
        P("segment", None, None),
        P("segment", None, None),
        P("segment", None, None),
        P("node", None),
        P(None, "node"),
        P("node", None),
        P("node"),
        P("node", None, None, None),
    )
    return jax.shard_map(
        body, mesh=mesh, in_specs=placed, out_specs=P("segment", "node", None), check_vma=False
    )
```

```python
import functools

import jax
import jax.numpy as jnp
from jax import lax
from jax.experimental import pallas as pl
from jax.experimental.pallas import tpu as pltpu
from jax.sharding import PartitionSpec as P

HEADS = 8
CORES = 2
EPSILON = 1e-05
CAP_LIMIT = 10.0
LOG2E = 1.4426950408889634
EXTRA = 16
TILE = 8
PARTS = 2
F32 = jnp.float32
BF16 = jnp.bfloat16
HBM = pl.BlockSpec(memory_space=pltpu.HBM)
VMEM = pl.BlockSpec(memory_space=pltpu.VMEM)


def ring_order(chips):
    return list(range(0, 1)) + list(range(1, chips, 2)) + list(range((chips - 1) // 2 * 2, 0, -2))


def ring_place(chip, chips):
    return jnp.where(chip % 2 == 1, (chip + 1) // 2, (chips - chip // 2) % chips)


def to_next_chip(value, devices, way):
    chips = devices // CORES
    order = ring_order(chips)
    pairs = [
        (order[i] * CORES + c, order[(i + way) % chips] * CORES + c)
        for i in range(chips)
        for c in range(CORES)
    ]
    return lax.ppermute(value, "node", pairs)


def swapped(value, devices, distance):
    return lax.ppermute(value, "node", [(d, d ^ distance) for d in range(devices)])


def swapped_parts(value, devices, parts):
    tiles = -(-value.shape[0] // 16)
    cuts = [0] + [16 * (-(-tiles * (i + 1) // parts)) for i in range(parts)]
    return [swapped(value[a:b], devices, 1) for a, b in zip(cuts, cuts[1:])]


def to_next_segment(value):
    count = lax.axis_size("segment")
    return lax.ppermute(value, "segment", [(s, (s + 1) % count) for s in range(count)])


def norm_rows(rows_in, gain_row):
    widened = rows_in.astype(F32)
    center = widened - jnp.mean(widened, axis=-1, keepdims=True)
    spread = jnp.mean(center * center, axis=-1, keepdims=True)
    return (center * lax.rsqrt(spread + EPSILON) * gain_row).astype(BF16)


def exp_capped(raw, scale):
    return jnp.exp2((CAP_LIMIT * LOG2E) * jnp.tanh(raw * (scale / CAP_LIMIT)))


def counts_of(index_rows, block_rows):
    rows = lax.broadcasted_iota(jnp.int32, (block_rows, index_rows.shape[1]), 0)
    total = jnp.zeros(rows.shape, F32)
    for j in range(index_rows.shape[0]):
        total = total + jnp.where(index_rows[j : j + 1, :] == rows, 1.0, 0.0)
    return total


def mm(a, b):
    return jnp.dot(a, b, preferred_element_type=F32)


def mm_nt(a, b):
    return lax.dot_general(a, b, (((1,), (1,)), ((), ())), preferred_element_type=F32)


def choose(mask_row, rows):
    lanes = mask_row.shape[1]
    count, width = rows.shape
    br = count // 2
    mask = jnp.broadcast_to(mask_row, (br, lanes))
    mask = jnp.concatenate([mask] * (width // lanes), axis=1)
    first, second = rows[:br, :].astype(F32), rows[br:, :].astype(F32)
    return jnp.where(mask > 0.5, second, first).astype(rows.dtype)


def halves(value):
    high = value.astype(BF16)
    low = (value - high.astype(F32)).astype(BF16)
    return jnp.concatenate([high, low], axis=0)


def of_own_head(shape):
    head = lax.broadcasted_iota(jnp.int32, shape, 0) % HEADS
    return head == lax.broadcasted_iota(jnp.int32, shape, 1) // (shape[1] // HEADS)


def add_pool(normed, vid_row, vkw_ref, pool_ref, weight_ref, scale, first):
    count = pool_ref.shape[0]
    raw = mm_nt(vkw_ref[...], normed)
    raw = raw[:count] + raw[count:]
    owner = lax.broadcasted_iota(jnp.int32, raw.shape, 0) // HEADS
    w = jnp.where(vid_row == owner.astype(F32), exp_capped(raw, scale), 0.0).astype(BF16)
    sums = mm(w, normed)
    totals = jnp.broadcast_to(
        jnp.sum(w.astype(F32), axis=1, keepdims=True), weight_ref.shape
    )
    pool_ref[...] = sums if first else pool_ref[...] + sums
    weight_ref[...] = totals if first else weight_ref[...] + totals


def start_copies(pairs, sems):
    copies = [pltpu.make_async_copy(src, dst, sems.at[i]) for i, (src, dst) in enumerate(pairs)]
    for copy in copies:
        copy.start()
    return copies


def pack_kernel(x_hbm, vid_hbm, load_ref, vid_ref, sems):
    rows = vid_ref.shape[1]
    copies = start_copies([(x_hbm, load_ref.at[:rows, :]), (vid_hbm, vid_ref)], sems)
    copies[1].wait()
    tile = jnp.broadcast_to(vid_ref[...].astype(F32), (TILE, rows))
    rest = jnp.zeros((TILE, load_ref.shape[1] - rows), F32)
    load_ref[rows:, :] = jnp.concatenate([tile, rest], axis=1).astype(BF16)
    copies[0].wait()


def vid_row(load_ref, rows):
    last = load_ref.shape[0]
    return load_ref[last - TILE :, :rows].astype(F32)[:1, :]


def load_rows(refs):
    last = refs[-1].shape[0] - TILE
    return jnp.concatenate([ref[...] for ref in refs[:-1]] + [refs[-1][:last, :]], axis=0)


def grouped(refs, sizes):
    groups = []
    for size in sizes:
        groups.append(refs[:size])
        refs = refs[size:]
    return groups


def attend(keys, values, counts, qbd, scale):
    p = (counts * exp_capped(mm(keys, qbd), scale)).astype(BF16)
    return mm(values, p)


def fold(o, num_ref, den_ref, b, t, add):
    wide = o.shape[0] - EXTRA
    head = wide // 2
    br = o.shape[1] // 2
    r0 = t * wide
    places = (
        (num_ref, slice(r0, r0 + head), o[:head, :br]),
        (num_ref, slice(r0 + head, r0 + wide), o[head:wide, br:]),
        (den_ref, slice(2 * t, 2 * t + 1), o[wide : wide + 1, :br]),
        (den_ref, slice(2 * t + 1, 2 * t + 2), o[wide : wide + 1, br:]),
    )
    for ref, part, value in places:
        if add:
            ref[b, part, :] += value
        else:
            ref[b, part, :] = value


def prep_kernel(
    load_ref, gain_hbm, win_hbm, vk_hbm, lrows_hbm, srows_hbm, sblock_hbm, scount_hbm, wo_hbm,
    qbd_ref, num_ref, den_ref, counts_ref, mask_ref, vcol_ref, wk_ref, wvt_ref, wo_ref, gain_ref,
    vkw_ref, pool_ref, weight_ref,
    wq_ref, wv_ref, vk_ref, lrows_ref, srows_ref, sblock_ref, scount_ref, want_ref, sems,
):
    width = load_ref.shape[1]
    rows = load_ref.shape[0] - TILE
    blocks, pairs, wide, _ = qbd_ref.shape
    chips = mask_ref.shape[1]
    slots = sblock_ref.shape[1]
    virtual = vk_ref.shape[0]
    br = rows // blocks
    head = width // HEADS
    scale = head ** (-0.5)
    copies = start_copies(
        [
            (gain_hbm, gain_ref), (sblock_hbm, sblock_ref), (scount_hbm, scount_ref),
            (srows_hbm, srows_ref), (lrows_hbm, lrows_ref), (vk_hbm, vk_ref),
            (win_hbm.at[:, width : 2 * width], wk_ref), (win_hbm.at[:, :width], wq_ref),
            (win_hbm.at[:, 2 * width :], wv_ref), (wo_hbm, wo_ref),
        ],
        sems,
    )
    counts_ref[...] = jnp.zeros(counts_ref.shape, F32)
    for copy in copies:
        copy.wait()
    normed = norm_rows(load_ref[:rows, :], gain_ref[...])
    k = mm(normed, wk_ref[...]).astype(BF16)
    v = mm(normed, wv_ref[...]).astype(BF16)
    qt = mm(normed, wq_ref[...]).astype(BF16).T
    vt = v.T
    wvt_ref[...] = wv_ref[...].T

    vkf = vk_ref[...].astype(F32)
    vkbd = jnp.concatenate(
        [jnp.broadcast_to(vkf[j : j + 1, :], (HEADS, width)) for j in range(virtual)], axis=0
    )
    vkbd = jnp.where(of_own_head(vkbd.shape), vkbd, 0.0).astype(BF16)
    vkw_ref[...] = halves(mm_nt(vkbd, wk_ref[...]))
    vid = vid_row(load_ref, rows)
    add_pool(normed, vid, vkw_ref, pool_ref, weight_ref, scale, True)
    vcol_ref[...] = jnp.broadcast_to(vid, (128, rows)).T

    me = lax.axis_index("node")
    place = ring_place(me // CORES, chips)
    core = me % CORES
    for d in range(chips * CORES):
        want_ref[d] = 0
    for b in range(blocks):
        for e in range(slots):
            entry = sblock_ref[b, e]
            want_ref[entry // blocks] = entry % blocks
    for d in range(chips * CORES):
        step = (place - ring_place(jnp.int32(d // CORES), chips) + chips) % chips
        far = jnp.where(core == d % CORES, 0, 1)
        mask_ref[far, step] = jnp.full(mask_ref.shape[2:], want_ref[d].astype(F32), F32)
    for b in range(blocks):
        for e in range(slots):
            device = sblock_ref[b, e] // blocks
            step = (place - ring_place(device // CORES, chips) + chips) % chips
            far = jnp.where(device % CORES == core, 0, 1)
            live = jnp.where(e < scount_ref[b], 1.0, 0.0).astype(F32)
            counts_ref[far, step, b] += counts_of(srows_ref[b, e], br) * live

    zero = jnp.zeros((head, br), BF16)
    ones = jnp.ones((EXTRA, br), BF16)
    for b in range(blocks):
        cols = slice(b * br, (b + 1) * br)
        counts = counts_of(lrows_ref[:, cols], br)
        counts2 = jnp.concatenate([counts, counts], axis=1)
        for t in range(pairs):
            r0 = t * wide
            mid = r0 + head
            end = r0 + wide
            bd = jnp.concatenate(
                [
                    jnp.concatenate([qt[r0:mid, cols], zero], axis=1),
                    jnp.concatenate([zero, qt[mid:end, cols]], axis=1),
                ],
                axis=0,
            )
            qbd_ref[b, t] = bd
            values = jnp.concatenate([vt[r0:end, cols], ones], axis=0)
            fold(attend(k[cols, r0:end], values, counts2, bd, scale), num_ref, den_ref, b, t, False)


def take_sources(
    names, loads, mask_ref, gain_ref, wk_ref, wvt_ref, vkw_ref,
    normed_ref, k_ref, vt_ref, pool_ref, weight_ref,
):
    width = k_ref.shape[1]
    chosen = []
    vids = []
    for i, ((far, step), pieces) in enumerate(zip(names, loads)):
        part = norm_rows(load_rows(pieces), gain_ref[...])
        rows = part.shape[0]
        normed_ref[i * rows : (i + 1) * rows, :] = part
        chosen.append(choose(mask_ref[far, step, :1, :], part))
        vids.append(vid_row(pieces[-1], rows))
    picked = jnp.concatenate(chosen, axis=0)
    k_ref[...] = mm(picked, wk_ref[...]).astype(BF16)
    vt_ref[...] = mm_nt(wvt_ref[...], picked).astype(BF16)
    scale = (width // HEADS) ** (-0.5)
    vid = jnp.concatenate(vids, axis=1)
    add_pool(normed_ref[...], vid, vkw_ref, pool_ref, weight_ref, scale, False)


def add_sources(names, b, counts_ref, qbd_ref, k_ref, vt_ref, num_ref, den_ref):
    _, pairs, wide, _ = qbd_ref.shape
    scale = (2 / wide) ** 0.5
    counts = jnp.concatenate([counts_ref[far, step, b] for far, step in names], axis=0)
    counts2 = jnp.concatenate([counts, counts], axis=1)
    ones = jnp.ones((EXTRA, counts.shape[0]), BF16)
    for t in range(pairs):
        cols = slice(t * wide, (t + 1) * wide)
        values = jnp.concatenate([vt_ref[cols, :], ones], axis=0)
        o = attend(k_ref[:, cols], values, counts2, qbd_ref[b, t], scale)
        fold(o, num_ref, den_ref, b, t, True)


def slots_kernel(
    names, sizes, mask_ref, gain_ref, wk_ref, wvt_ref, vkw_ref, counts_ref, qbd_ref,
    num_in, den_in, pool_in, weight_in, *refs
):
    loads = grouped(refs, sizes)
    num_ref, den_ref, pool_ref, weight_ref, normed_ref, k_ref, vt_ref = refs[sum(sizes) :]
    num_ref[...] = num_in[...]
    den_ref[...] = den_in[...]
    pool_ref[...] = pool_in[...]
    weight_ref[...] = weight_in[...]
    take_sources(
        names, loads, mask_ref, gain_ref, wk_ref, wvt_ref, vkw_ref,
        normed_ref, k_ref, vt_ref, pool_ref, weight_ref,
    )
    for b in range(num_ref.shape[0]):
        add_sources(names, b, counts_ref, qbd_ref, k_ref, vt_ref, num_ref, den_ref)


def finish_kernel(
    names, mask_ref, gain_ref, wk_ref, wvt_ref, vkw_ref, counts_ref, qbd_ref,
    num_in, den_in, pool_in, weight_in, last_ref, vcol_ref, load_ref, wo_ref,
    out_ref, num_ref, den_ref, pool_ref, weight_ref, normed_ref, k_ref, vt_ref,
):
    slots_kernel(
        names, (1,), mask_ref, gain_ref, wk_ref, wvt_ref, vkw_ref, counts_ref, qbd_ref,
        num_in, den_in, pool_in, weight_in, last_ref,
        num_ref, den_ref, pool_ref, weight_ref, normed_ref, k_ref, vt_ref,
    )
    blocks, width, br = num_ref.shape
    head = width // HEADS
    lanes = vcol_ref.shape[1]
    count = pool_ref.shape[0]
    weight = jnp.concatenate([weight_ref[...]] * (width // lanes), axis=1)
    both = mm_nt(halves(pool_ref[...] / weight), wvt_ref[...])
    both = jnp.where(of_own_head((count, width)), both[:count] + both[count:], 0.0)
    pooled = [
        jnp.sum(both[j : j + HEADS], axis=0, keepdims=True) for j in range(0, count, HEADS)
    ]
    for b in range(blocks):
        part = slice(b * br, (b + 1) * br)
        vid = vcol_ref[part, :]
        att = jnp.concatenate(
            [
                num_ref[b, h * head : (h + 1) * head, :] / den_ref[b, h : h + 1, :]
                for h in range(HEADS)
            ],
            axis=0,
        ).T
        pieces = []
        for c in range(0, width, lanes):
            own = jnp.broadcast_to(pooled[0][:, c : c + lanes], (br, lanes))
            for j in range(1, len(pooled)):
                own = jnp.where(vid == float(j), pooled[j][:, c : c + lanes], own)
            pieces.append((att[:, c : c + lanes] + own).astype(BF16))
        mixed = jnp.concatenate(pieces, axis=1)
        out_ref[part, :] = (load_ref[part, :].astype(F32) + mm(mixed, wo_ref[...])).astype(BF16)


def params(mib):
    return pltpu.CompilerParams(vmem_limit_bytes=mib * 2**20)


def cost(flops):
    return pl.CostEstimate(flops=flops, bytes_accessed=1024, transcendentals=0)


def body(
    activations,
    norm_gain,
    project_in,
    project_out,
    virtual_keys,
    virtual_id,
    local_rows,
    slot_block,
    slot_count,
    slot_rows,
):
    _, rows, width = activations.shape
    br = slot_rows.shape[3]
    slots = slot_block.shape[1]
    blocks = rows // br
    devices = lax.axis_size("node")
    chips = devices // CORES
    virtual = virtual_keys.shape[1]
    pairs = HEADS // 2
    wide = width // pairs
    shape = jax.ShapeDtypeStruct
    after = lax.optimization_barrier
    unit = 2**16

    load = pl.pallas_call(
        pack_kernel,
        out_shape=shape((rows + TILE, width), BF16),
        in_specs=[HBM] * 2,
        out_specs=VMEM,
        scratch_shapes=[pltpu.VMEM((1, rows), jnp.int32), pltpu.SemaphoreType.DMA((2,))],
        compiler_params=params(24),
        cost_estimate=cost(unit),
        name="pack_rows",
    )(
        pltpu.with_memory_space_constraint(activations[0], pltpu.HBM),
        pltpu.with_memory_space_constraint(virtual_id.reshape(1, rows), pltpu.HBM),
    )
    near = {1: to_next_chip(load, devices, 1)}
    far = {0: swapped(load, devices, 1)}

    accumulators = (
        shape((blocks, width, br), F32),
        shape((blocks, HEADS, br), F32),
        shape((virtual * HEADS, width), F32),
        shape((virtual * HEADS, 128), F32),
    )
    square = shape((width, width), BF16)
    qbd, num, den, counts, mask, vcol, wk, wvt, wo, gain, vkw, pool, weight = pl.pallas_call(
        prep_kernel,
        out_shape=(
            (shape((blocks, pairs, wide, 2 * br), BF16),)
            + accumulators[:2]
            + (
                shape((CORES, chips, blocks, br, br), F32),
                shape((CORES, chips, 8, 128), F32),
                shape((rows, 128), F32),
                square,
                square,
                square,
                shape((1, width), F32),
                shape((2 * virtual * HEADS, width), BF16),
            )
            + accumulators[2:]
        ),
        in_specs=[VMEM] + [HBM] * 8,
        out_specs=[VMEM] * 13,
        scratch_shapes=[
            pltpu.VMEM((width, width), BF16),
            pltpu.VMEM((width, width), BF16),
            pltpu.VMEM((virtual, width), BF16),
            pltpu.VMEM(local_rows.shape, jnp.int32),
            pltpu.VMEM(slot_rows.shape, jnp.int32),
            pltpu.SMEM((blocks, slots), jnp.int32),
            pltpu.SMEM((blocks,), jnp.int32),
            pltpu.SMEM((devices,), jnp.int32),
            pltpu.SemaphoreType.DMA((10,)),
        ],
        compiler_params=params(32),
        cost_estimate=cost(unit),
        name="prepare",
    )(
        load,
        *[
            pltpu.with_memory_space_constraint(value, pltpu.HBM)
            for value in (
                norm_gain, project_in[0], virtual_keys[0], local_rows, slot_rows, slot_block,
                slot_count, project_out[0],
            )
        ],
    )

    def work(count):
        return [
            pltpu.VMEM((count * rows, width), BF16),
            pltpu.VMEM((count * br, width), BF16),
            pltpu.VMEM((width, count * br), BF16),
        ]

    if chips > 2:
        back, den = after((load, den))
        near[chips - 1] = to_next_chip(back, devices, -1)
    sums = (num, den, pool, weight)

    def arrive(step, sums):
        near[step], first = after((near[step], sums[1]))
        return (sums[0], first) + sums[2:]

    def slots_call(names, sums, name):
        loads = [(far if other else near)[step] for other, step in names]
        loads = [load if isinstance(load, list) else [load] for load in loads]
        sizes = tuple(len(load) for load in loads)
        return pl.pallas_call(
            functools.partial(slots_kernel, tuple(names), sizes),
            out_shape=accumulators,
            in_specs=[VMEM] * (11 + sum(sizes)),
            out_specs=[VMEM] * 4,
            scratch_shapes=work(len(names)),
            compiler_params=params(40),
            cost_estimate=cost(unit),
            name=name,
        )(
            mask, gain, wk, wvt, vkw, counts, qbd, *sums,
            *[piece for load in loads for piece in load],
        )

    ahead = chips // 2
    order = []
    for s in range(1, ahead + 1):
        order.append((s, 1))
        if s < chips - s:
            order.append((chips - s, -1))
    sums = slots_call([(1, 0)], sums, "slots_own")

    def hop_on(step, way):
        nexts = step + way
        if nexts not in near and (nexts, way) in order:
            near[nexts] = to_next_chip(near[step], devices, way)

    firsts = order[:-1][:2]
    for step, way in firsts:
        sums = arrive(step, sums)
        hop_on(step, way)
    for step, _ in firsts:
        far[step] = swapped_parts(near[step], devices, PARTS)
    if firsts:
        sums = slots_call([(0, step) for step, _ in firsts], sums, "slots_near")
        sums = slots_call([(1, step) for step, _ in firsts], sums, "slots_far")
    for i, (step, way) in enumerate(order[len(firsts) :]):
        sums = arrive(step, sums)
        hop_on(step, way)
        far[step] = swapped(near[step], devices, 1)
        names = [(0, step), (1, step)]
        if step == order[-1][0]:
            names = names[:1]
        sums = slots_call(names, sums, "slots_%d" % i)
    names = ((1, order[-1][0]),)
    updated = pl.pallas_call(
        functools.partial(finish_kernel, names),
        out_shape=shape((rows, width), BF16),
        in_specs=[VMEM] * 15,
        out_specs=VMEM,
        scratch_shapes=[pltpu.VMEM(leaf.shape, leaf.dtype) for leaf in accumulators] + work(1),
        compiler_params=params(40),
        cost_estimate=cost(unit),
        name="finish",
    )(
        mask, gain, wk, wvt, vkw, counts, qbd, *sums, far[names[0][1]], vcol, load, wo
    )
    return to_next_segment(updated[None])


def solution(mesh):
    placed = (
        P("segment", "node", None),
        P("segment", None),
        P("segment", None, None),
        P("segment", None, None),
        P("segment", None, None),
        P("node", None),
        P(None, "node"),
        P("node", None),
        P("node"),
        P("node", None, None, None),
    )
    return jax.shard_map(
        body, mesh=mesh, in_specs=placed, out_specs=P("segment", "node", None), check_vma=False
    )
```

```python
import functools

import jax
import jax.numpy as jnp
from jax import lax
from jax.experimental import pallas as pl
from jax.experimental.pallas import tpu as pltpu
from jax.sharding import PartitionSpec as P

HEADS = 8
CORES = 2
EPSILON = 1e-05
CAP_LIMIT = 10.0
LOG2E = 1.4426950408889634
EXTRA = 16
PARTS = 2
F32 = jnp.float32
BF16 = jnp.bfloat16
HBM = pl.BlockSpec(memory_space=pltpu.HBM)
VMEM = pl.BlockSpec(memory_space=pltpu.VMEM)


def ring_order(chips):
    return list(range(0, 1)) + list(range(1, chips, 2)) + list(range((chips - 1) // 2 * 2, 0, -2))


def ring_place(chip, chips):
    return jnp.where(chip % 2 == 1, (chip + 1) // 2, (chips - chip // 2) % chips)


def to_next_chip(value, devices, way):
    chips = devices // CORES
    order = ring_order(chips)
    pairs = [
        (order[i] * CORES + c, order[(i + way) % chips] * CORES + c)
        for i in range(chips)
        for c in range(CORES)
    ]
    return lax.ppermute(value, "node", pairs)


def swapped(value, devices, distance):
    return lax.ppermute(value, "node", [(d, d ^ distance) for d in range(devices)])


def swapped_parts(value, devices, parts):
    tiles = value.shape[0] // 16
    cuts = [0] + [16 * (-(-tiles * (i + 1) // parts)) for i in range(parts)]
    return [swapped(value[a:b], devices, 1) for a, b in zip(cuts, cuts[1:])]


def to_next_segment(value):
    count = lax.axis_size("segment")
    return lax.ppermute(value, "segment", [(s, (s + 1) % count) for s in range(count)])


def norm_rows(rows_in, gain_row):
    widened = rows_in.astype(F32)
    center = widened - jnp.mean(widened, axis=-1, keepdims=True)
    spread = jnp.mean(center * center, axis=-1, keepdims=True)
    return (center * lax.rsqrt(spread + EPSILON) * gain_row).astype(BF16)


def exp_capped(raw, scale):
    return jnp.exp2((CAP_LIMIT * LOG2E) * jnp.tanh(raw * (scale / CAP_LIMIT)))


def counts_of(index_rows, block_rows):
    rows = lax.broadcasted_iota(jnp.int32, (block_rows, index_rows.shape[1]), 0)
    total = jnp.zeros(rows.shape, F32)
    for j in range(index_rows.shape[0]):
        total = total + jnp.where(index_rows[j : j + 1, :] == rows, 1.0, 0.0)
    return total


def mm(a, b):
    return jnp.dot(a, b, preferred_element_type=F32)


def mm_nt(a, b):
    return lax.dot_general(a, b, (((1,), (1,)), ((), ())), preferred_element_type=F32)


def choose(mask_row, rows):
    lanes = mask_row.shape[1]
    count, width = rows.shape
    br = count // 2
    mask = jnp.broadcast_to(mask_row, (br, lanes))
    mask = jnp.concatenate([mask] * (width // lanes), axis=1)
    first, second = rows[:br, :].astype(F32), rows[br:, :].astype(F32)
    return jnp.where(mask > 0.5, second, first).astype(rows.dtype)


def halves(value):
    high = value.astype(BF16)
    low = (value - high.astype(F32)).astype(BF16)
    return jnp.concatenate([high, low], axis=0)


def of_own_head(shape):
    head = lax.broadcasted_iota(jnp.int32, shape, 0) % HEADS
    return head == lax.broadcasted_iota(jnp.int32, shape, 1) // (shape[1] // HEADS)


def add_pool(normed, vid_row, vkw_ref, pool_ref, weight_ref, scale, first):
    count = pool_ref.shape[0]
    raw = mm_nt(vkw_ref[...], normed)
    raw = raw[:count] + raw[count:]
    owner = lax.broadcasted_iota(jnp.int32, raw.shape, 0) // HEADS
    w = jnp.where(vid_row == owner.astype(F32), exp_capped(raw, scale), 0.0).astype(BF16)
    sums = mm(w, normed)
    totals = jnp.broadcast_to(
        jnp.sum(w.astype(F32), axis=1, keepdims=True), weight_ref.shape
    )
    pool_ref[...] = sums if first else pool_ref[...] + sums
    weight_ref[...] = totals if first else weight_ref[...] + totals


def start_copies(pairs, sems):
    copies = [pltpu.make_async_copy(src, dst, sems.at[i]) for i, (src, dst) in enumerate(pairs)]
    for copy in copies:
        copy.start()
    return copies


def pack_kernel(x_hbm, vid_hbm, load_ref, vid_ref, sems):
    rows = vid_ref.shape[1]
    copies = start_copies([(x_hbm, load_ref.at[:rows, :]), (vid_hbm, vid_ref)], sems)
    copies[1].wait()
    tile = jnp.broadcast_to(vid_ref[...].astype(F32), (EXTRA, rows))
    rest = jnp.zeros((EXTRA, load_ref.shape[1] - rows), F32)
    load_ref[rows:, :] = jnp.concatenate([tile, rest], axis=1).astype(BF16)
    copies[0].wait()


def vid_row(load_ref, rows):
    last = load_ref.shape[0]
    return load_ref[last - EXTRA :, :rows].astype(F32)[:1, :]


def load_rows(refs):
    last = refs[-1].shape[0] - EXTRA
    return jnp.concatenate([ref[...] for ref in refs[:-1]] + [refs[-1][:last, :]], axis=0)


def grouped(refs, sizes):
    groups = []
    for size in sizes:
        groups.append(refs[:size])
        refs = refs[size:]
    return groups


def attend(keys, values, counts, qbd, scale):
    p = (counts * exp_capped(mm(keys, qbd), scale)).astype(BF16)
    return mm(values, p)


def fold(o, num_ref, den_ref, b, t, add):
    wide = o.shape[0] - EXTRA
    head = wide // 2
    br = o.shape[1] // 2
    r0 = t * wide
    places = (
        (num_ref, slice(r0, r0 + head), o[:head, :br]),
        (num_ref, slice(r0 + head, r0 + wide), o[head:wide, br:]),
        (den_ref, slice(2 * t, 2 * t + 1), o[wide : wide + 1, :br]),
        (den_ref, slice(2 * t + 1, 2 * t + 2), o[wide : wide + 1, br:]),
    )
    for ref, part, value in places:
        if add:
            ref[b, part, :] += value
        else:
            ref[b, part, :] = value


def prep_kernel(
    load_ref, gain_hbm, win_hbm, vk_hbm, lrows_hbm, srows_hbm, sblock_hbm, scount_hbm, wo_hbm,
    qbd_ref, num_ref, den_ref, counts_ref, mask_ref, vcol_ref, wk_ref, wvt_ref, wo_ref, gain_ref,
    vkw_ref, pool_ref, weight_ref,
    wq_ref, wv_ref, vk_ref, lrows_ref, srows_ref, sblock_ref, scount_ref, want_ref, sems,
):
    width = load_ref.shape[1]
    rows = load_ref.shape[0] - EXTRA
    blocks, pairs, wide, _ = qbd_ref.shape
    chips = mask_ref.shape[1]
    slots = sblock_ref.shape[1]
    virtual = vk_ref.shape[0]
    br = rows // blocks
    head = width // HEADS
    scale = head ** (-0.5)
    copies = start_copies(
        [
            (gain_hbm, gain_ref), (sblock_hbm, sblock_ref), (scount_hbm, scount_ref),
            (srows_hbm, srows_ref), (lrows_hbm, lrows_ref), (vk_hbm, vk_ref),
            (win_hbm.at[:, width : 2 * width], wk_ref), (win_hbm.at[:, :width], wq_ref),
            (win_hbm.at[:, 2 * width :], wv_ref), (wo_hbm, wo_ref),
        ],
        sems,
    )
    counts_ref[...] = jnp.zeros(counts_ref.shape, F32)
    for copy in copies:
        copy.wait()
    normed = norm_rows(load_ref[:rows, :], gain_ref[...])
    k = mm(normed, wk_ref[...]).astype(BF16)
    v = mm(normed, wv_ref[...]).astype(BF16)
    qt = mm(normed, wq_ref[...]).astype(BF16).T
    vt = v.T
    wvt_ref[...] = wv_ref[...].T

    vkf = vk_ref[...].astype(F32)
    vkbd = jnp.concatenate(
        [jnp.broadcast_to(vkf[j : j + 1, :], (HEADS, width)) for j in range(virtual)], axis=0
    )
    vkbd = jnp.where(of_own_head(vkbd.shape), vkbd, 0.0).astype(BF16)
    vkw_ref[...] = halves(mm_nt(vkbd, wk_ref[...]))
    vid = vid_row(load_ref, rows)
    add_pool(normed, vid, vkw_ref, pool_ref, weight_ref, scale, True)
    vcol_ref[...] = jnp.broadcast_to(vid, (128, rows)).T

    me = lax.axis_index("node")
    place = ring_place(me // CORES, chips)
    core = me % CORES
    for d in range(chips * CORES):
        want_ref[d] = 0
    for b in range(blocks):
        for e in range(slots):
            entry = sblock_ref[b, e]
            want_ref[entry // blocks] = entry % blocks
    for d in range(chips * CORES):
        step = (place - ring_place(jnp.int32(d // CORES), chips) + chips) % chips
        far = jnp.where(core == d % CORES, 0, 1)
        mask_ref[far, step] = jnp.full(mask_ref.shape[2:], want_ref[d].astype(F32), F32)
    for b in range(blocks):
        for e in range(slots):
            device = sblock_ref[b, e] // blocks
            step = (place - ring_place(device // CORES, chips) + chips) % chips
            far = jnp.where(device % CORES == core, 0, 1)
            live = jnp.where(e < scount_ref[b], 1.0, 0.0).astype(F32)
            counts_ref[far, step, b] += counts_of(srows_ref[b, e], br) * live

    zero = jnp.zeros((head, br), BF16)
    ones = jnp.ones((EXTRA, br), BF16)
    for b in range(blocks):
        cols = slice(b * br, (b + 1) * br)
        counts = counts_of(lrows_ref[:, cols], br)
        counts2 = jnp.concatenate([counts, counts], axis=1)
        for t in range(pairs):
            r0 = t * wide
            mid = r0 + head
            end = r0 + wide
            bd = jnp.concatenate(
                [
                    jnp.concatenate([qt[r0:mid, cols], zero], axis=1),
                    jnp.concatenate([zero, qt[mid:end, cols]], axis=1),
                ],
                axis=0,
            )
            qbd_ref[b, t] = bd
            values = jnp.concatenate([vt[r0:end, cols], ones], axis=0)
            fold(attend(k[cols, r0:end], values, counts2, bd, scale), num_ref, den_ref, b, t, False)


def take_sources(
    names, loads, mask_ref, gain_ref, wk_ref, wvt_ref, vkw_ref,
    normed_ref, k_ref, vt_ref, pool_ref, weight_ref,
):
    width = k_ref.shape[1]
    chosen = []
    vids = []
    for i, ((far, step), pieces) in enumerate(zip(names, loads)):
        part = norm_rows(load_rows(pieces), gain_ref[...])
        rows = part.shape[0]
        normed_ref[i * rows : (i + 1) * rows, :] = part
        chosen.append(choose(mask_ref[far, step, :1, :], part))
        vids.append(vid_row(pieces[-1], rows))
    picked = jnp.concatenate(chosen, axis=0)
    k_ref[...] = mm(picked, wk_ref[...]).astype(BF16)
    vt_ref[...] = mm_nt(wvt_ref[...], picked).astype(BF16)
    scale = (width // HEADS) ** (-0.5)
    vid = jnp.concatenate(vids, axis=1)
    add_pool(normed_ref[...], vid, vkw_ref, pool_ref, weight_ref, scale, False)


def add_sources(names, b, counts_ref, qbd_ref, k_ref, vt_ref, num_ref, den_ref):
    _, pairs, wide, _ = qbd_ref.shape
    scale = (2 / wide) ** 0.5
    counts = jnp.concatenate([counts_ref[far, step, b] for far, step in names], axis=0)
    counts2 = jnp.concatenate([counts, counts], axis=1)
    ones = jnp.ones((EXTRA, counts.shape[0]), BF16)
    for t in range(pairs):
        cols = slice(t * wide, (t + 1) * wide)
        values = jnp.concatenate([vt_ref[cols, :], ones], axis=0)
        o = attend(k_ref[:, cols], values, counts2, qbd_ref[b, t], scale)
        fold(o, num_ref, den_ref, b, t, True)


def slots_kernel(
    names, sizes, mask_ref, gain_ref, wk_ref, wvt_ref, vkw_ref, counts_ref, qbd_ref,
    num_in, den_in, pool_in, weight_in, *refs
):
    loads = grouped(refs, sizes)
    num_ref, den_ref, pool_ref, weight_ref, normed_ref, k_ref, vt_ref = refs[sum(sizes) :]
    num_ref[...] = num_in[...]
    den_ref[...] = den_in[...]
    pool_ref[...] = pool_in[...]
    weight_ref[...] = weight_in[...]
    take_sources(
        names, loads, mask_ref, gain_ref, wk_ref, wvt_ref, vkw_ref,
        normed_ref, k_ref, vt_ref, pool_ref, weight_ref,
    )
    for b in range(num_ref.shape[0]):
        add_sources(names, b, counts_ref, qbd_ref, k_ref, vt_ref, num_ref, den_ref)


def finish_kernel(names, b, lead, *refs):
    if lead:
        (
            mask_ref, gain_ref, wk_ref, wvt_ref, vkw_ref, pool_in, weight_in, last_ref,
            counts_ref, qbd_ref, num_in, den_in, vcol_ref, load_ref, wo_ref,
            out_ref, k_ref, vt_ref, pooled_ref,
            num_ref, den_ref, pool_ref, weight_ref, normed_ref,
        ) = refs
    else:
        (
            k_ref, vt_ref, pooled_ref,
            counts_ref, qbd_ref, num_in, den_in, vcol_ref, load_ref, wo_ref,
            out_ref, num_ref, den_ref,
        ) = refs
    _, width, br = num_ref.shape
    head = width // HEADS
    lanes = vcol_ref.shape[1]
    num_ref[b] = num_in[b]
    den_ref[b] = den_in[b]
    if lead:
        pool_ref[...] = pool_in[...]
        weight_ref[...] = weight_in[...]
        take_sources(
            names, [[last_ref]], mask_ref, gain_ref, wk_ref, wvt_ref, vkw_ref,
            normed_ref, k_ref, vt_ref, pool_ref, weight_ref,
        )
        count = pool_ref.shape[0]
        weight = jnp.concatenate([weight_ref[...]] * (width // lanes), axis=1)
        both = mm_nt(halves(pool_ref[...] / weight), wvt_ref[...])
        both = jnp.where(of_own_head((count, width)), both[:count] + both[count:], 0.0)
        for j in range(0, count, HEADS):
            pooled_ref[j // HEADS : j // HEADS + 1, :] = jnp.sum(
                both[j : j + HEADS], axis=0, keepdims=True
            )
    add_sources(names, b, counts_ref, qbd_ref, k_ref, vt_ref, num_ref, den_ref)
    part = slice(b * br, (b + 1) * br)
    vid = vcol_ref[part, :]
    att = jnp.concatenate(
        [
            num_ref[b, h * head : (h + 1) * head, :] / den_ref[b, h : h + 1, :]
            for h in range(HEADS)
        ],
        axis=0,
    ).T
    pieces = []
    for c in range(0, width, lanes):
        own = jnp.broadcast_to(pooled_ref[0:1, c : c + lanes], (br, lanes))
        for j in range(1, pooled_ref.shape[0]):
            own = jnp.where(vid == float(j), pooled_ref[j : j + 1, c : c + lanes], own)
        pieces.append((att[:, c : c + lanes] + own).astype(BF16))
    mixed = jnp.concatenate(pieces, axis=1)
    out_ref[...] = (load_ref[part, :].astype(F32) + mm(mixed, wo_ref[...])).astype(BF16)


def place_kernel(b, rows_ref, *refs):
    out_ref, sems = refs[-2:]
    br = rows_ref.shape[0]
    copy = pltpu.make_async_copy(rows_ref, out_ref.at[0, b * br : (b + 1) * br, :], sems.at[0])
    copy.start()
    copy.wait()


def params(mib):
    return pltpu.CompilerParams(vmem_limit_bytes=mib * 2**20)


def cost(flops):
    return pl.CostEstimate(flops=flops, bytes_accessed=1024, transcendentals=0)


def body(
    activations,
    norm_gain,
    project_in,
    project_out,
    virtual_keys,
    virtual_id,
    local_rows,
    slot_block,
    slot_count,
    slot_rows,
):
    _, rows, width = activations.shape
    br = slot_rows.shape[3]
    slots = slot_block.shape[1]
    blocks = rows // br
    devices = lax.axis_size("node")
    chips = devices // CORES
    virtual = virtual_keys.shape[1]
    pairs = HEADS // 2
    wide = width // pairs
    shape = jax.ShapeDtypeStruct
    after = lax.optimization_barrier
    unit = 2**16

    load = pl.pallas_call(
        pack_kernel,
        out_shape=shape((rows + EXTRA, width), BF16),
        in_specs=[HBM] * 2,
        out_specs=VMEM,
        scratch_shapes=[pltpu.VMEM((1, rows), jnp.int32), pltpu.SemaphoreType.DMA((2,))],
        compiler_params=params(24),
        cost_estimate=cost(unit),
        name="pack_rows",
    )(
        pltpu.with_memory_space_constraint(activations[0], pltpu.HBM),
        pltpu.with_memory_space_constraint(virtual_id.reshape(1, rows), pltpu.HBM),
    )
    near = {1: to_next_chip(load, devices, 1)}
    far = {0: swapped(load, devices, 1)}

    accumulators = (
        shape((blocks, width, br), F32),
        shape((blocks, HEADS, br), F32),
        shape((virtual * HEADS, width), F32),
        shape((virtual * HEADS, 128), F32),
    )
    square = shape((width, width), BF16)
    qbd, num, den, counts, mask, vcol, wk, wvt, wo, gain, vkw, pool, weight = pl.pallas_call(
        prep_kernel,
        out_shape=(
            (shape((blocks, pairs, wide, 2 * br), BF16),)
            + accumulators[:2]
            + (
                shape((CORES, chips, blocks, br, br), F32),
                shape((CORES, chips, 8, 128), F32),
                shape((rows, 128), F32),
                square,
                square,
                square,
                shape((1, width), F32),
                shape((2 * virtual * HEADS, width), BF16),
            )
            + accumulators[2:]
        ),
        in_specs=[VMEM] + [HBM] * 8,
        out_specs=[VMEM] * 13,
        scratch_shapes=[
            pltpu.VMEM((width, width), BF16),
            pltpu.VMEM((width, width), BF16),
            pltpu.VMEM((virtual, width), BF16),
            pltpu.VMEM(local_rows.shape, jnp.int32),
            pltpu.VMEM(slot_rows.shape, jnp.int32),
            pltpu.SMEM((blocks, slots), jnp.int32),
            pltpu.SMEM((blocks,), jnp.int32),
            pltpu.SMEM((devices,), jnp.int32),
            pltpu.SemaphoreType.DMA((10,)),
        ],
        compiler_params=params(32),
        cost_estimate=cost(unit),
        name="prepare",
    )(
        load,
        *[
            pltpu.with_memory_space_constraint(value, pltpu.HBM)
            for value in (
                norm_gain, project_in[0], virtual_keys[0], local_rows, slot_rows, slot_block,
                slot_count, project_out[0],
            )
        ],
    )

    def work(count):
        return [
            pltpu.VMEM((count * rows, width), BF16),
            pltpu.VMEM((count * br, width), BF16),
            pltpu.VMEM((width, count * br), BF16),
        ]

    if chips > 2:
        back, den = after((load, den))
        near[chips - 1] = to_next_chip(back, devices, -1)
    sums = (num, den, pool, weight)

    def arrive(step, sums):
        near[step], first = after((near[step], sums[1]))
        return (sums[0], first) + sums[2:]

    def slots_call(names, sums, name):
        loads = [(far if other else near)[step] for other, step in names]
        loads = [load if isinstance(load, list) else [load] for load in loads]
        sizes = tuple(len(load) for load in loads)
        return pl.pallas_call(
            functools.partial(slots_kernel, tuple(names), sizes),
            out_shape=accumulators,
            in_specs=[VMEM] * (11 + sum(sizes)),
            out_specs=[VMEM] * 4,
            scratch_shapes=work(len(names)),
            compiler_params=params(40),
            cost_estimate=cost(unit),
            name=name,
        )(
            mask, gain, wk, wvt, vkw, counts, qbd, *sums,
            *[piece for load in loads for piece in load],
        )

    ahead = chips // 2
    order = []
    for s in range(1, ahead + 1):
        order.append((s, 1))
        if s < chips - s:
            order.append((chips - s, -1))
    sums = slots_call([(1, 0)], sums, "slots_own")

    def hop_on(step, way):
        nexts = step + way
        if nexts not in near and (nexts, way) in order:
            near[nexts] = to_next_chip(near[step], devices, way)

    firsts = order[:-1][:2]
    for step, way in firsts:
        sums = arrive(step, sums)
        hop_on(step, way)
    for step, _ in firsts:
        far[step] = swapped_parts(near[step], devices, PARTS)
    if firsts:
        sums = slots_call([(0, step) for step, _ in firsts], sums, "slots_near")
        sums = slots_call([(1, step) for step, _ in firsts], sums, "slots_far")
    for i, (step, way) in enumerate(order[len(firsts) :]):
        sums = arrive(step, sums)
        hop_on(step, way)
        far[step] = swapped(near[step], devices, 1)
        names = [(0, step), (1, step)]
        if step == order[-1][0]:
            names = names[:1]
        sums = slots_call(names, sums, "slots_%d" % i)
    names = ((1, order[-1][0]),)
    shared = (counts, qbd, sums[0], sums[1], vcol, load, wo)
    scratch = [pltpu.VMEM(leaf.shape, leaf.dtype) for leaf in accumulators]
    carried = (
        shape((br, width), BF16), shape((width, br), BF16), shape((virtual, width), F32)
    )
    results = []
    for b in range(blocks):
        lead = b == 0
        outs = pl.pallas_call(
            functools.partial(finish_kernel, names, b, lead),
            out_shape=(shape((br, width), BF16),) + (carried if lead else ()),
            in_specs=[VMEM] * (15 if lead else 10),
            out_specs=(VMEM,) * (4 if lead else 1),
            scratch_shapes=scratch + work(1)[:1] if lead else scratch[:2],
            compiler_params=params(40),
            cost_estimate=cost(unit),
            name="finish_%d" % b,
        )(
            *(
                (mask, gain, wk, wvt, vkw, sums[2], sums[3], far[names[0][1]])
                if lead
                else kept
            ),
            *shared,
        )
        if lead:
            kept = tuple(outs[1:])
        results.append(to_next_segment(outs[0]))
    joined = None
    for b in range(blocks):
        earlier = [] if joined is None else [joined]
        joined = pl.pallas_call(
            functools.partial(place_kernel, b),
            out_shape=shape((1, rows, width), BF16),
            in_specs=[VMEM] + [HBM] * len(earlier),
            out_specs=HBM,
            scratch_shapes=[pltpu.SemaphoreType.DMA((1,))],
            input_output_aliases={1: 0} if earlier else {},
            compiler_params=params(24),
            cost_estimate=cost(unit),
            name="place_%d" % b,
        )(results[b], *earlier)
    return joined


def solution(mesh):
    placed = (
        P("segment", "node", None),
        P("segment", None),
        P("segment", None, None),
        P("segment", None, None),
        P("segment", None, None),
        P("node", None),
        P(None, "node"),
        P("node", None),
        P("node"),
        P("node", None, None, None),
    )
    return jax.shard_map(
        body, mesh=mesh, in_specs=placed, out_specs=P("segment", "node", None), check_vma=False
    )
```

```python
import functools

import jax
import jax.numpy as jnp
from jax import lax
from jax.experimental import pallas as pl
from jax.experimental.pallas import tpu as pltpu
from jax.sharding import PartitionSpec as P

HEADS = 8
CORES = 2
EPSILON = 1e-05
CAP_LIMIT = 10.0
LOG2E = 1.4426950408889634
EXTRA = 16
PARTS = 2
F32 = jnp.float32
BF16 = jnp.bfloat16
HBM = pl.BlockSpec(memory_space=pltpu.HBM)
VMEM = pl.BlockSpec(memory_space=pltpu.VMEM)


def ring_order(chips):
    return list(range(0, 1)) + list(range(1, chips, 2)) + list(range((chips - 1) // 2 * 2, 0, -2))


def ring_place(chip, chips):
    return jnp.where(chip % 2 == 1, (chip + 1) // 2, (chips - chip // 2) % chips)


def to_next_chip(value, devices, way):
    chips = devices // CORES
    order = ring_order(chips)
    pairs = [
        (order[i] * CORES + c, order[(i + way) % chips] * CORES + c)
        for i in range(chips)
        for c in range(CORES)
    ]
    return lax.ppermute(value, "node", pairs)


def swapped(value, devices, distance):
    return lax.ppermute(value, "node", [(d, d ^ distance) for d in range(devices)])


def swapped_parts(value, devices, parts):
    tiles = value.shape[0] // 16
    cuts = [0] + [16 * (-(-tiles * (i + 1) // parts)) for i in range(parts)]
    return [swapped(value[a:b], devices, 1) for a, b in zip(cuts, cuts[1:])]


def to_next_segment(value):
    count = lax.axis_size("segment")
    return lax.ppermute(value, "segment", [(s, (s + 1) % count) for s in range(count)])


def norm_rows(rows_in, gain_row):
    widened = rows_in.astype(F32)
    center = widened - jnp.mean(widened, axis=-1, keepdims=True)
    spread = jnp.mean(center * center, axis=-1, keepdims=True)
    return (center * lax.rsqrt(spread + EPSILON) * gain_row).astype(BF16)


def exp_capped(raw, scale):
    return jnp.exp2((CAP_LIMIT * LOG2E) * jnp.tanh(raw * (scale / CAP_LIMIT)))


def counts_of(index_rows, block_rows):
    rows = lax.broadcasted_iota(jnp.int32, (block_rows, index_rows.shape[1]), 0)
    total = jnp.zeros(rows.shape, F32)
    for j in range(index_rows.shape[0]):
        total = total + jnp.where(index_rows[j : j + 1, :] == rows, 1.0, 0.0)
    return total


def mm(a, b):
    return jnp.dot(a, b, preferred_element_type=F32)


def mm_nt(a, b):
    return lax.dot_general(a, b, (((1,), (1,)), ((), ())), preferred_element_type=F32)


def choose(mask_row, rows):
    lanes = mask_row.shape[1]
    count, width = rows.shape
    br = count // 2
    mask = jnp.broadcast_to(mask_row, (br, lanes))
    mask = jnp.concatenate([mask] * (width // lanes), axis=1)
    first, second = rows[:br, :].astype(F32), rows[br:, :].astype(F32)
    return jnp.where(mask > 0.5, second, first).astype(rows.dtype)


def halves(value):
    high = value.astype(BF16)
    low = (value - high.astype(F32)).astype(BF16)
    return jnp.concatenate([high, low], axis=0)


def of_own_head(shape):
    head = lax.broadcasted_iota(jnp.int32, shape, 0) % HEADS
    return head == lax.broadcasted_iota(jnp.int32, shape, 1) // (shape[1] // HEADS)


def add_pool(normed, vid_row, vkw_ref, pool_ref, weight_ref, scale, first):
    count = pool_ref.shape[0]
    raw = mm_nt(vkw_ref[...], normed)
    raw = raw[:count] + raw[count:]
    owner = lax.broadcasted_iota(jnp.int32, raw.shape, 0) // HEADS
    w = jnp.where(vid_row == owner.astype(F32), exp_capped(raw, scale), 0.0).astype(BF16)
    sums = mm(w, normed)
    totals = jnp.broadcast_to(
        jnp.sum(w.astype(F32), axis=1, keepdims=True), weight_ref.shape
    )
    pool_ref[...] = sums if first else pool_ref[...] + sums
    weight_ref[...] = totals if first else weight_ref[...] + totals


def start_copies(pairs, sems):
    copies = [pltpu.make_async_copy(src, dst, sems.at[i]) for i, (src, dst) in enumerate(pairs)]
    for copy in copies:
        copy.start()
    return copies


def pack_kernel(x_hbm, vid_hbm, load_ref, vid_ref, sems):
    rows = vid_ref.shape[1]
    copies = start_copies([(x_hbm, load_ref.at[:rows, :]), (vid_hbm, vid_ref)], sems)
    copies[1].wait()
    tile = jnp.broadcast_to(vid_ref[...].astype(F32), (EXTRA, rows))
    rest = jnp.zeros((EXTRA, load_ref.shape[1] - rows), F32)
    load_ref[rows:, :] = jnp.concatenate([tile, rest], axis=1).astype(BF16)
    copies[0].wait()


def vid_row(load_ref, rows):
    last = load_ref.shape[0]
    return load_ref[last - EXTRA :, :rows].astype(F32)[:1, :]


def load_rows(refs):
    last = refs[-1].shape[0] - EXTRA
    return jnp.concatenate([ref[...] for ref in refs[:-1]] + [refs[-1][:last, :]], axis=0)


def grouped(refs, sizes):
    groups = []
    for size in sizes:
        groups.append(refs[:size])
        refs = refs[size:]
    return groups


def attend(keys, values, counts, qbd, scale):
    p = (counts * exp_capped(mm(keys, qbd), scale)).astype(BF16)
    return mm(values, p)


def fold(o, num_ref, den_ref, b, t, add):
    wide = o.shape[0] - EXTRA
    head = wide // 2
    br = o.shape[1] // 2
    r0 = t * wide
    places = (
        (num_ref, slice(r0, r0 + head), o[:head, :br]),
        (num_ref, slice(r0 + head, r0 + wide), o[head:wide, br:]),
        (den_ref, slice(2 * t, 2 * t + 1), o[wide : wide + 1, :br]),
        (den_ref, slice(2 * t + 1, 2 * t + 2), o[wide : wide + 1, br:]),
    )
    for ref, part, value in places:
        if add:
            ref[b, part, :] += value
        else:
            ref[b, part, :] = value


def prep_kernel(
    load_ref, gain_hbm, win_hbm, vk_hbm, lrows_hbm, srows_hbm, sblock_hbm, scount_hbm, wo_hbm,
    qbd_ref, num_ref, den_ref, counts_ref, mask_ref, vcol_ref, wk_ref, wvt_ref, wo_ref, gain_ref,
    vkw_ref, pool_ref, weight_ref,
    wq_ref, wv_ref, vk_ref, lrows_ref, srows_ref, sblock_ref, scount_ref, want_ref, sems,
):
    width = load_ref.shape[1]
    rows = load_ref.shape[0] - EXTRA
    blocks, pairs, wide, _ = qbd_ref.shape
    chips = mask_ref.shape[1]
    slots = sblock_ref.shape[1]
    virtual = vk_ref.shape[0]
    br = rows // blocks
    head = width // HEADS
    scale = head ** (-0.5)
    copies = start_copies(
        [
            (gain_hbm, gain_ref), (sblock_hbm, sblock_ref), (scount_hbm, scount_ref),
            (srows_hbm, srows_ref), (lrows_hbm, lrows_ref), (vk_hbm, vk_ref),
            (win_hbm.at[:, width : 2 * width], wk_ref), (win_hbm.at[:, :width], wq_ref),
            (win_hbm.at[:, 2 * width :], wv_ref), (wo_hbm, wo_ref),
        ],
        sems,
    )
    counts_ref[...] = jnp.zeros(counts_ref.shape, F32)
    for copy in copies:
        copy.wait()
    normed = norm_rows(load_ref[:rows, :], gain_ref[...])
    k = mm(normed, wk_ref[...]).astype(BF16)
    v = mm(normed, wv_ref[...]).astype(BF16)
    qt = mm(normed, wq_ref[...]).astype(BF16).T
    vt = v.T
    wvt_ref[...] = wv_ref[...].T

    vkf = vk_ref[...].astype(F32)
    vkbd = jnp.concatenate(
        [jnp.broadcast_to(vkf[j : j + 1, :], (HEADS, width)) for j in range(virtual)], axis=0
    )
    vkbd = jnp.where(of_own_head(vkbd.shape), vkbd, 0.0).astype(BF16)
    vkw_ref[...] = halves(mm_nt(vkbd, wk_ref[...]))
    vid = vid_row(load_ref, rows)
    add_pool(normed, vid, vkw_ref, pool_ref, weight_ref, scale, True)
    vcol_ref[...] = jnp.broadcast_to(vid, (128, rows)).T

    me = lax.axis_index("node")
    place = ring_place(me // CORES, chips)
    core = me % CORES
    for d in range(chips * CORES):
        want_ref[d] = 0
    for b in range(blocks):
        for e in range(slots):
            entry = sblock_ref[b, e]
            want_ref[entry // blocks] = entry % blocks
    for d in range(chips * CORES):
        step = (place - ring_place(jnp.int32(d // CORES), chips) + chips) % chips
        far = jnp.where(core == d % CORES, 0, 1)
        mask_ref[far, step] = jnp.full(mask_ref.shape[2:], want_ref[d].astype(F32), F32)
    for b in range(blocks):
        for e in range(slots):
            device = sblock_ref[b, e] // blocks
            step = (place - ring_place(device // CORES, chips) + chips) % chips
            far = jnp.where(device % CORES == core, 0, 1)
            live = jnp.where(e < scount_ref[b], 1.0, 0.0).astype(F32)
            counts_ref[far, step, b] += counts_of(srows_ref[b, e], br) * live

    zero = jnp.zeros((head, br), BF16)
    ones = jnp.ones((EXTRA, br), BF16)
    for b in range(blocks):
        cols = slice(b * br, (b + 1) * br)
        counts = counts_of(lrows_ref[:, cols], br)
        counts2 = jnp.concatenate([counts, counts], axis=1)
        for t in range(pairs):
            r0 = t * wide
            mid = r0 + head
            end = r0 + wide
            bd = jnp.concatenate(
                [
                    jnp.concatenate([qt[r0:mid, cols], zero], axis=1),
                    jnp.concatenate([zero, qt[mid:end, cols]], axis=1),
                ],
                axis=0,
            )
            qbd_ref[b, t] = bd
            values = jnp.concatenate([vt[r0:end, cols], ones], axis=0)
            fold(attend(k[cols, r0:end], values, counts2, bd, scale), num_ref, den_ref, b, t, False)


def take_sources(
    names, loads, mask_ref, gain_ref, wk_ref, wvt_ref, vkw_ref,
    normed_ref, k_ref, vt_ref, pool_ref, weight_ref,
):
    width = k_ref.shape[1]
    chosen = []
    vids = []
    for i, ((far, step), pieces) in enumerate(zip(names, loads)):
        part = norm_rows(load_rows(pieces), gain_ref[...])
        rows = part.shape[0]
        normed_ref[i * rows : (i + 1) * rows, :] = part
        chosen.append(choose(mask_ref[far, step, :1, :], part))
        vids.append(vid_row(pieces[-1], rows))
    picked = jnp.concatenate(chosen, axis=0)
    k_ref[...] = mm(picked, wk_ref[...]).astype(BF16)
    vt_ref[...] = mm_nt(wvt_ref[...], picked).astype(BF16)
    scale = (width // HEADS) ** (-0.5)
    vid = jnp.concatenate(vids, axis=1)
    add_pool(normed_ref[...], vid, vkw_ref, pool_ref, weight_ref, scale, False)


def add_sources(names, b, counts_ref, qbd_ref, k_ref, vt_ref, num_ref, den_ref):
    _, pairs, wide, _ = qbd_ref.shape
    scale = (2 / wide) ** 0.5
    counts = jnp.concatenate([counts_ref[far, step, b] for far, step in names], axis=0)
    counts2 = jnp.concatenate([counts, counts], axis=1)
    ones = jnp.ones((EXTRA, counts.shape[0]), BF16)
    for t in range(pairs):
        cols = slice(t * wide, (t + 1) * wide)
        values = jnp.concatenate([vt_ref[cols, :], ones], axis=0)
        o = attend(k_ref[:, cols], values, counts2, qbd_ref[b, t], scale)
        fold(o, num_ref, den_ref, b, t, True)


def slots_kernel(
    names, sizes, mask_ref, gain_ref, wk_ref, wvt_ref, vkw_ref, counts_ref, qbd_ref,
    num_in, den_in, pool_in, weight_in, *refs
):
    loads = grouped(refs, sizes)
    num_ref, den_ref, pool_ref, weight_ref, normed_ref, k_ref, vt_ref = refs[sum(sizes) :]
    num_ref[...] = num_in[...]
    den_ref[...] = den_in[...]
    pool_ref[...] = pool_in[...]
    weight_ref[...] = weight_in[...]
    take_sources(
        names, loads, mask_ref, gain_ref, wk_ref, wvt_ref, vkw_ref,
        normed_ref, k_ref, vt_ref, pool_ref, weight_ref,
    )
    for b in range(num_ref.shape[0]):
        add_sources(names, b, counts_ref, qbd_ref, k_ref, vt_ref, num_ref, den_ref)


def finish_kernel(names, b, lead, *refs):
    if lead:
        (
            mask_ref, gain_ref, wk_ref, wvt_ref, vkw_ref, pool_in, weight_in, last_ref,
            counts_ref, qbd_ref, num_in, den_in, vcol_ref, load_ref, wo_ref,
            out_ref, k_ref, vt_ref, pooled_ref,
            num_ref, den_ref, pool_ref, weight_ref, normed_ref,
        ) = refs
    else:
        (
            k_ref, vt_ref, pooled_ref,
            counts_ref, qbd_ref, num_in, den_in, vcol_ref, load_ref, wo_ref,
            out_ref, num_ref, den_ref,
        ) = refs
    _, width, br = num_ref.shape
    head = width // HEADS
    lanes = vcol_ref.shape[1]
    num_ref[b] = num_in[b]
    den_ref[b] = den_in[b]
    if lead:
        pool_ref[...] = pool_in[...]
        weight_ref[...] = weight_in[...]
        take_sources(
            names, [[last_ref]], mask_ref, gain_ref, wk_ref, wvt_ref, vkw_ref,
            normed_ref, k_ref, vt_ref, pool_ref, weight_ref,
        )
        count = pool_ref.shape[0]
        weight = jnp.concatenate([weight_ref[...]] * (width // lanes), axis=1)
        both = mm_nt(halves(pool_ref[...] / weight), wvt_ref[...])
        both = jnp.where(of_own_head((count, width)), both[:count] + both[count:], 0.0)
        for j in range(0, count, HEADS):
            pooled_ref[j // HEADS : j // HEADS + 1, :] = jnp.sum(
                both[j : j + HEADS], axis=0, keepdims=True
            )
    add_sources(names, b, counts_ref, qbd_ref, k_ref, vt_ref, num_ref, den_ref)
    part = slice(b * br, (b + 1) * br)
    vid = vcol_ref[part, :]
    att = jnp.concatenate(
        [
            num_ref[b, h * head : (h + 1) * head, :] / den_ref[b, h : h + 1, :]
            for h in range(HEADS)
        ],
        axis=0,
    ).T
    pieces = []
    for c in range(0, width, lanes):
        own = jnp.broadcast_to(pooled_ref[0:1, c : c + lanes], (br, lanes))
        for j in range(1, pooled_ref.shape[0]):
            own = jnp.where(vid == float(j), pooled_ref[j : j + 1, c : c + lanes], own)
        pieces.append((att[:, c : c + lanes] + own).astype(BF16))
    mixed = jnp.concatenate(pieces, axis=1)
    out_ref[...] = (load_ref[part, :].astype(F32) + mm(mixed, wo_ref[...])).astype(BF16)


def place_kernel(b, rows_ref, *refs):
    out_ref, sems = refs[-2:]
    br = rows_ref.shape[0]
    copy = pltpu.make_async_copy(rows_ref, out_ref.at[0, b * br : (b + 1) * br, :], sems.at[0])
    copy.start()
    copy.wait()


def params(mib):
    return pltpu.CompilerParams(vmem_limit_bytes=mib * 2**20)


def cost(flops):
    return pl.CostEstimate(flops=flops, bytes_accessed=1024, transcendentals=0)


def body(
    activations,
    norm_gain,
    project_in,
    project_out,
    virtual_keys,
    virtual_id,
    local_rows,
    slot_block,
    slot_count,
    slot_rows,
):
    _, rows, width = activations.shape
    br = slot_rows.shape[3]
    slots = slot_block.shape[1]
    blocks = rows // br
    devices = lax.axis_size("node")
    chips = devices // CORES
    virtual = virtual_keys.shape[1]
    pairs = HEADS // 2
    wide = width // pairs
    shape = jax.ShapeDtypeStruct
    after = lax.optimization_barrier
    unit = 2**16

    load = pl.pallas_call(
        pack_kernel,
        out_shape=shape((rows + EXTRA, width), BF16),
        in_specs=[HBM] * 2,
        out_specs=VMEM,
        scratch_shapes=[pltpu.VMEM((1, rows), jnp.int32), pltpu.SemaphoreType.DMA((2,))],
        compiler_params=params(24),
        cost_estimate=cost(unit),
        name="pack_rows",
    )(
        pltpu.with_memory_space_constraint(activations[0], pltpu.HBM),
        pltpu.with_memory_space_constraint(virtual_id.reshape(1, rows), pltpu.HBM),
    )
    near = {1: to_next_chip(load, devices, 1)}
    far = {0: swapped(load, devices, 1)}

    accumulators = (
        shape((blocks, width, br), F32),
        shape((blocks, HEADS, br), F32),
        shape((virtual * HEADS, width), F32),
        shape((virtual * HEADS, 128), F32),
    )
    square = shape((width, width), BF16)
    qbd, num, den, counts, mask, vcol, wk, wvt, wo, gain, vkw, pool, weight = pl.pallas_call(
        prep_kernel,
        out_shape=(
            (shape((blocks, pairs, wide, 2 * br), BF16),)
            + accumulators[:2]
            + (
                shape((CORES, chips, blocks, br, br), F32),
                shape((CORES, chips, 8, 128), F32),
                shape((rows, 128), F32),
                square,
                square,
                square,
                shape((1, width), F32),
                shape((2 * virtual * HEADS, width), BF16),
            )
            + accumulators[2:]
        ),
        in_specs=[VMEM] + [HBM] * 8,
        out_specs=[VMEM] * 13,
        scratch_shapes=[
            pltpu.VMEM((width, width), BF16),
            pltpu.VMEM((width, width), BF16),
            pltpu.VMEM((virtual, width), BF16),
            pltpu.VMEM(local_rows.shape, jnp.int32),
            pltpu.VMEM(slot_rows.shape, jnp.int32),
            pltpu.SMEM((blocks, slots), jnp.int32),
            pltpu.SMEM((blocks,), jnp.int32),
            pltpu.SMEM((devices,), jnp.int32),
            pltpu.SemaphoreType.DMA((10,)),
        ],
        compiler_params=params(32),
        cost_estimate=cost(unit),
        name="prepare",
    )(
        load,
        *[
            pltpu.with_memory_space_constraint(value, pltpu.HBM)
            for value in (
                norm_gain, project_in[0], virtual_keys[0], local_rows, slot_rows, slot_block,
                slot_count, project_out[0],
            )
        ],
    )

    def work(count):
        return [
            pltpu.VMEM((count * rows, width), BF16),
            pltpu.VMEM((count * br, width), BF16),
            pltpu.VMEM((width, count * br), BF16),
        ]

    if chips > 2:
        back, den = after((load, den))
        near[chips - 1] = to_next_chip(back, devices, -1)
    sums = (num, den, pool, weight)

    def arrive(step, sums):
        near[step], first = after((near[step], sums[1]))
        return (sums[0], first) + sums[2:]

    def slots_call(names, sums, name):
        loads = [(far if other else near)[step] for other, step in names]
        loads = [load if isinstance(load, list) else [load] for load in loads]
        sizes = tuple(len(load) for load in loads)
        return pl.pallas_call(
            functools.partial(slots_kernel, tuple(names), sizes),
            out_shape=accumulators,
            in_specs=[VMEM] * (11 + sum(sizes)),
            out_specs=[VMEM] * 4,
            scratch_shapes=work(len(names)),
            compiler_params=params(40),
            cost_estimate=cost(unit),
            name=name,
        )(
            mask, gain, wk, wvt, vkw, counts, qbd, *sums,
            *[piece for load in loads for piece in load],
        )

    ahead = chips // 2
    order = []
    for s in range(1, ahead + 1):
        order.append((s, 1))
        if s < chips - s:
            order.append((chips - s, -1))
    sums = slots_call([(1, 0)], sums, "slots_own")

    def hop_on(step, way):
        nexts = step + way
        if nexts not in near and (nexts, way) in order:
            near[nexts] = to_next_chip(near[step], devices, way)

    firsts = order[:-1][:2]
    for step, way in firsts:
        sums = arrive(step, sums)
        hop_on(step, way)
    for step, _ in firsts:
        far[step] = swapped_parts(near[step], devices, PARTS)
    if firsts:
        names = [(other, step) for other in range(CORES) for step, _ in firsts]
        sums = slots_call(names, sums, "slots_both")
    for i, (step, way) in enumerate(order[len(firsts) :]):
        sums = arrive(step, sums)
        hop_on(step, way)
        far[step] = swapped(near[step], devices, 1)
        names = [(0, step), (1, step)]
        if step == order[-1][0]:
            names = names[:1]
        sums = slots_call(names, sums, "slots_%d" % i)
    names = ((1, order[-1][0]),)
    shared = (counts, qbd, sums[0], sums[1], vcol, load, wo)
    scratch = [pltpu.VMEM(leaf.shape, leaf.dtype) for leaf in accumulators]
    carried = (
        shape((br, width), BF16), shape((width, br), BF16), shape((virtual, width), F32)
    )
    results = []
    for b in range(blocks):
        lead = b == 0
        outs = pl.pallas_call(
            functools.partial(finish_kernel, names, b, lead),
            out_shape=(shape((br, width), BF16),) + (carried if lead else ()),
            in_specs=[VMEM] * (15 if lead else 10),
            out_specs=(VMEM,) * (4 if lead else 1),
            scratch_shapes=scratch + work(1)[:1] if lead else scratch[:2],
            compiler_params=params(40),
            cost_estimate=cost(unit),
            name="finish_%d" % b,
        )(
            *(
                (mask, gain, wk, wvt, vkw, sums[2], sums[3], far[names[0][1]])
                if lead
                else kept
            ),
            *shared,
        )
        if lead:
            kept = tuple(outs[1:])
        results.append(to_next_segment(outs[0]))
    joined = None
    for b in range(blocks):
        earlier = [] if joined is None else [joined]
        joined = pl.pallas_call(
            functools.partial(place_kernel, b),
            out_shape=shape((1, rows, width), BF16),
            in_specs=[VMEM] + [HBM] * len(earlier),
            out_specs=HBM,
            scratch_shapes=[pltpu.SemaphoreType.DMA((1,))],
            input_output_aliases={1: 0} if earlier else {},
            compiler_params=params(24),
            cost_estimate=cost(unit),
            name="place_%d" % b,
        )(results[b], *earlier)
    return joined


def solution(mesh):
    placed = (
        P("segment", "node", None),
        P("segment", None),
        P("segment", None, None),
        P("segment", None, None),
        P("segment", None, None),
        P("node", None),
        P(None, "node"),
        P("node", None),
        P("node"),
        P("node", None, None, None),
    )
    return jax.shard_map(
        body, mesh=mesh, in_specs=placed, out_specs=P("segment", "node", None), check_vma=False
    )
```
